32 devices in a mesh: dp: 16 (over z, y, core), tensor: 2 (over x).
Axes of the slice: x: 2, y: 2, z: 4, core: 2. Of those that a mesh axis runs over, the one named last changes fastest.
Arguments:
- inputs: bfloat16 [32, 512, 768], P('dp'), may hold values from -6 to 6
- lengths: int32 [32], P('dp'), may hold values from 16 to 512, as said below
- w_query: bfloat16 [768, 768], P(None, 'tensor'), may hold values from -0.21875 to 0.21875
- b_query: bfloat16 [768], P('tensor'), may hold values from -3 to 3
- w_key: bfloat16 [768, 768], P(None, 'tensor'), may hold values from -0.21875 to 0.21875
- w_value: bfloat16 [768, 768], P(None, 'tensor'), may hold values from -0.21875 to 0.21875
- b_value: bfloat16 [768], P('tensor'), may hold values from -3 to 3
- w_output: bfloat16 [768, 768], P('tensor'), may hold values from -0.875 to 0.875
- b_output: bfloat16 [768], replicated, may hold values from -3 to 3
- gain_one: bfloat16 [768], replicated, may hold values from 0.5 to 1.5
- shift_one: bfloat16 [768], replicated, may hold values from -3 to 3
- w_up: bfloat16 [768, 3072], P(None, 'tensor'), may hold values from -0.21875 to 0.21875
- b_up: bfloat16 [3072], P('tensor'), may hold values from -3 to 3
- w_down: bfloat16 [3072, 768], P('tensor'), may hold values from -0.109375 to 0.109375
- b_down: bfloat16 [768], replicated, may hold values from -3 to 3
- gain_two: bfloat16 [768], replicated, may hold values from 0.5 to 1.5
- shift_two: bfloat16 [768], replicated, may hold values from -3 to 3
- cotangent: bfloat16 [32, 512, 768], P('dp'), may hold values from -6 to 6
Outputs:
- layer_out: bfloat16 [32, 512, 768], P('dp')
- grad_inputs: bfloat16 [32, 512, 768], P('dp')
- grad_w_query: float32 [768, 768], P('dp', 'tensor')
- grad_b_query: float32 [768], P('tensor')
- grad_w_key: float32 [768, 768], P('dp', 'tensor')
- grad_w_value: float32 [768, 768], P('dp', 'tensor')
- grad_b_value: float32 [768], P('tensor')
- grad_w_output: float32 [768, 768], P('tensor', 'dp')
- grad_b_output: float32 [768], P('dp')
- grad_gain_one: float32 [768], P('dp')
- grad_shift_one: float32 [768], P('dp')
- grad_w_up: float32 [768, 3072], P('dp', 'tensor')
- grad_b_up: float32 [3072], P('tensor')
- grad_w_down: float32 [3072, 768], P('tensor', 'dp')
- grad_b_down: float32 [768], P('dp')
- grad_gain_two: float32 [768], P('dp')
- grad_shift_two: float32 [768], P('dp')
The draws below stay inside these ranges and needn't reach their ends.
Inputs may be any that keep to these rules, and one draw needn't show every extreme that they name: `lengths`: positions at or past a sentence's length are padding; some sentence has length 512 in every draw.
All inputs are finite; a program needn't handle non-finite values.
Results may differ from the reference program's by a relative error of at most 0.013.
Values sent between devices are 32-bit elements; how exact they have to be, the bound alone decides.
No kernel may reach another device: no remote copies, remote signals or barrier semaphores. Data moves between devices by JAX's collectives and lax.ppermute only.
A program may use at most 128 MiB of HBM per device.

```python
import math
import jax
import jax.numpy as jnp
from jax import lax

D = 768
DH = 64
FF = 3072
SEQ_LEN = 512
SEQS = 32


def draw_lengths(key, part):
    key = jax.random.fold_in(key, 7)
    first_key, second_key = jax.random.split(key, 2)
    lowest = max(1, SEQ_LEN // 32)
    span = max(SEQ_LEN - lowest, 1)
    uniform_part = jax.random.randint(first_key, (SEQS,), 0, span + 1)
    tailed = lowest + uniform_part * uniform_part // span * uniform_part // span
    longest = jax.random.randint(second_key, (), 0, SEQS)
    tailed = jnp.where(jnp.arange(SEQS) == longest, SEQ_LEN, tailed)
    return jnp.minimum(tailed, SEQ_LEN).astype(jnp.int32)


def raised(drawn, rng, source, target, parts, factor):
    def block_of(dim):
        return (jnp.arange(drawn.shape[dim]) // (drawn.shape[dim] // parts)).reshape((-1,) + (1,) * (drawn.ndim - 1 - dim))

    one_side = jax.random.permutation(rng, parts)[block_of(target)]
    second = (block_of(target) + parts // 2) % parts
    return jnp.where((block_of(source) == one_side) | (block_of(source) == second), factor * drawn, drawn)


def block_levels(rng, extent, cuts, low, top_value):
    def one(position, shards_of):
        draws = jax.random.uniform(jax.random.fold_in(jax.random.fold_in(rng, 6), position), (shards_of,), jnp.float32, low / len(cuts), top_value / len(cuts))
        return jnp.repeat(jnp.exp(draws), extent[position] // shards_of).reshape((-1,) + (1,) * (len(extent) - position - 1))

    factor_of = one(*cuts[0])
    for cut in cuts[1:]:
        factor_of = factor_of * one(*cut)
    return factor_of


def gaussian(rng, shape, deviation, bound, shards=(), kind=jnp.bfloat16):
    values = jax.random.normal(rng, shape, jnp.float32) * deviation
    if len(shards) > 0:
        values = block_levels(rng, shape, shards, -0.22, 0.18) * values
    return jnp.clip(values, min=-bound, max=bound).astype(kind)


def bell_draw_with(key, shape, scale, bound, cuts, heavy, kind=jnp.bfloat16):
    drawn = scale * jax.random.normal(key, shape, jnp.float32)
    if cuts:
        drawn = drawn * block_levels(key, shape, cuts, -0.22, 0.18)
    return jnp.clip(raised(drawn, jax.random.fold_in(key, 3), *heavy), -bound, bound).astype(kind)


def setup_inputs(seed: int = 0) -> dict:
    arg_keys = jax.random.split(jax.random.key(seed), 19)
    inputs = bell_draw_with(arg_keys[0], (SEQS, SEQ_LEN, D), 1.0, 6.0, ((0, 16),), (0, 2, 16, 2.0))
    lengths = draw_lengths(jax.random.fold_in(arg_keys[18], 71), 0)
    w_query = gaussian(arg_keys[2], (D, D), D ** -0.5, 0.21875, ((1, 2),))
    b_query = gaussian(arg_keys[3], (D,), 0.5, 3.0, ((0, 2),))
    w_key = gaussian(arg_keys[4], (D, D), D ** -0.5, 0.21875, ((1, 2),))
    w_value = gaussian(arg_keys[5], (D, D), D ** -0.5, 0.21875, ((1, 2),))
    b_value = gaussian(arg_keys[6], (D,), 0.5, 3.0, ((0, 2),))
    w_output = gaussian(arg_keys[7], (D, D), (D // 16) ** -0.5, 0.875, ((0, 2),))
    b_output = gaussian(arg_keys[8], (D,), 0.5, 3.0)
    gain_one = jnp.clip(jax.random.uniform(arg_keys[9], (D,), jnp.float32, 0.5, 1.5), 0.5, 1.5).astype(jnp.bfloat16)
    shift_one = gaussian(arg_keys[10], (D,), 0.5, 3.0)
    w_up = gaussian(arg_keys[11], (D, FF), D ** -0.5, 0.21875, ((1, 2),))
    b_up = gaussian(arg_keys[12], (FF,), 0.5, 3.0, ((0, 2),))
    w_down = gaussian(arg_keys[13], (FF, D), FF ** -0.5, 0.109375, ((0, 2),))
    b_down = gaussian(arg_keys[14], (D,), 0.5, 3.0)
    gain_two = jnp.clip(jax.random.uniform(arg_keys[15], (D,), jnp.float32, 0.5, 1.5), 0.5, 1.5).astype(jnp.bfloat16)
    shift_two = gaussian(arg_keys[16], (D,), 0.5, 3.0)
    cotangent = bell_draw_with(arg_keys[17], (SEQS, SEQ_LEN, D), 1.0, 6.0, ((0, 16),), (0, 2, 16, 2.0))
    return {"inputs": inputs, "lengths": lengths, "w_query": w_query, "b_query": b_query, "w_key": w_key, "w_value": w_value, "b_value": b_value, "w_output": w_output, "b_output": b_output, "gain_one": gain_one, "shift_one": shift_one, "w_up": w_up, "b_up": b_up, "w_down": w_down, "b_down": b_down, "gain_two": gain_two, "shift_two": shift_two, "cotangent": cotangent}


norm_eps = 1e-12
masked_score = -1000000000.0

@jax.custom_vjp
def low(v):
    return lax.optimization_barrier(v.astype(jnp.bfloat16)).astype(jnp.float32)

@jax.custom_vjp
def low_back(v):
    return v

def low_keep(v):
    return (low(v), None)

def low_pass(kept, grad):
    return (grad,)

def back_keep(v):
    return (v, None)

def back_low(kept, grad):
    return (low(grad),)
low.defvjp(low_keep, low_pass)
low_back.defvjp(back_keep, back_low)

def matmul(left, right):
    return jnp.dot(left, right, precision=lax.Precision.HIGHEST)

def layer_norm(values, gain, shift):
    center = values - lax.optimization_barrier(jnp.mean(values, axis=-1, keepdims=True))
    spread = lax.optimization_barrier(jnp.mean(center * center, axis=-1, keepdims=True))
    return center * lax.rsqrt(spread + norm_eps) * gain + shift

def forward(inputs, valid, w_query, b_query, w_key, w_value, b_value, w_output, b_output, gain_one, shift_one, w_up, b_up, w_down, b_down, gain_two, shift_two):
    count, length, width = inputs.shape
    flat = inputs.reshape(count * length, width)
    heads = width // DH
    query = low(low_back(matmul(flat, w_query) + b_query)).reshape(count, length, heads, DH)
    keys = low(low_back(matmul(flat, w_key))).reshape(count, length, heads, DH)
    values = low(low_back(matmul(flat, w_value) + b_value)).reshape(count, length, heads, DH)
    scores = jnp.einsum('sqhd,skhd->shqk', query, keys, precision=lax.Precision.HIGHEST) * 0.125
    scores = jnp.where(valid[:, None, None, :], low_back(scores), masked_score)
    top = lax.optimization_barrier(jnp.max(scores, axis=-1, keepdims=True))
    expo = jnp.exp(scores - top)
    probs = expo / lax.optimization_barrier(jnp.sum(expo, axis=-1, keepdims=True))
    context = jnp.einsum('shqk,skhd->sqhd', low(probs), values, precision=lax.Precision.HIGHEST)
    context = low_back(low(context)).reshape(count * length, width)
    attn = low_back(matmul(context, w_output)) + b_output
    first = layer_norm(flat + attn, gain_one, shift_one)
    pre = low_back(matmul(low(first), w_up) + b_up)
    act = low(jax.nn.gelu(pre, approximate=False))
    ffn = low_back(matmul(act, w_down)) + b_down
    return layer_norm(first + ffn, gain_two, shift_two).reshape(count, length, width)

def reference(inputs, lengths, w_query, b_query, w_key, w_value, b_value, w_output, b_output, gain_one, shift_one, w_up, b_up, w_down, b_down, gain_two, shift_two, cotangent):
    params = tuple((p.astype(jnp.float32) for p in (w_query, b_query, w_key, w_value, b_value, w_output, b_output, gain_one, shift_one, w_up, b_up, w_down, b_down, gain_two, shift_two)))
    group = math.gcd(SEQS, max(1, 4096 // SEQ_LEN))
    blocks = SEQS // group
    positions = jnp.arange(SEQ_LEN, dtype=jnp.int32)
    valid_all = positions[None, :] < lengths.astype(jnp.int32)[:, None]
    stacked = inputs.reshape(blocks, group, SEQ_LEN, D)
    valid_blocks = valid_all.reshape(blocks, group, SEQ_LEN)
    tangents = cotangent.reshape(blocks, group, SEQ_LEN, D)

    def one_group(totals, pieces):
        inputs_now, valid_now, tangent_now = pieces

        def apply(inputs_float, *weights):
            return forward(inputs_float, valid_now, *weights)
        result, pullback = jax.vjp(apply, inputs_now.astype(jnp.float32), *params)
        grads = pullback(tangent_now.astype(jnp.float32))
        totals = tuple((a_sum + a_new for a_sum, a_new in zip(totals, grads[1:])))
        return (totals, (result.astype(jnp.bfloat16), grads[0].astype(jnp.bfloat16)))
    start = tuple((jnp.zeros_like(p) for p in params))
    summed, (outputs, input_grads) = lax.scan(one_group, start, (stacked, valid_blocks, tangents))
    return (outputs.reshape(SEQS, SEQ_LEN, D), input_grads.reshape(SEQS, SEQ_LEN, D), summed[0], summed[1], summed[2], summed[3], summed[4], summed[5], summed[6], summed[7], summed[8], summed[9], summed[10], summed[11], summed[12], summed[13], summed[14])
```

```python
import functools
import math

import jax
import jax.numpy as jnp
from jax import lax
from jax.experimental import pallas as pl
from jax.experimental.pallas import tpu as pltpu
from jax.sharding import PartitionSpec as P

DH = 64
PAIR = 2 * DH

norm_eps = 1e-12
masked_score = -1000000000.0
PARAMS = pltpu.CompilerParams(vmem_limit_bytes=48 * 1024 * 1024)


def over_rows(left, right):
    return lax.dot_general(
        left, right, (((0,), (0,)), ((), ())), preferred_element_type=jnp.float32
    )


def against(left, right):
    return lax.dot_general(
        left, right, (((1,), (1,)), ((), ())), preferred_element_type=jnp.float32
    )


def plain(left, right):
    return jnp.dot(left, right, preferred_element_type=jnp.float32)


def norm_forward(values, gain, shift):
    center = values - jnp.mean(values, axis=-1, keepdims=True)
    spread = jnp.mean(center * center, axis=-1, keepdims=True)
    inverse = lax.rsqrt(spread + norm_eps)
    normed = center * inverse
    return (normed * gain + shift, normed, inverse)


def norm_backward(grad, normed, inverse, gain):
    scaled = grad * gain
    mean_one = jnp.mean(scaled, axis=-1, keepdims=True)
    mean_two = jnp.mean(scaled * normed, axis=-1, keepdims=True)
    return inverse * (scaled - mean_one - normed * mean_two)


def gelu_both(value):
    phi_big = 0.5 + 0.5 * lax.erf(value * math.sqrt(0.5))
    phi_small = jnp.exp(-0.5 * value * value) * (1.0 / math.sqrt(2.0 * math.pi))
    return (value * phi_big).astype(jnp.bfloat16), (phi_big + value * phi_small).astype(jnp.bfloat16)


def swap_x(value):
    return lax.ppermute(value, "tensor", [(0, 1), (1, 0)])


def swap_dp(value, bit, n):
    return lax.ppermute(value, "dp", [(i, i ^ bit) for i in range(n)])


def place_kernel(slots, me_ref, *refs):
    out = refs[-1]
    rows = refs[0].shape[0]
    for slot, piece in zip(slots, refs[:-1]):
        at = jnp.bitwise_xor(jnp.bitwise_and(me_ref[0], 7), slot) * rows
        out[pl.ds(pl.multiple_of(at, rows), rows), :] = piece[...].astype(out.dtype)


def fetch_other(own, me, n, first, second):
    rows = own.shape[0] // 8
    mine = lax.dynamic_slice_in_dim(own, jnp.bitwise_and(me, 7) * rows, rows, 0)
    a = swap_x(mine.astype(jnp.float32))
    b = swap_dp(a, first, n)
    c, d = swap_dp(a, second, n), swap_dp(b, second, n)
    pieces = [a, b, c, d] + [swap_dp(v, 1, n) for v in (a, b, c, d)]
    slots = [0, first, second, first | second]
    slots = slots + [s | 1 for s in slots]
    return pl.pallas_call(
        functools.partial(place_kernel, slots),
        out_shape=jax.ShapeDtypeStruct(own.shape, own.dtype),
        in_specs=[pl.BlockSpec(memory_space=pltpu.SMEM)]
        + [pl.BlockSpec(memory_space=pltpu.VMEM)] * 8,
        out_specs=pl.BlockSpec(memory_space=pltpu.VMEM),
        compiler_params=PARAMS,
    )(me.reshape(1), *pieces)


def relative_chunks(n, order):
    steps = len(order)
    return [
        sum(bit for j, bit in enumerate(order) if (r >> (steps - 1 - j)) & 1) for r in range(n)
    ]


def turn_kernel(chunks, me_ref, x_ref, out_ref, scratch):
    rows = out_ref.shape[0] // len(chunks)
    scratch[...] = x_ref[...].T
    for r, chunk in enumerate(chunks):
        at = pl.multiple_of(jnp.bitwise_xor(me_ref[0], chunk) * rows, rows)
        out_ref[r * rows : (r + 1) * rows, :] = scratch[pl.ds(at, rows), :]


def turned(x, me, n, order):
    chunks = relative_chunks(n, order)
    rows = x.shape[1] // n
    if rows % 16:
        wanted = jnp.bitwise_xor(me, jnp.array(chunks, jnp.int32))
        return x.T.reshape(n, rows, x.shape[0])[wanted].reshape(x.shape[1], x.shape[0])
    return pl.pallas_call(
        functools.partial(turn_kernel, chunks),
        out_shape=jax.ShapeDtypeStruct((x.shape[1], x.shape[0]), x.dtype),
        in_specs=[
            pl.BlockSpec(memory_space=pltpu.SMEM),
            pl.BlockSpec(memory_space=pltpu.VMEM),
        ],
        out_specs=pl.BlockSpec(memory_space=pltpu.VMEM),
        scratch_shapes=[pltpu.VMEM((x.shape[1], x.shape[0]), x.dtype)],
        compiler_params=PARAMS,
    )(me.reshape(1), x)


def scatter_sum(grad, n, order):
    for bit in order:
        half = grad.shape[0] // 2
        grad = grad[:half] + swap_dp(grad[half:], bit, n)
    return grad


def total_sum(value, n, order):
    for bit in order:
        value = value + swap_dp(value, bit, n)
    return value


def attend_kernel(len_ref, x_ref, ctx_ref, lse_ref):
    length = x_ref.shape[0]
    real = len_ref[pl.program_id(0)]
    lane = lax.broadcasted_iota(jnp.int32, (1, PAIR), 1)
    valid = lax.broadcasted_iota(jnp.int32, (length, 1), 0) < real
    query = x_ref[:, 0:PAIR] * jnp.bfloat16(0.125)
    keys = x_ref[:, PAIR : 2 * PAIR]
    values_t = x_ref[:, 2 * PAIR : 3 * PAIR].T
    outs, logs = [], []
    for h in range(2):
        mine = (lane < DH) if h == 0 else (lane >= DH)
        q = jnp.where(mine, query, jnp.bfloat16(0))
        s = against(keys, q)
        s = jnp.where(valid, s, masked_score)
        top = jnp.max(s, axis=0, keepdims=True)
        e = jnp.exp(s - top)
        total = jnp.sum(e, axis=0, keepdims=True)
        p = (e * (1.0 / total)).astype(jnp.bfloat16)
        outs.append(plain(values_t[h * DH : (h + 1) * DH, :], p))
        logs.append(top + jnp.log(total))
    ctx_ref[...] = jnp.concatenate(outs, axis=0).T.astype(jnp.bfloat16)
    lse_ref[0, 0] = jnp.concatenate(logs, axis=0)


def attend(lengths, qkv, count):
    tokens, width = qkv.shape
    length = tokens // count
    pairs = width // (3 * PAIR)
    return pl.pallas_call(
        attend_kernel,
        grid=(count, pairs),
        in_specs=[
            pl.BlockSpec(memory_space=pltpu.SMEM),
            pl.BlockSpec((length, 3 * PAIR), lambda s, p: (s, p)),
        ],
        out_specs=[
            pl.BlockSpec((length, PAIR), lambda s, p: (s, p)),
            pl.BlockSpec((1, 1, 2, length), lambda s, p: (s, p, 0, 0)),
        ],
        out_shape=[
            jax.ShapeDtypeStruct((tokens, pairs * PAIR), jnp.bfloat16),
            jax.ShapeDtypeStruct((count, pairs, 2, length), jnp.float32),
        ],
        compiler_params=PARAMS,
        cost_estimate=pl.CostEstimate(
            flops=4 * tokens * length * 4 * pairs * PAIR, bytes_accessed=8 * tokens * width, transcendentals=0
        ),
    )(lengths, qkv)


def attend_back_kernel(len_ref, x_ref, lse_ref, dc_ref, out_ref):
    length = x_ref.shape[0]
    real = len_ref[pl.program_id(0)]
    lane = lax.broadcasted_iota(jnp.int32, (1, PAIR), 1)
    valid = lax.broadcasted_iota(jnp.int32, (length, 1), 0) < real
    query = x_ref[:, 0:PAIR] * jnp.bfloat16(0.125)
    keys = x_ref[:, PAIR : 2 * PAIR]
    keys_t = keys.T
    values = x_ref[:, 2 * PAIR : 3 * PAIR]
    d_ctx = dc_ref[...]
    dq, dk, dv = [], [], []
    for h in range(2):
        mine = (lane < DH) if h == 0 else (lane >= DH)
        q = jnp.where(mine, query, jnp.bfloat16(0))
        s = against(keys, q)
        s = jnp.where(valid, s, masked_score)
        p = jnp.exp(s - lse_ref[0, 0, h : h + 1, :])
        dv.append(plain(p.astype(jnp.bfloat16), d_ctx))
        dp = against(values, jnp.where(mine, d_ctx, jnp.bfloat16(0)))
        row = jnp.sum(p * dp, axis=0, keepdims=True)
        ds = (p * (dp - row)).astype(jnp.bfloat16)
        dk.append(plain(ds, query))
        dq.append(plain(keys_t[h * DH : (h + 1) * DH, :], ds))
    first = lane < DH
    out_ref[:, 0:PAIR] = (jnp.concatenate(dq, axis=0) * 0.125).T.astype(jnp.bfloat16)
    out_ref[:, PAIR : 2 * PAIR] = jnp.where(first, dk[0], dk[1]).astype(jnp.bfloat16)
    out_ref[:, 2 * PAIR : 3 * PAIR] = jnp.where(first, dv[0], dv[1]).astype(jnp.bfloat16)


def attend_back(lengths, qkv, lse, d_ctx, count):
    tokens, width = qkv.shape
    length = tokens // count
    pairs = width // (3 * PAIR)
    return pl.pallas_call(
        attend_back_kernel,
        grid=(count, pairs),
        in_specs=[
            pl.BlockSpec(memory_space=pltpu.SMEM),
            pl.BlockSpec((length, 3 * PAIR), lambda s, p: (s, p)),
            pl.BlockSpec((1, 1, 2, length), lambda s, p: (s, p, 0, 0)),
            pl.BlockSpec((length, PAIR), lambda s, p: (s, p)),
        ],
        out_specs=pl.BlockSpec((length, 3 * PAIR), lambda s, p: (s, p)),
        out_shape=jax.ShapeDtypeStruct((tokens, width), jnp.bfloat16),
        compiler_params=PARAMS,
        cost_estimate=pl.CostEstimate(
            flops=10 * tokens * length * 4 * pairs * PAIR, bytes_accessed=8 * tokens * width, transcendentals=0
        ),
    )(lengths, qkv, lse, d_ctx)


def by_pairs(q, k, v):
    rows = q.shape[0]
    pairs = q.shape[1] // PAIR
    parts = [a.reshape(rows, pairs, 1, PAIR) for a in (q, k, v)]
    return jnp.concatenate(parts, axis=2).reshape(rows, pairs * 3 * PAIR)


def per_device(
    inputs,
    lengths,
    w_query,
    b_query,
    w_key,
    w_value,
    b_value,
    w_output,
    b_output,
    gain_one,
    shift_one,
    w_up,
    b_up,
    w_down,
    b_down,
    gain_two,
    shift_two,
    cotangent,
    *,
    n,
):
    f32 = jnp.float32
    count, length, width = inputs.shape
    local = w_query.shape[1]
    flat = inputs.reshape(count * length, width)
    me = lax.axis_index("dp").astype(jnp.int32)
    bits = [1 << i for i in range(n.bit_length() - 1)]
    y_first = tuple(bits)
    z_first = (bits[0], bits[2], bits[1]) + tuple(bits[3:])

    wqkv = by_pairs(w_query, w_key, w_value)
    zero = jnp.zeros((local,), f32)
    bqkv = by_pairs(b_query.astype(f32)[None], zero[None], b_value.astype(f32)[None])
    biases = swap_x(jnp.concatenate([bqkv[0], b_up.astype(f32)])[None])
    bqkv_far, b_up_far = biases[:, : 3 * local], biases[:, 3 * local :]
    wqkv_far = fetch_other(wqkv, me, n, 2, 4)
    wo_far = fetch_other(w_output, me, n, 4, 2)
    wu_far = fetch_other(w_up, me, n, 2, 4)
    wd_far = fetch_other(w_down, me, n, 4, 2)

    gain_first = gain_one.astype(f32)
    gain_second = gain_two.astype(f32)

    qkv = (plain(flat, wqkv) + bqkv).astype(jnp.bfloat16)
    ctx, lse = attend(lengths, qkv, count)
    qkv_far = (plain(flat, wqkv_far) + bqkv_far).astype(jnp.bfloat16)
    ctx_far, lse_far = attend(lengths, qkv_far, count)
    attn = plain(ctx, w_output) + plain(ctx_far, wo_far)
    residual_one = flat.astype(f32) + attn + b_output.astype(f32)
    first, normed_one, inverse_one = norm_forward(residual_one, gain_first, shift_one.astype(f32))
    first_low = first.astype(jnp.bfloat16)
    act, slope = gelu_both(plain(first_low, w_up) + b_up.astype(f32))
    act_far, slope_far = gelu_both(plain(first_low, wu_far) + b_up_far)
    ffn = plain(act, w_down) + plain(act_far, wd_far)
    residual_two = first + ffn + b_down.astype(f32)
    final, normed_two, inverse_two = norm_forward(residual_two, gain_second, shift_two.astype(f32))
    layer_out = final.astype(jnp.bfloat16).reshape(count, length, width)

    tangent = cotangent.reshape(count * length, width).astype(f32)
    grad_gain_two = jnp.sum(tangent * normed_two, axis=0)
    grad_shift_two = jnp.sum(tangent, axis=0)
    d_second = norm_backward(tangent, normed_two, inverse_two, gain_second)
    d_ffn = d_second.astype(jnp.bfloat16)
    grad_b_down = jnp.sum(d_second, axis=0)
    sum_down = scatter_sum(plain(turned(d_ffn, me, n, y_first), act), n, y_first)
    d_pre = (against(d_ffn, w_down) * slope.astype(f32)).astype(jnp.bfloat16)
    grad_b_up = jnp.sum(d_pre.astype(f32), axis=0)
    sum_up = scatter_sum(plain(turned(first_low, me, n, y_first), d_pre), n, y_first)
    d_pre_far = (against(d_ffn, wd_far) * slope_far.astype(f32)).astype(jnp.bfloat16)
    d_first = d_second + against(d_pre, w_up) + against(d_pre_far, wu_far)
    grad_gain_one = jnp.sum(d_first * normed_one, axis=0)
    grad_shift_one = jnp.sum(d_first, axis=0)
    d_res_one = norm_backward(d_first, normed_one, inverse_one, gain_first)
    d_attn = d_res_one.astype(jnp.bfloat16)
    grad_b_output = jnp.sum(d_res_one, axis=0)
    sum_output = scatter_sum(plain(turned(d_attn, me, n, y_first), ctx), n, y_first)
    d_ctx = against(d_attn, w_output).astype(jnp.bfloat16)
    d_ctx_far = against(d_attn, wo_far).astype(jnp.bfloat16)
    d_qkv = attend_back(lengths, qkv, lse, d_ctx, count)
    grad_bqkv = jnp.sum(d_qkv.astype(f32), axis=0)
    sum_qkv = scatter_sum(plain(turned(flat, me, n, z_first), d_qkv), n, z_first)
    d_qkv_far = attend_back(lengths, qkv_far, lse_far, d_ctx_far, count)
    d_inputs = d_res_one + against(d_qkv, wqkv) + against(d_qkv_far, wqkv_far)
    grad_inputs = d_inputs.astype(jnp.bfloat16).reshape(count, length, width)

    vectors = jnp.concatenate(
        [
            grad_b_output,
            grad_gain_one,
            grad_shift_one,
            grad_b_down,
            grad_gain_two,
            grad_shift_two,
            grad_b_up,
            grad_bqkv,
        ]
    ).reshape(-1, 384)
    vectors = total_sum(vectors, n, y_first).reshape(-1)
    rows = width // n
    shared = lax.dynamic_slice_in_dim(vectors[: 6 * width].reshape(6, width), me * rows, rows, 1)
    hidden = b_up.shape[0]
    sum_b_up = vectors[6 * width : 6 * width + hidden]
    sum_bqkv = vectors[6 * width + hidden :].reshape(-1, 3, PAIR)
    split = sum_qkv.reshape(rows, -1, 3, PAIR)
    return (
        layer_out,
        grad_inputs,
        split[:, :, 0].reshape(rows, local),
        sum_bqkv[:, 0].reshape(local),
        split[:, :, 1].reshape(rows, local),
        split[:, :, 2].reshape(rows, local),
        sum_bqkv[:, 2].reshape(local),
        sum_output.T,
        shared[0],
        shared[1],
        shared[2],
        sum_up,
        sum_b_up,
        sum_down.T,
        shared[3],
        shared[4],
        shared[5],
    )


def solution(mesh):
    in_specs = (
        P("dp", None, None),
        P("dp"),
        P(None, "tensor"),
        P("tensor"),
        P(None, "tensor"),
        P(None, "tensor"),
        P("tensor"),
        P("tensor", None),
        P(),
        P(),
        P(),
        P(None, "tensor"),
        P("tensor"),
        P("tensor", None),
        P(),
        P(),
        P(),
        P("dp", None, None),
    )
    out_specs = (
        P("dp", None, None),
        P("dp", None, None),
        P("dp", "tensor"),
        P("tensor"),
        P("dp", "tensor"),
        P("dp", "tensor"),
        P("tensor"),
        P("tensor", "dp"),
        P("dp"),
        P("dp"),
        P("dp"),
        P("dp", "tensor"),
        P("tensor"),
        P("tensor", "dp"),
        P("dp"),
        P("dp"),
        P("dp"),
    )
    return jax.shard_map(
        functools.partial(per_device, n=mesh.shape["dp"]),
        mesh=mesh,
        in_specs=in_specs,
        out_specs=out_specs,
        check_vma=False,
    )
```

```python
import functools
import math

import jax
import jax.numpy as jnp
from jax import lax
from jax.experimental import pallas as pl
from jax.experimental.pallas import tpu as pltpu
from jax.sharding import PartitionSpec as P

DH = 64
PAIR = 2 * DH
ROWS = 256
WIDE = 512
GRANT = 60 * 1024 * 1024
FLYING = 3 * 1024 * 1024
LONG = pl.CostEstimate(flops=10**13, bytes_accessed=10**6, transcendentals=0)

norm_eps = 1e-12
masked_score = -1000000000.0
BF = jnp.bfloat16
F32 = jnp.float32
SMEM = pl.BlockSpec(memory_space=pltpu.SMEM)
VMEM = pl.BlockSpec(memory_space=pltpu.VMEM)
ANY = pl.BlockSpec(memory_space=pl.ANY)


def shape(dims, kind):
    return jax.ShapeDtypeStruct(tuple(dims), kind)


def against(left, right):
    return lax.dot_general(left, right, (((1,), (1,)), ((), ())), preferred_element_type=F32)


def over_rows(left, right):
    return lax.dot_general(left, right, (((0,), (0,)), ((), ())), preferred_element_type=F32)


def plain(left, right):
    return jnp.dot(left, right, preferred_element_type=F32)


def tie(value, *before):
    return pl.pallas_call(
        lambda *refs: None,
        in_specs=[ANY] * (1 + len(before)),
        out_specs=ANY,
        out_shape=shape(value.shape, value.dtype),
        input_output_aliases={0: 0},
        compiler_params=pltpu.CompilerParams(vmem_limit_bytes=GRANT),
        cost_estimate=LONG,
    )(value, *before)


def pause(*before):
    return pl.pallas_call(
        lambda *refs: None,
        in_specs=[ANY] * len(before),
        out_specs=ANY,
        out_shape=shape((8, PAIR), F32),
        cost_estimate=LONG,
    )(*before)


class Order:
    def __init__(self, me):
        self.me, self.last = me, ()

    def then(self, value):
        self.last = (pause(*self.last),)
        value = tie(value, *self.last)
        self.last = (value,)
        return value

    def now(self, *values):
        self.last = tuple(values)


def call(body, order, args, outs, in_specs, out_specs, grid, scratch=(), alias=None):
    count, after = len(args), order.last

    def run(*refs):
        body(*refs[:count], *refs[count + len(after) :])

    result = pl.pallas_call(
        run,
        grid=grid,
        in_specs=list(in_specs) + [ANY] * len(after),
        out_specs=list(out_specs),
        out_shape=outs,
        scratch_shapes=list(scratch),
        input_output_aliases=alias or {},
        compiler_params=pltpu.CompilerParams(vmem_limit_bytes=GRANT),
        cost_estimate=LONG,
    )(*args, *after)
    order.now(result[0])
    return result


def everything(array):
    return [(slice(None),) * len(array.shape)]


def by_rows(array):
    return [(slice(i, i + ROWS), slice(None)) for i in range(0, array.shape[0], ROWS)]


def by_columns(array, width):
    return [(slice(None), slice(i, i + width)) for i in range(0, array.shape[1], width)]


class Stream:
    def __init__(self, ins, in_parts, out_parts, far, near, sems, queue, always):
        self.always = always
        self.in_far, self.out_far = far[:ins], far[ins:]
        self.ins, self.outs = near[:ins], near[ins:]
        self.in_parts, self.out_parts = in_parts, out_parts
        self.in_sems, self.out_sems = sems[:ins], sems[ins:]
        self.queue, self.started, self.waited, self.flying, self.sent = queue, 0, set(), 0, []
        self.top_up()

    def fetch(self, k, c):
        at = self.in_parts[k][c]
        return pltpu.make_async_copy(self.in_far[k].at[at], self.ins[k].at[at], self.in_sems[k].at[c])

    def size(self, k, c):
        return math.prod(self.ins[k].at[self.in_parts[k][c]].shape) * self.ins[k].dtype.itemsize

    def start_next(self):
        k, c = self.queue[self.started]
        self.fetch(k, c).start()
        self.flying += self.size(k, c)
        self.started += 1

    def top_up(self):
        while self.started < len(self.queue) and self.flying < FLYING:
            self.start_next()

    def need(self, k, c=0):
        if (k, c) not in self.waited:
            self.waited.add((k, c))
            while (k, c) not in self.queue[: self.started]:
                self.start_next()
            self.fetch(k, c).wait()
            self.flying -= self.size(k, c)
            self.top_up()
        return self.ins[k]

    def step(self, needs, emits, work):
        for k, c in needs:
            self.need(k, c)
        pl.when(self.always)(work)
        for k, c in emits:
            self.emit(k, c)

    def emit(self, k, c=0):
        at = self.out_parts[k][c]
        copy = pltpu.make_async_copy(self.outs[k].at[at], self.out_far[k].at[at], self.out_sems[k].at[c])
        copy.start()
        self.sent.append(copy)


def stream(body, order, ins, outs, scratch=()):
    smem = (order.me,)
    arrays = [i[0] for i in ins]
    in_parts, out_parts = [i[1] for i in ins], [o[1] for o in outs]
    after, n_in, n_out = order.last, len(ins), len(outs)
    queue = [(c, k) for k, p in enumerate(in_parts) for c in range(len(p))]
    queue = [(k, c) for late, c, k in sorted((len(ins[k]) > 2, c, k) for c, k in queue)]

    def run(*refs):
        small, refs = refs[: len(smem)], refs[len(smem) :]
        far_in, refs = refs[:n_in], refs[n_in + len(after) :]
        far_out, refs = refs[:n_out], refs[n_out:]
        near, refs = refs[: n_in + n_out], refs[n_in + n_out :]
        sems, rest = refs[: n_in + n_out], refs[n_in + n_out :]
        io = Stream(n_in, in_parts, out_parts, far_in + far_out, near, sems, queue, small[0][0] >= 0)
        body(io, small[0][0], *rest)
        for k, c in queue:
            io.need(k, c)
        for copy in io.sent:
            copy.wait()

    result = pl.pallas_call(
        run,
        in_specs=[SMEM] * len(smem) + [ANY] * (n_in + len(after)),
        out_specs=[ANY] * n_out,
        out_shape=[o[0] for o in outs],
        scratch_shapes=[pltpu.VMEM(a.shape, a.dtype) for a in arrays]
        + [pltpu.VMEM(o[0].shape, o[0].dtype) for o in outs]
        + [pltpu.SemaphoreType.DMA((len(p),)) for p in in_parts + out_parts]
        + list(scratch),
        compiler_params=pltpu.CompilerParams(vmem_limit_bytes=GRANT),
        cost_estimate=LONG,
    )(*smem, *arrays, *after)
    order.now(result[0])
    return result


def whole(*dims):
    return pl.BlockSpec(dims, lambda *i: (0,) * len(dims))


def row_blocks(tokens):
    return [slice(i, i + ROWS) for i in range(0, tokens, ROWS)]


def swap_x(value):
    return lax.ppermute(value, "tensor", [(0, 1), (1, 0)])


def swap_dp(value, bit, n):
    return lax.ppermute(value, "dp", [(i, i ^ bit) for i in range(n)])


def index_of(me, bits):
    total = 0
    for j, bit in enumerate(bits):
        total = total + jnp.where(jnp.bitwise_and(me, bit) != 0, 1 << j, 0)
    return total


class Gather:
    def __init__(self, mine, bits, n):
        self.bits, self.n = bits, n
        self.pieces = {0: swap_x(mine)}

    def hop(self, order, slot, *steps):
        self.pieces[slot] = order.then(self.pieces[slot])
        for j in steps:
            self.pieces[slot | (1 << j)] = swap_dp(self.pieces[slot], self.bits[j], self.n)

    def place(self, order, me, outs, put):
        slots = list(self.pieces)
        dims = self.pieces[0].shape

        def body(me_ref, *refs):
            base = index_of(me_ref[0], self.bits)
            for slot, piece in zip(slots, refs):
                put(jnp.bitwise_xor(base, slot), piece, *refs[len(slots) :])

        return call(
            body,
            order,
            (me, *[self.pieces[s] for s in slots]),
            [shape(o, BF) for o in outs],
            [SMEM] + [whole(*dims)] * len(slots),
            [whole(*o) for o in outs],
            (1,))


def put_rows(place, piece, out):
    rows = piece.shape[0]
    out[pl.ds(pl.multiple_of(place * rows, rows), rows), :] = piece[...].astype(BF)


def put_with_output(place, piece, out, out_two):
    rows, width = piece.shape[0], out.shape[1]
    put_rows(place, piece.at[:, :width], out)
    few, half = rows // 2, out_two.shape[1] // 2
    at = pl.ds(pl.multiple_of(place * few, few), few)
    out_two[at, :half] = piece[:few, width:].astype(BF)
    out_two[at, half:] = piece[few:, width:].astype(BF)


class Split:
    def __init__(self, rows, width, block, n, order_of_bits):
        self.rows, self.width, self.block, self.n, self.bits = rows, width, block, n, order_of_bits
        steps = len(order_of_bits)
        self.chunks = [
            sum(bit for j, bit in enumerate(order_of_bits) if (r >> (steps - 1 - j)) & 1) for r in range(n)
        ]
        self.inside = (rows // n) % 8 == 0
        half = shape((rows // 2, width), F32)
        self.outs = [(half, by_columns(half, block))] * 2
        self.scratch = pltpu.VMEM((rows, block), F32)

    def write(self, io, first, me, full, done, left, right):
        send, keep = io.outs[first : first + 2]
        small, half = self.rows // self.n, self.rows // 2
        lanes = slice(done * self.block, (done + 1) * self.block)
        full[...] = over_rows(left, right)
        for r, chunk in enumerate(self.chunks):
            out, low = (keep, r * small) if r < self.n // 2 else (send, r * small - half)
            at = jnp.bitwise_xor(me, chunk) * small if self.inside else r * small
            at = pl.multiple_of(at, small) if self.inside else at
            out[low : low + small, lanes] = full[pl.ds(at, small), :]

    def scatter(self, me, send, keep, order):
        if not self.inside:
            wanted = jnp.bitwise_xor(me[0], jnp.array(self.chunks, jnp.int32))
            full = jnp.concatenate([keep, send], axis=0).reshape(self.n, -1, self.width)[wanted]
            full = full.reshape(self.rows, self.width)
            keep, send = full[: self.rows // 2], full[self.rows // 2 :]
        order.now(send)
        return Scatter(send, keep, self.n, self.bits)


def add_rows(order, parts, low, high):
    width = parts[0].shape[1]
    lanes = [slice(i, i + width // 2) for i in (0, width // 2)]
    out = shape((high - low, width), F32)

    def body(io, me):
        for c, lane in enumerate(lanes):

            def work():
                total = io.ins[0][low:high, lane]
                for k in range(1, len(parts)):
                    total = total + io.ins[k][low:high, lane]
                io.outs[0][:, lane] = total

            io.step([(k, c) for k in range(len(parts))], [(0, c)], work)

    ins = [(p, [(slice(low, high), lane) for lane in lanes]) for p in parts]
    return stream(body, order, ins, [(out, [(slice(None), lane) for lane in lanes])])[0]


class Scatter:
    def __init__(self, send, keep, n, order_of_bits):
        self.n, self.bits, self.step = n, order_of_bits, 0
        self.parts = [keep, swap_dp(send, self.bits[0], n)]

    def advance(self, order):
        self.step += 1
        self.parts[-1] = order.then(self.parts[-1])
        size, width = self.parts[-1].shape
        last = self.step == len(self.bits)
        low, high = (0, size) if last else (size // 2, size)
        if (high - low) % 8 == 0:
            total = add_rows(order, self.parts, low, high)
        else:
            total = self.parts[0][low:high]
            for part in self.parts[1:]:
                total = total + part[low:high]
            order.now(total)
        if last:
            self.result = total
        else:
            self.parts.append(swap_dp(total, self.bits[self.step], self.n))


def attend_body(real, x, w, bias, qkv_ref, ctx_ref, lse_ref):
    length = x.shape[0]
    qkv = (plain(x, w) + bias).astype(BF)
    qkv_ref[...] = qkv
    lane = lax.broadcasted_iota(jnp.int32, (1, PAIR), 1)
    valid = lax.broadcasted_iota(jnp.int32, (length, 1), 0) < real
    query = qkv[:, 0:PAIR] * BF(0.125)
    keys = qkv[:, PAIR : 2 * PAIR]
    values_t = qkv[:, 2 * PAIR : 3 * PAIR].T
    outs, logs = [], []
    for h in range(2):
        mine = (lane < DH) if h == 0 else (lane >= DH)
        q = jnp.where(mine, query, BF(0))
        s = against(keys, q)
        s = jnp.where(valid, s, masked_score)
        top = jnp.max(s, axis=0, keepdims=True)
        e = jnp.exp(s - top)
        total = jnp.sum(e, axis=0, keepdims=True)
        p = (e * (1.0 / total)).astype(BF)
        outs.append(plain(values_t[h * DH : (h + 1) * DH, :], p))
        logs.append(top + jnp.log(total))
    ctx_ref[...] = jnp.concatenate(outs, axis=0).T.astype(BF)
    lse_ref[0, 0] = jnp.concatenate(logs, axis=0)


def attend(order, lengths, flat, weights, biases, count, pairs, which, kept=()):
    tokens, width = flat.shape
    length = tokens // count
    own = len(weights) == 3
    first, steps = which[0], len(which)
    if own:
        w_specs = [pl.BlockSpec((width, PAIR), lambda p, s: (0, first + p))] * 3
    else:
        w_specs = [pl.BlockSpec((width, 3 * PAIR), lambda p, s: (0, p))]
    b_specs = [pl.BlockSpec((1, PAIR), lambda p, s, at=at: (0, at // PAIR + first + p)) for _, at in biases]
    many = len(weights)

    def body(len_ref, x_ref, *refs):
        ws, bs, outs = refs[:many], refs[many : many + 2], refs[many + 2 + len(kept) :]
        w = jnp.concatenate([r[...] for r in ws], axis=1) if own else ws[0][...]
        bias = jnp.concatenate([bs[0][...], jnp.zeros((1, PAIR), F32), bs[1][...]], axis=1)
        attend_body(len_ref[pl.program_id(1)], x_ref[...], w, bias, *outs)

    return call(
        body,
        order,
        (lengths, flat, *weights, *[b for b, _ in biases], *kept),
        [
            shape((tokens, 3 * PAIR * pairs), BF),
            shape((tokens, PAIR * pairs), BF),
            shape((count, pairs, 2, length), F32),
        ],
        [SMEM, pl.BlockSpec((length, width), lambda p, s: (s, 0))] + w_specs + b_specs + [ANY] * len(kept),
        [
            pl.BlockSpec((length, 3 * PAIR), lambda p, s: (s, first + p)),
            pl.BlockSpec((length, PAIR), lambda p, s: (s, first + p)),
            pl.BlockSpec((1, 1, 2, length), lambda p, s: (s, first + p, 0, 0)),
        ],
        (steps, count),
        alias={4 + many + j: j for j in range(len(kept))})


def attend_back_body(len_ref, x_ref, lse_ref, dc_ref, out_ref):
    length = x_ref.shape[0]
    real = len_ref[pl.program_id(1)]
    lane = lax.broadcasted_iota(jnp.int32, (1, PAIR), 1)
    valid = lax.broadcasted_iota(jnp.int32, (length, 1), 0) < real
    query = x_ref[:, 0:PAIR] * BF(0.125)
    keys = x_ref[:, PAIR : 2 * PAIR]
    keys_t = keys.T
    values = x_ref[:, 2 * PAIR : 3 * PAIR]
    d_ctx = dc_ref[...]
    dq, dk, dv = [], [], []
    for h in range(2):
        mine = (lane < DH) if h == 0 else (lane >= DH)
        q = jnp.where(mine, query, BF(0))
        s = against(keys, q)
        s = jnp.where(valid, s, masked_score)
        p = jnp.exp(s - lse_ref[0, 0, h : h + 1, :])
        dv.append(plain(p.astype(BF), d_ctx))
        dp = against(values, jnp.where(mine, d_ctx, BF(0)))
        row = jnp.sum(p * dp, axis=0, keepdims=True)
        ds = (p * (dp - row)).astype(BF)
        dk.append(plain(ds, query))
        dq.append(plain(keys_t[h * DH : (h + 1) * DH, :], ds))
    first = lane < DH
    out_ref[:, 0:PAIR] = (jnp.concatenate(dq, axis=0) * 0.125).T.astype(BF)
    out_ref[:, PAIR : 2 * PAIR] = jnp.where(first, dk[0], dk[1]).astype(BF)
    out_ref[:, 2 * PAIR : 3 * PAIR] = jnp.where(first, dv[0], dv[1]).astype(BF)


def attend_back(order, lengths, qkv, lse, d_ctx, count, which):
    tokens = qkv.shape[0]
    length = tokens // count
    first, steps = which[0], len(which)
    return call(
        attend_back_body,
        order,
        (lengths, qkv, lse, d_ctx),
        [shape((tokens, 3 * PAIR * steps), BF)],
        [
            SMEM,
            pl.BlockSpec((length, 3 * PAIR), lambda p, s: (s, first + p)),
            pl.BlockSpec((1, 1, 2, length), lambda p, s: (s, first + p, 0, 0)),
            pl.BlockSpec((length, PAIR), lambda p, s: (s, first + p)),
        ],
        [pl.BlockSpec((length, 3 * PAIR), lambda p, s: (s, p))],
        (steps, count))[0]


def gelu_both(value):
    phi_big = 0.5 + 0.5 * lax.erf(value * math.sqrt(0.5))
    phi_small = jnp.exp(-0.5 * value * value) * (1.0 / math.sqrt(2.0 * math.pi))
    return (value * phi_big).astype(BF), (phi_big + value * phi_small).astype(BF)


def normalize(values):
    center = values - jnp.mean(values, axis=-1, keepdims=True)
    spread = jnp.mean(center * center, axis=-1, keepdims=True)
    inverse = lax.rsqrt(spread + norm_eps)
    return center * inverse, inverse


def norm_backward(grad, normed, inverse, gain):
    scaled = grad * gain
    mean_one = jnp.mean(scaled, axis=-1, keepdims=True)
    mean_two = jnp.mean(scaled * normed, axis=-1, keepdims=True)
    return inverse * (scaled - mean_one - normed * mean_two)


def column_sum(values):
    return jnp.sum(values, axis=0, keepdims=True)


def add_to(ref, first, values):
    ref[...] = values if first else ref[...] + values


def forward_own(order, ctx, ctx_far, flat, w_output, wo_far, w_up, w_down, vec, spots):
    tokens, width = flat.shape
    hidden = w_up.shape[1]
    outs = [shape((tokens, w), BF) for w in (width, width, hidden, hidden, width)] + [shape((tokens, 1), F32)]

    def body(io, me):
        own, far, x, wo, wof, v, wu, wd = io.ins
        low_o, normed_o, act_o, slope_o, part_o, rstd_o = io.outs
        for c, r in enumerate(row_blocks(tokens)):

            def norm():
                attn = plain(own[r, :], wo[...]) + plain(far[r, :], wof[...])
                residual = x[r, :].astype(F32) + attn + spots(v, "b_output")
                normed, inverse = normalize(residual)
                normed_o[r, :] = normed.astype(BF)
                rstd_o[r, :] = inverse
                low_o[r, :] = (normed * spots(v, "gain_one") + spots(v, "shift_one")).astype(BF)

            def up():
                act, slope = gelu_both(plain(low_o[r, :], wu[...]) + spots(v, "b_up"))
                act_o[r, :] = act
                slope_o[r, :] = slope

            def down():
                part_o[r, :] = plain(act_o[r, :], wd[...]).astype(BF)

            io.step([(0, c), (1, c), (2, c), (3, 0), (4, 0), (5, 0)], [(0, c), (1, c), (5, c)], norm)
            io.step([(6, 0)], [(2, c), (3, c)], up)
            io.step([(7, 0)], [(4, c)], down)

    ins = [(a, by_rows(a)) for a in (ctx, ctx_far, flat)]
    ins += [(a, everything(a)) for a in (w_output, wo_far, vec, w_up, w_down)]
    return stream(body, order, ins, [(o, by_rows(o)) for o in outs])


def forward_far(order, low, wu_parts, wd_far, part, normed, vec, vec_far, cotangent, act_own, spots, split):
    tokens, width = low.shape
    wide, hidden = wu_parts[0].shape[1], wd_far.shape[0]
    outs = [shape((tokens, w), BF) for w in (width, width, hidden)]
    sums = shape((3, width), F32)

    def body(io, me, full, acts):
        low_r, wu_one, wu_two, vf, wd, v, part_r, normed_r, tan_r, act_r = io.ins
        dffn_o, out_o, slope_o, sums_o = io.outs[2:]
        for c, r in enumerate(row_blocks(tokens)):

            def up():
                bias = spots(vf, "b_up")
                for j, wu in enumerate((wu_one, wu_two)):
                    lanes = slice(j * wide, (j + 1) * wide)
                    acts[:, lanes], slope_o[r, lanes] = gelu_both(plain(low_r[r, :], wu[...]) + bias[:, lanes])

            def down():
                ffn = part_r[r, :].astype(F32) + plain(acts[...], wd[...]) + spots(v, "b_down")
                first = normed_r[r, :].astype(F32) * spots(v, "gain_one") + spots(v, "shift_one")
                normed_two, inverse = normalize(first + ffn)
                gain = spots(v, "gain_two")
                out_o[r, :] = (normed_two * gain + spots(v, "shift_two")).astype(BF)
                tangent = tan_r[r, :].astype(F32)
                d_second = norm_backward(tangent, normed_two, inverse, gain)
                dffn_o[r, :] = d_second.astype(BF)
                more = [column_sum(d_second), column_sum(tangent * normed_two), column_sum(tangent)]
                add_to(sums_o, c == 0, jnp.concatenate(more, axis=0))

            io.step([(0, c), (1, 0), (2, 0), (3, 0)], [(4, c)], up)
            io.step([(4, 0), (5, 0), (6, c), (7, c), (8, c)], [(2, c), (3, c)], down)
        io.emit(5)
        for j in range(split.width // split.block):
            lanes = slice(j * split.block, (j + 1) * split.block)
            work = functools.partial(lambda j, lanes: split.write(io, 0, me, full, j, dffn_o[...], act_r[:, lanes]), j, lanes)
            io.step([(9, j)], [(0, j), (1, j)], work)

    ins = [(low, by_rows(low))] + [(a, everything(a)) for a in (*wu_parts, vec_far, wd_far, vec)]
    ins += [(a, by_rows(a)) for a in (part, normed, cotangent)] + [(act_own, by_columns(act_own, split.block), True)]
    outs = split.outs + [(o, by_rows(o)) for o in outs] + [(sums, everything(sums))]
    return stream(body, order, ins, outs, [split.scratch, pltpu.VMEM((ROWS, hidden), BF)])


def backward_own(order, d_ffn, slope, w_up, w_down, low, split):
    tokens, width = d_ffn.shape
    hidden = w_up.shape[1]

    def body(io, me, full, d_pres):
        d, wd, slope_r, wu, low_r = io.ins
        part_o, sums_o = io.outs[2:]
        for c, r in enumerate(row_blocks(tokens)):

            def pre():
                d_pre = (against(d[r, :], wd[...]) * slope_r[r, :].astype(F32)).astype(BF)
                d_pres[r, :] = d_pre
                add_to(sums_o, c == 0, column_sum(d_pre.astype(F32)))

            def first():
                part_o[r, :] = against(d_pres[r, :], wu[...]).astype(BF)

            io.step([(0, c), (1, 0), (2, c)], [], pre)
            io.step([(3, 0)], [(2, c)], first)
        io.emit(3)
        for j in range(split.width // split.block):
            lanes = slice(j * split.block, (j + 1) * split.block)
            work = functools.partial(lambda j, lanes: split.write(io, 0, me, full, j, low_r[...], d_pres[:, lanes]), j, lanes)
            io.step([(4, 0)], [(0, j), (1, j)], work)

    ins = [(d_ffn, by_rows(d_ffn)), (w_down, everything(w_down)), (slope, by_rows(slope))]
    ins += [(w_up, everything(w_up)), (low, everything(low), True)]
    part, sums = shape((tokens, width), BF), shape((1, hidden), F32)
    outs = split.outs + [(part, by_rows(part)), (sums, everything(sums))]
    return stream(body, order, ins, outs, [split.scratch, pltpu.VMEM((tokens, hidden), BF)])


def backward_far(order, d_ffn, slope, wu_parts, wd_far, part, normed, inverse, w_output, wo_far, vec, spots):
    tokens, width = d_ffn.shape
    local, wide, hidden = w_output.shape[0], wu_parts[0].shape[1], wd_far.shape[0]

    def body(io, me, d_pres):
        d, wd, slope_r, wu_one, wu_two, part_r, norm, inv, wo, wof, v = io.ins
        dattn_o, dctx_o, dfar_o, sums_o = io.outs
        for c, r in enumerate(row_blocks(tokens)):

            def pre():
                d_pres[...] = (against(d[r, :], wd[...]) * slope_r[r, :].astype(F32)).astype(BF)

            def first():
                d_first = d[r, :].astype(F32) + part_r[r, :].astype(F32)
                for j, wu in enumerate((wu_one, wu_two)):
                    d_first = d_first + against(d_pres[:, j * wide : (j + 1) * wide], wu[...])
                normed_one = norm[r, :].astype(F32)
                d_res = norm_backward(d_first, normed_one, inv[r, :], spots(v, "gain_one"))
                dattn_o[r, :] = d_res.astype(BF)
                more = [column_sum(d_res), column_sum(d_first * normed_one), column_sum(d_first)]
                add_to(sums_o, c == 0, jnp.concatenate(more, axis=0))

            def heads():
                dctx_o[r, :] = against(dattn_o[r, :], wo[...]).astype(BF)
                dfar_o[r, :] = against(dattn_o[r, :], wof[...]).astype(BF)

            io.step([(0, c), (1, 0), (2, c)], [], pre)
            io.step([(3, 0), (4, 0), (5, c), (6, c), (7, c), (10, 0)], [(0, c)], first)
            io.step([(8, 0), (9, 0)], [(1, c), (2, c)], heads)
        io.emit(3)

    ins = [(d_ffn, by_rows(d_ffn)), (wd_far, everything(wd_far)), (slope, by_rows(slope))]
    ins += [(a, everything(a)) for a in wu_parts]
    ins += [(a, by_rows(a)) for a in (part, normed, inverse)]
    ins += [(a, everything(a)) for a in (w_output, wo_far, vec)]
    outs = [shape((tokens, w), BF) for w in (width, local, local)]
    sums = shape((3, width), F32)
    outs = [(o, by_rows(o)) for o in outs] + [(sums, everything(sums))]
    return stream(body, order, ins, outs, [pltpu.VMEM((ROWS, hidden), BF)])


def weight_grad(order, pairs, split):
    ins, sums = [], shape((1, split.width), F32)
    for left, right in pairs:
        ins += [(left, everything(left)), (right, by_columns(right, split.block))]

    def body(io, me, full):
        done = 0
        for p, (_, right) in enumerate(pairs):
            for c in range(right.shape[1] // split.block):

                def work(p, c, done):
                    block = io.ins[2 * p + 1][:, c * split.block : (c + 1) * split.block]
                    lanes = slice(done * split.block, (done + 1) * split.block)
                    io.outs[2][:, lanes] = column_sum(block.astype(F32))
                    split.write(io, 0, me, full, done, io.ins[2 * p][...], block)

                work = functools.partial(work, p, c, done)
                io.step([(2 * p, 0), (2 * p + 1, c)], [(0, done), (1, done)], work)
                done += 1
        io.emit(2)

    outs = split.outs + [(sums, everything(sums))]
    return stream(body, order, ins, outs, [split.scratch])


def small_call(body, order, args, out):
    return pl.pallas_call(
        lambda *refs: body(*refs[: len(args)], refs[-1]),
        in_specs=[VMEM] * len(args) + [ANY] * len(order.last),
        out_specs=VMEM,
        out_shape=out,
        compiler_params=pltpu.CompilerParams(vmem_limit_bytes=GRANT),
        cost_estimate=LONG,
    )(*args, *order.last)


def line_up_sums(order, parts):
    total = sum(v.shape[0] * (v.shape[1] - first) for v, first in parts)

    def body(*refs):
        at = 0
        for ref, (v, first) in zip(refs, parts):
            for row in range(v.shape[0]):
                size = v.shape[1] - first
                refs[-1][:, at : at + size] = ref[row : row + 1, first:]
                at += size

    result = small_call(body, order, [v for v, _ in parts], shape((1, total), F32))
    order.now(result)
    return result


def add_two(order, left, right):
    def body(a, b, out):
        out[...] = a[...] + b[...]

    result = small_call(body, order, [left, right], shape(left.shape, F32))
    order.now(result)
    return result


def inputs_grad(order, d_res, grads, w_own, w_far):
    tokens, width = d_res.shape
    pairs = w_own[0].shape[1] // PAIR
    wide = 6 * PAIR * pairs
    after, many, blocks = order.last, len(grads), tokens // ROWS

    def body(me_ref, *refs):
        always = me_ref[0] >= 0
        res_far, gs, (wq, wk, wv) = refs[0], refs[1 : 1 + many], refs[1 + many : 4 + many]
        wfs = refs[4 + many : 4 + many + len(w_far)]
        out_far, res, g_all, w_all, out, w_sem, g_sem, res_sem, out_sem = refs[4 + many + len(w_far) + len(after) :]
        w_copies, g_copies = [], []
        for p in range(pairs):
            for j, w in enumerate((wq, wk, wv)):
                at = (3 * p + j) * PAIR
                src, dst = w.at[:, p * PAIR : (p + 1) * PAIR], w_all.at[:, at : at + PAIR]
                w_copies.append(pltpu.make_async_copy(src, dst, w_sem.at[3 * p + j]))
        at = wide // 2
        for k, w in enumerate(wfs):
            size = w.shape[1]
            w_copies.append(pltpu.make_async_copy(w, w_all.at[:, at : at + size], w_sem.at[3 * pairs + k]))
            at += size
        for c, r in enumerate(row_blocks(tokens)):
            at, copies = 0, []
            for k, g in enumerate(gs):
                size = g.shape[1]
                copies.append(pltpu.make_async_copy(g.at[r, :], g_all.at[r, at : at + size], g_sem.at[c, k]))
                at += size
            copies.append(pltpu.make_async_copy(res_far.at[r, :], res.at[r, :], res_sem.at[c]))
            g_copies.append(copies)
        for copy in w_copies + [x for copies in g_copies for x in copies]:
            copy.start()
        for copy in w_copies:
            copy.wait()
        sent = []
        for c, r in enumerate(row_blocks(tokens)):
            for copy in g_copies[c]:
                copy.wait()

            @pl.when(always)
            def _():
                out[r, :] = (res[r, :].astype(F32) + against(g_all[r, :], w_all[...])).astype(BF)

            sent.append(pltpu.make_async_copy(out.at[r, :], out_far.at[r, :], out_sem.at[c]))
            sent[-1].start()
        for copy in sent:
            copy.wait()

    result = pl.pallas_call(
        body,
        in_specs=[SMEM] + [ANY] * (4 + many + len(w_far) + len(after)),
        out_specs=ANY,
        out_shape=shape((tokens, width), BF),
        scratch_shapes=[
            pltpu.VMEM((tokens, width), BF),
            pltpu.VMEM((tokens, wide), BF),
            pltpu.VMEM((width, wide), BF),
            pltpu.VMEM((tokens, width), BF),
            pltpu.SemaphoreType.DMA((3 * pairs + len(w_far),)),
            pltpu.SemaphoreType.DMA((blocks, many)),
            pltpu.SemaphoreType.DMA((blocks,)),
            pltpu.SemaphoreType.DMA((blocks,)),
        ],
        compiler_params=pltpu.CompilerParams(vmem_limit_bytes=GRANT),
        cost_estimate=LONG,
    )(order.me, d_res, *grads, *w_own, *w_far, *after)
    order.now(result)
    return result


def per_device(
    inputs,
    lengths,
    w_query,
    b_query,
    w_key,
    w_value,
    b_value,
    w_output,
    b_output,
    gain_one,
    shift_one,
    w_up,
    b_up,
    w_down,
    b_down,
    gain_two,
    shift_two,
    cotangent,
    *,
    n,
):
    count, length, width = inputs.shape
    local, hidden = w_query.shape[1], w_up.shape[1]
    pairs = local // PAIR
    tokens = count * length
    flat = inputs.reshape(tokens, width)
    tangent = cotangent.reshape(tokens, width)
    me = lax.axis_index("dp").astype(jnp.int32).reshape(1)
    names = ("b_up", "b_query", "b_value", "b_output", "gain_one", "shift_one", "b_down", "gain_two", "shift_two")
    given = (b_up, b_query, b_value, b_output, gain_one, shift_one, b_down, gain_two, shift_two)
    offsets, at = {}, 0
    for name, v in zip(names, given):
        offsets[name] = (at, v.shape[0])
        at += v.shape[0]

    def line_up(*refs):
        for name, ref in zip(names, refs):
            start, size = offsets[name]
            refs[-1][:, start : start + size] = ref[...].astype(F32).reshape(1, size)

    vec = pl.pallas_call(
        line_up,
        in_specs=[VMEM] * len(given),
        out_specs=VMEM,
        out_shape=shape((1, at), F32),
    )(*given)

    def spots(ref, name):
        start, size = offsets[name]
        return ref[:, start : start + size]

    y_bits, z_bits = (1, 2), (1, 4)
    quarter, half, few = width // 4, hidden // 2, local // 4

    def prepare(me_ref, wqy, wky, wvy, wq, wk, wv, wo, wd, wuy, wuz, one, two, down, up_one, up_two):
        def heads(w3, p, out, at):
            for j, w in enumerate(w3):
                out[:, at + j * PAIR : at + (j + 1) * PAIR] = w[:, p * PAIR : (p + 1) * PAIR].astype(F32)

        heads((wqy, wky, wvy), 0, one, 0)
        for p in range(1, pairs):
            heads((wq, wk, wv), p, two, 3 * PAIR * (p - 1))
        rest = 3 * PAIR * (pairs - 1)
        two[:few, rest:] = wo[:, : width // 2].astype(F32)
        two[few:, rest:] = wo[:, width // 2 :].astype(F32)
        down[...] = wd[...].astype(F32)
        up_one[...] = wuy[...].astype(F32)
        up_two[...] = wuz[...].astype(F32)

    def piece(rows, cols, which, col=0):
        return pl.BlockSpec((rows, cols), lambda i, m: (index_of(m[0], which), col))

    def single(rows, cols):
        return pl.BlockSpec((rows, cols), lambda i, m: (0, 0))

    d_bits, d_rows = (1, 2, 4), hidden // 8
    sizes = [(quarter, 3 * PAIR), (quarter, 3 * PAIR * (pairs - 1) + width // 2), (d_rows, width)] + [(quarter, half)] * 2
    own_w = (w_query, w_key, w_value)
    sends = pl.pallas_call(
        prepare,
        grid_spec=pltpu.PrefetchScalarGridSpec(
            num_scalar_prefetch=1,
            grid=(1,),
            in_specs=[piece(quarter, local, y_bits)] * 3
            + [piece(quarter, local, z_bits)] * 3
            + [piece(few, width, z_bits), piece(d_rows, width, d_bits)]
            + [piece(quarter, half, y_bits), piece(quarter, half, y_bits, 1)],
            out_specs=[single(*s) for s in sizes],
        ),
        out_shape=[shape(s, F32) for s in sizes],
        compiler_params=pltpu.CompilerParams(vmem_limit_bytes=GRANT),
        cost_estimate=LONG,
    )(me, *own_w, *own_w, w_output, w_down, w_up, w_up)
    vec_far = swap_x(vec)
    all_bits = (y_bits, z_bits, d_bits, y_bits, y_bits)
    one, two, down, up_one, up_two = [Gather(v, b, n) for v, b in zip(sends, all_bits)]

    order = Order(me)
    order.now(sends[0])
    bias_at = [offsets["b_query"][0], offsets["b_value"][0]]
    own_bias = [(vec, a) for a in bias_at]

    own = attend(order, lengths, flat, own_w, own_bias, count, pairs, (0,))
    vec_far = order.then(vec_far)
    qkv, ctx, lse = attend(order, lengths, flat, own_w, own_bias, count, pairs, range(1, pairs), own)
    one.hop(order, 0, 1, 0)
    far_bias = [(vec_far, a) for a in bias_at]
    one.hop(order, 1)
    one.hop(order, 2, 0)
    one.hop(order, 3)
    w_one = one.place(order, me, [(width, 3 * PAIR)], put_rows)
    two.hop(order, 0, 1, 0)
    far = attend(order, lengths, flat, w_one, far_bias, count, pairs, (0,))
    two.hop(order, 1)
    down.hop(order, 0, 1, 2, 0)
    down.hop(order, 1)
    up_one.hop(order, 0, 1, 0)
    two.hop(order, 2, 0)
    up_one.hop(order, 1)
    down.hop(order, 2, 2, 0)
    two.hop(order, 3)
    w_two, wo_far = two.place(order, me, [(width, 3 * PAIR * (pairs - 1)), (local, width)], put_with_output)
    up_two.hop(order, 0, 1, 0)
    down.hop(order, 3)
    far = attend(order, lengths, flat, (w_two,), far_bias, count, pairs, range(1, pairs), far)
    qkv_far, ctx_far, lse_far = far
    up_two.hop(order, 1)
    down.hop(order, 4, 0)
    up_one.hop(order, 2, 0)
    low, normed, act, slope, part, inverse = forward_own(
        order, ctx, ctx_far, flat, w_output, wo_far, w_up, w_down, vec, spots
    )
    down.hop(order, 5)
    down.hop(order, 6, 0)
    up_one.hop(order, 3)
    wu_one = up_one.place(order, me, [(width, half)], put_rows)
    up_two.hop(order, 2, 0)
    down.hop(order, 7)
    (wd_far,) = down.place(order, me, [(hidden, width)], put_rows)
    up_two.hop(order, 3)
    wu_far = (*wu_one, *up_two.place(order, me, [(width, half)], put_rows))

    bits = [1 << i for i in range(n.bit_length() - 1)]
    y_first = tuple(bits)
    z_first = (bits[0], bits[2], bits[1]) + tuple(bits[3:])
    block = WIDE if hidden % WIDE == 0 else hidden
    down_split, up_split = Split(width, hidden, block, n, y_first), Split(width, hidden, block, n, z_first)
    group_splits = [Split(width, 6 * PAIR, 3 * PAIR, n, bits_of) for bits_of in (y_first, z_first)]
    send, keep, d_ffn, layer_out, slope_far, sums_two = forward_far(
        order, low, wu_far, wd_far, part, normed, vec, vec_far, tangent, act, spots, down_split
    )
    down_sum = down_split.scatter(me, send, keep, order)
    send, keep, d_part, sums_up = backward_own(order, d_ffn, slope, w_up, w_down, low, up_split)
    up_sum = up_split.scatter(me, send, keep, order)

    class Vectors:
        def __init__(self, parts):
            self.value, self.step = line_up_sums(order, parts), 0
            self.send()

        def send(self):
            self.arriving = swap_dp(self.value, bits[self.step], n)
            self.step += 1

        def advance(self):
            self.value = add_two(order, self.value, order.then(self.arriving))
            if self.step < len(bits):
                self.send()

    early = Vectors([(sums_two, 0), (sums_up, 0)])
    down_sum.advance(order)
    up_sum.advance(order)
    early.advance()
    d_attn, d_ctx, d_ctx_far, sums_one = backward_far(
        order, d_ffn, slope_far, wu_far, wd_far, d_part, normed, inverse, w_output, wo_far, vec, spots
    )
    d_own = [attend_back(order, lengths, qkv, lse, d_ctx, count, (0,))]
    send, keep, sums_a = weight_grad(order, [(d_attn, ctx), (flat, d_own[0])], group_splits[0])
    group_one = group_splits[0].scatter(me, send, keep, order)
    down_sum.advance(order)
    up_sum.advance(order)
    group_one.advance(order)
    early.advance()
    d_own.append(attend_back(order, lengths, qkv, lse, d_ctx, count, range(1, pairs)))
    send, keep, sums_b = weight_grad(order, [(flat, d_own[1])], group_splits[1])
    group_two = group_splits[1].scatter(me, send, keep, order)
    late = Vectors([(sums_one, 0), (sums_a, local), (sums_b, 0)])
    down_sum.advance(order)
    group_two.advance(order)
    late.advance()
    d_far = [attend_back(order, lengths, qkv_far, lse_far, d_ctx_far, count, (0,))]
    up_sum.advance(order)
    group_one.advance(order)
    early.advance()
    d_far.append(attend_back(order, lengths, qkv_far, lse_far, d_ctx_far, count, range(1, pairs)))
    group_two.advance(order)
    group_one.advance(order)
    late.advance()
    grad_inputs = inputs_grad(order, d_attn, d_own + d_far, own_w, (*w_one, w_two))
    down_sum.advance(order)
    group_two.advance(order)
    late.advance()
    early.advance()
    up_sum.advance(order)
    group_one.advance(order)
    late.advance()
    group_two.advance(order)
    waiting = [down_sum, up_sum, group_one, group_two]
    for s in waiting:
        while s.step < len(bits):
            s.advance(order)
    for s in (early, late):
        while s.step < len(bits):
            s.advance()
    early, late = early.value.reshape(-1), late.value.reshape(-1)
    vectors = jnp.concatenate([late[: 3 * width], early, late[3 * width :]])
    rows = width // n
    shared = lax.dynamic_slice_in_dim(vectors[: 6 * width].reshape(6, width), me[0] * rows, rows, 1)
    shared_rows = width // n
    sum_qkv = jnp.concatenate([group_one.result[:, local:], group_two.result], axis=1).reshape(shared_rows, pairs, 3, PAIR)
    sum_b_up = vectors[6 * width : 6 * width + hidden]
    sum_bqkv = vectors[6 * width + hidden :].reshape(pairs, 3, PAIR)
    return (
        layer_out.reshape(count, length, width),
        grad_inputs.reshape(count, length, width),
        sum_qkv[:, :, 0].reshape(shared_rows, local),
        sum_bqkv[:, 0].reshape(local),
        sum_qkv[:, :, 1].reshape(shared_rows, local),
        sum_qkv[:, :, 2].reshape(shared_rows, local),
        sum_bqkv[:, 2].reshape(local),
        group_one.result[:, :local].T,
        shared[0],
        shared[1],
        shared[2],
        up_sum.result,
        sum_b_up,
        down_sum.result.T,
        shared[3],
        shared[4],
        shared[5],
    )


def solution(mesh):
    in_specs = (
        P("dp", None, None),
        P("dp"),
        P(None, "tensor"),
        P("tensor"),
        P(None, "tensor"),
        P(None, "tensor"),
        P("tensor"),
        P("tensor", None),
        P(),
        P(),
        P(),
        P(None, "tensor"),
        P("tensor"),
        P("tensor", None),
        P(),
        P(),
        P(),
        P("dp", None, None),
    )
    out_specs = (
        P("dp", None, None),
        P("dp", None, None),
        P("dp", "tensor"),
        P("tensor"),
        P("dp", "tensor"),
        P("dp", "tensor"),
        P("tensor"),
        P("tensor", "dp"),
        P("dp"),
        P("dp"),
        P("dp"),
        P("dp", "tensor"),
        P("tensor"),
        P("tensor", "dp"),
        P("dp"),
        P("dp"),
        P("dp"),
    )
    return jax.shard_map(
        functools.partial(per_device, n=mesh.shape["dp"]),
        mesh=mesh,
        in_specs=in_specs,
        out_specs=out_specs,
        check_vma=False,
    )
```

```python
import functools
import math

import jax
import jax.numpy as jnp
from jax import lax
from jax.experimental import pallas as pl
from jax.experimental.pallas import tpu as pltpu
from jax.sharding import PartitionSpec as P

DH = 64
PAIR = 2 * DH
PLAN = ('D', 'U', 'E', 'B2', 'O0', 'G1', 'D', 'U', 'A', 'O1', 'G2', 'D', 'U', 'B', 'L', 'FA', 'A', 'B', 'L1', 'IG', 'D', 'U', 'A', 'B', 'L2', 'A', 'B', 'L3')
ROWS = 512
WIDE = 512
GRANT = 60 * 1024 * 1024
FLYING = 6 * 1024 * 1024
LONG = pl.CostEstimate(flops=10**13, bytes_accessed=10**6, transcendentals=0)

norm_eps = 1e-12
masked_score = -1000000000.0
BF = jnp.bfloat16
F32 = jnp.float32
SMEM = pl.BlockSpec(memory_space=pltpu.SMEM)
VMEM = pl.BlockSpec(memory_space=pltpu.VMEM)
ANY = pl.BlockSpec(memory_space=pl.ANY)


def shape(dims, kind):
    return jax.ShapeDtypeStruct(tuple(dims), kind)


def against(left, right):
    return lax.dot_general(left, right, (((1,), (1,)), ((), ())), preferred_element_type=F32)


def over_rows(left, right):
    return lax.dot_general(left, right, (((0,), (0,)), ((), ())), preferred_element_type=F32)


def plain(left, right):
    return jnp.dot(left, right, preferred_element_type=F32)


def tie(value, *before):
    return pl.pallas_call(
        lambda *refs: None,
        in_specs=[ANY] * (1 + len(before)),
        out_specs=ANY,
        out_shape=shape(value.shape, value.dtype),
        input_output_aliases={0: 0},
        compiler_params=pltpu.CompilerParams(vmem_limit_bytes=GRANT),
        cost_estimate=LONG,
    )(value, *before)


def pause(*before):
    return pl.pallas_call(
        lambda *refs: None,
        in_specs=[ANY] * len(before),
        out_specs=ANY,
        out_shape=shape((8, PAIR), F32),
        cost_estimate=LONG,
    )(*before)


class Order:
    def __init__(self, me):
        self.me, self.last = me, ()

    def then(self, value):
        self.last = (pause(*self.last),)
        value = tie(value, *self.last)
        self.last = (value,)
        return value

    def now(self, *values):
        self.last = tuple(values)


def call(body, order, args, outs, in_specs, out_specs, grid, scratch=(), alias=None):
    count, after = len(args), order.last

    def run(*refs):
        body(*refs[:count], *refs[count + len(after) :])

    result = pl.pallas_call(
        run,
        grid=grid,
        in_specs=list(in_specs) + [ANY] * len(after),
        out_specs=list(out_specs),
        out_shape=outs,
        scratch_shapes=list(scratch),
        input_output_aliases=alias or {},
        compiler_params=pltpu.CompilerParams(vmem_limit_bytes=GRANT),
        cost_estimate=LONG,
    )(*args, *after)
    order.now(result[0])
    return result


def everything(array):
    return [(slice(None),) * len(array.shape)]


def by_rows(array):
    return [(slice(i, i + ROWS), slice(None)) for i in range(0, array.shape[0], ROWS)]


def by_columns(array, width):
    return [(slice(None), slice(i, i + width)) for i in range(0, array.shape[1], width)]


class Stream:
    def __init__(self, ins, in_parts, out_parts, far, near, sems, queue, always):
        self.always = always
        self.in_far, self.out_far = far[:ins], far[ins:]
        self.ins, self.outs = near[:ins], near[ins:]
        self.in_parts, self.out_parts = in_parts, out_parts
        self.in_sems, self.out_sems = sems[:ins], sems[ins:]
        self.queue, self.started, self.waited, self.flying, self.sent = queue, 0, set(), 0, []
        self.top_up()

    def fetch(self, k, c):
        at = self.in_parts[k][c]
        return pltpu.make_async_copy(self.in_far[k].at[at], self.ins[k].at[at], self.in_sems[k].at[c])

    def size(self, k, c):
        return math.prod(self.ins[k].at[self.in_parts[k][c]].shape) * self.ins[k].dtype.itemsize

    def start_next(self):
        k, c = self.queue[self.started]
        self.fetch(k, c).start()
        self.flying += self.size(k, c)
        self.started += 1

    def top_up(self):
        while self.started < len(self.queue) and self.flying < FLYING:
            self.start_next()

    def need(self, k, c=0):
        if (k, c) not in self.waited:
            self.waited.add((k, c))
            while (k, c) not in self.queue[: self.started]:
                self.start_next()
            self.fetch(k, c).wait()
            self.flying -= self.size(k, c)
            self.top_up()
        return self.ins[k]

    def step(self, needs, emits, work):
        for k, c in needs:
            self.need(k, c)
        pl.when(self.always)(work)
        for k, c in emits:
            self.emit(k, c)

    def emit(self, k, c=0):
        at = self.out_parts[k][c]
        copy = pltpu.make_async_copy(self.outs[k].at[at], self.out_far[k].at[at], self.out_sems[k].at[c])
        copy.start()
        self.sent.append(copy)


def stream(body, order, ins, outs, scratch=()):
    smem = (order.me,)
    arrays = [i[0] for i in ins]
    in_parts, out_parts = [i[1] for i in ins], [o[1] for o in outs]
    after, n_in, n_out = order.last, len(ins), len(outs)
    queue = [(c, k) for k, p in enumerate(in_parts) for c in range(len(p))]
    queue = [(k, c) for late, c, k in sorted((len(ins[k]) > 2, c, k) for c, k in queue)]

    def run(*refs):
        small, refs = refs[: len(smem)], refs[len(smem) :]
        far_in, refs = refs[:n_in], refs[n_in + len(after) :]
        far_out, refs = refs[:n_out], refs[n_out:]
        near, refs = refs[: n_in + n_out], refs[n_in + n_out :]
        sems, rest = refs[: n_in + n_out], refs[n_in + n_out :]
        io = Stream(n_in, in_parts, out_parts, far_in + far_out, near, sems, queue, small[0][0] >= 0)
        body(io, small[0][0], *rest)
        for k, c in queue:
            io.need(k, c)
        for copy in io.sent:
            copy.wait()

    result = pl.pallas_call(
        run,
        in_specs=[SMEM] * len(smem) + [ANY] * (n_in + len(after)),
        out_specs=[ANY] * n_out,
        out_shape=[o[0] for o in outs],
        scratch_shapes=[pltpu.VMEM(a.shape, a.dtype) for a in arrays]
        + [pltpu.VMEM(o[0].shape, o[0].dtype) for o in outs]
        + [pltpu.SemaphoreType.DMA((len(p),)) for p in in_parts + out_parts]
        + list(scratch),
        compiler_params=pltpu.CompilerParams(vmem_limit_bytes=GRANT),
        cost_estimate=LONG,
    )(*smem, *arrays, *after)
    order.now(result[0])
    return result


def whole(*dims):
    return pl.BlockSpec(dims, lambda *i: (0,) * len(dims))


def row_blocks(tokens):
    return [slice(i, i + ROWS) for i in range(0, tokens, ROWS)]


def swap_x(value):
    return lax.ppermute(value, "tensor", [(0, 1), (1, 0)])


def swap_dp(value, bit, n):
    return lax.ppermute(value, "dp", [(i, i ^ bit) for i in range(n)])


def index_of(me, bits):
    total = 0
    for j, bit in enumerate(bits):
        total = total + jnp.where(jnp.bitwise_and(me, bit) != 0, 1 << j, 0)
    return total


class Gather:
    def __init__(self, mine, bits, n):
        self.bits, self.n = bits, n
        self.pieces = {0: swap_x(mine)}

    def hop(self, order, slot, *steps):
        self.pieces[slot] = order.then(self.pieces[slot])
        for j in steps:
            self.pieces[slot | (1 << j)] = swap_dp(self.pieces[slot], self.bits[j], self.n)

    def place(self, order, me, outs, put):
        slots = list(self.pieces)
        dims = self.pieces[0].shape

        def body(me_ref, *refs):
            base = index_of(me_ref[0], self.bits)
            for slot, piece in zip(slots, refs):
                put(jnp.bitwise_xor(base, slot), piece, *refs[len(slots) :])

        return call(
            body,
            order,
            (me, *[self.pieces[s] for s in slots]),
            [shape(o, BF) for o in outs],
            [SMEM] + [whole(*dims)] * len(slots),
            [whole(*o) for o in outs],
            (1,))


def put_rows(place, piece, out):
    rows = piece.shape[0]
    out[pl.ds(pl.multiple_of(place * rows, rows), rows), :] = piece[...].astype(BF)


def put_with_output(place, piece, out, out_two):
    rows, width = piece.shape[0], out.shape[1]
    put_rows(place, piece.at[:, :width], out)
    few, half = rows // 2, out_two.shape[1] // 2
    at = pl.ds(pl.multiple_of(place * few, few), few)
    out_two[at, :half] = piece[:few, width:].astype(BF)
    out_two[at, half:] = piece[few:, width:].astype(BF)


class Split:
    def __init__(self, rows, width, block, n, order_of_bits):
        self.rows, self.width, self.block, self.n, self.bits = rows, width, block, n, order_of_bits
        steps = len(order_of_bits)
        self.chunks = [
            sum(bit for j, bit in enumerate(order_of_bits) if (r >> (steps - 1 - j)) & 1) for r in range(n)
        ]
        self.inside = (rows // n) % 8 == 0
        half = shape((rows // 2, width), F32)
        self.outs = [(half, by_columns(half, block))] * 2
        self.scratch = pltpu.VMEM((rows, block), F32)

    def write(self, io, first, me, full, done, left, right):
        send, keep = io.outs[first : first + 2]
        small, half = self.rows // self.n, self.rows // 2
        lanes = slice(done * self.block, (done + 1) * self.block)
        full[...] = over_rows(left, right)
        for r, chunk in enumerate(self.chunks):
            out, low = (keep, r * small) if r < self.n // 2 else (send, r * small - half)
            at = jnp.bitwise_xor(me, chunk) * small if self.inside else r * small
            at = pl.multiple_of(at, small) if self.inside else at
            out[low : low + small, lanes] = full[pl.ds(at, small), :]

    def scatter(self, me, send, keep, order):
        if not self.inside:
            wanted = jnp.bitwise_xor(me[0], jnp.array(self.chunks, jnp.int32))
            full = jnp.concatenate([keep, send], axis=0).reshape(self.n, -1, self.width)[wanted]
            full = full.reshape(self.rows, self.width)
            keep, send = full[: self.rows // 2], full[self.rows // 2 :]
        order.now(send)
        return Scatter(send, keep, self.n, self.bits)


def add_rows(order, sums):
    ins, outs, places = [], [], []
    for parts, low, high in sums:
        width = parts[0].shape[1]
        lanes = [slice(i, i + width // 2) for i in (0, width // 2)]
        out = shape((high - low, width), F32)
        places.append((len(ins), len(parts), low, high, lanes))
        ins += [(p, [(slice(low, high), lane) for lane in lanes]) for p in parts]
        outs.append((out, [(slice(None), lane) for lane in lanes]))

    def body(io, me):
        for c in range(2):
            for k, (first, count, low, high, lanes) in enumerate(places):

                def work():
                    total = io.ins[first][low:high, lanes[c]]
                    for j in range(1, count):
                        total = total + io.ins[first + j][low:high, lanes[c]]
                    io.outs[k][:, lanes[c]] = total

                io.step([(first + j, c) for j in range(count)], [(k, c)], work)

    return stream(body, order, ins, outs)


def advance(order, *scatters):
    sums = []
    for s in scatters:
        s.step += 1
        s.parts[-1] = order.then(s.parts[-1])
        size = s.parts[-1].shape[0]
        sums.append((s.parts, *((0, size) if s.step == len(s.bits) else (size // 2, size))))
    if all((high - low) % 8 == 0 for _, low, high in sums):
        totals = add_rows(order, sums)
    else:
        totals = [sum(p[low:high] for p in parts[1:]) + parts[0][low:high] for parts, low, high in sums]
        order.now(*totals)
    for s, total in zip(scatters, totals):
        if s.step == len(s.bits):
            s.result = total
        else:
            s.parts.append(swap_dp(total, s.bits[s.step], s.n))


class Scatter:
    def __init__(self, send, keep, n, order_of_bits):
        self.n, self.bits, self.step = n, order_of_bits, 0
        self.parts = [keep, swap_dp(send, self.bits[0], n)]


def by_length(real, length, work):
    quarter = length // 4
    for k in range(1, 5):
        fits = real <= quarter if k == 1 else (real > quarter * (k - 1)) & (real <= quarter * k)
        pl.when(real > quarter * 3 if k == 4 else fits)(functools.partial(work, quarter * k))


def attend_body(real, x, w, bias, qkv_ref, ctx_ref, lse_ref):
    length = x.shape[0]
    qkv_ref[...] = (plain(x, w) + bias).astype(BF)
    lane = lax.broadcasted_iota(jnp.int32, (1, PAIR), 1)

    def work(count):
        valid = lax.broadcasted_iota(jnp.int32, (count, 1), 0) < real
        query = qkv_ref[:, 0:PAIR] * BF(0.125)
        keys = qkv_ref[:count, PAIR : 2 * PAIR]
        values_t = qkv_ref[:count, 2 * PAIR : 3 * PAIR].T
        outs, logs = [], []
        for h in range(2):
            mine = (lane < DH) if h == 0 else (lane >= DH)
            q = jnp.where(mine, query, BF(0))
            s = against(keys, q)
            s = jnp.where(valid, s, masked_score)
            top = jnp.max(s, axis=0, keepdims=True)
            e = jnp.exp(s - top)
            total = jnp.sum(e, axis=0, keepdims=True)
            p = (e * (1.0 / total)).astype(BF)
            outs.append(plain(values_t[h * DH : (h + 1) * DH, :], p))
            logs.append(top + jnp.log(total))
        ctx_ref[...] = jnp.concatenate(outs, axis=0).T.astype(BF)
        lse_ref[0, 0] = jnp.concatenate(logs, axis=0)

    by_length(real, length, work)


def attend(order, lengths, flat, weights, biases, count, pairs, which, kept=()):
    tokens, width = flat.shape
    length = tokens // count
    own = len(weights) == 3
    first, steps = which[0], len(which)
    if own:
        w_specs = [pl.BlockSpec((width, PAIR), lambda p, s: (0, first + p))] * 3
    else:
        w_specs = [pl.BlockSpec((width, 3 * PAIR), lambda p, s: (0, p))]
    b_specs = [pl.BlockSpec((1, PAIR), lambda p, s, at=at: (0, at // PAIR + first + p)) for _, at in biases]
    many = len(weights)

    def body(len_ref, x_ref, *refs):
        ws, bs, outs = refs[:many], refs[many : many + 2], refs[many + 2 + len(kept) :]
        w = jnp.concatenate([r[...] for r in ws], axis=1) if own else ws[0][...]
        bias = jnp.concatenate([bs[0][...], jnp.zeros((1, PAIR), F32), bs[1][...]], axis=1)
        attend_body(len_ref[pl.program_id(1)], x_ref[...], w, bias, *outs)

    return call(
        body,
        order,
        (lengths, flat, *weights, *[b for b, _ in biases], *kept),
        [
            shape((tokens, 3 * PAIR * pairs), BF),
            shape((tokens, PAIR * pairs), BF),
            shape((count, pairs, 2, length), F32),
        ],
        [SMEM, pl.BlockSpec((length, width), lambda p, s: (s, 0))] + w_specs + b_specs + [ANY] * len(kept),
        [
            pl.BlockSpec((length, 3 * PAIR), lambda p, s: (s, first + p)),
            pl.BlockSpec((length, PAIR), lambda p, s: (s, first + p)),
            pl.BlockSpec((1, 1, 2, length), lambda p, s: (s, first + p, 0, 0)),
        ],
        (steps, count),
        alias={4 + many + j: j for j in range(len(kept))})


def attend_back_body(len_ref, x_ref, lse_ref, dc_ref, out_ref):
    length = x_ref.shape[0]
    real = len_ref[pl.program_id(1)]
    lane = lax.broadcasted_iota(jnp.int32, (1, PAIR), 1)

    def work(count):
        valid = lax.broadcasted_iota(jnp.int32, (count, 1), 0) < real
        query = x_ref[:, 0:PAIR] * BF(0.125)
        keys = x_ref[:count, PAIR : 2 * PAIR]
        keys_t = keys.T
        values = x_ref[:count, 2 * PAIR : 3 * PAIR]
        d_ctx = dc_ref[...]
        dq, dk, dv = [], [], []
        for h in range(2):
            mine = (lane < DH) if h == 0 else (lane >= DH)
            q = jnp.where(mine, query, BF(0))
            s = against(keys, q)
            s = jnp.where(valid, s, masked_score)
            p = jnp.exp(s - lse_ref[0, 0, h : h + 1, :])
            dv.append(plain(p.astype(BF), d_ctx))
            dp = against(values, jnp.where(mine, d_ctx, BF(0)))
            row = jnp.sum(p * dp, axis=0, keepdims=True)
            ds = (p * (dp - row)).astype(BF)
            dk.append(plain(ds, query))
            dq.append(plain(keys_t[h * DH : (h + 1) * DH, :], ds))
        first = lane < DH
        out_ref[:, 0:PAIR] = (jnp.concatenate(dq, axis=0) * 0.125).T.astype(BF)
        out_ref[:count, PAIR : 2 * PAIR] = jnp.where(first, dk[0], dk[1]).astype(BF)
        out_ref[:count, 2 * PAIR : 3 * PAIR] = jnp.where(first, dv[0], dv[1]).astype(BF)
        if count < length:
            out_ref[count:, PAIR : 3 * PAIR] = jnp.zeros((length - count, 2 * PAIR), BF)

    by_length(real, length, work)


def attend_back(order, lengths, qkv, lse, d_ctx, count, which):
    tokens = qkv.shape[0]
    length = tokens // count
    first, steps = which[0], len(which)
    return call(
        attend_back_body,
        order,
        (lengths, qkv, lse, d_ctx),
        [shape((tokens, 3 * PAIR * steps), BF)],
        [
            SMEM,
            pl.BlockSpec((length, 3 * PAIR), lambda p, s: (s, first + p)),
            pl.BlockSpec((1, 1, 2, length), lambda p, s: (s, first + p, 0, 0)),
            pl.BlockSpec((length, PAIR), lambda p, s: (s, first + p)),
        ],
        [pl.BlockSpec((length, 3 * PAIR), lambda p, s: (s, p))],
        (steps, count))[0]


def gelu_both(value):
    phi_big = 0.5 + 0.5 * lax.erf(value * math.sqrt(0.5))
    phi_small = jnp.exp(-0.5 * value * value) * (1.0 / math.sqrt(2.0 * math.pi))
    return (value * phi_big).astype(BF), (phi_big + value * phi_small).astype(BF)


def normalize(values):
    center = values - jnp.mean(values, axis=-1, keepdims=True)
    spread = jnp.mean(center * center, axis=-1, keepdims=True)
    inverse = lax.rsqrt(spread + norm_eps)
    return center * inverse, inverse


def norm_backward(grad, normed, inverse, gain):
    scaled = grad * gain
    mean_one = jnp.mean(scaled, axis=-1, keepdims=True)
    mean_two = jnp.mean(scaled * normed, axis=-1, keepdims=True)
    return inverse * (scaled - mean_one - normed * mean_two)


def column_sum(values):
    return jnp.sum(values, axis=0, keepdims=True)


def add_to(ref, first, values):
    ref[...] = values if first else ref[...] + values


def forward_own(order, ctx, ctx_far, flat, w_output, wo_far, w_up, w_down, vec, spots):
    tokens, width = flat.shape
    hidden = w_up.shape[1]
    outs = [shape((tokens, w), BF) for w in (width, width, hidden, hidden, width)] + [shape((tokens, 1), F32)]

    def body(io, me):
        own, far, x, wo, wof, v, wu, wd = io.ins
        low_o, normed_o, act_o, slope_o, part_o, rstd_o = io.outs
        for c, r in enumerate(row_blocks(tokens)):

            def norm():
                attn = plain(own[r, :], wo[...]) + plain(far[r, :], wof[...])
                residual = x[r, :].astype(F32) + attn + spots(v, "b_output")
                normed, inverse = normalize(residual)
                normed_o[r, :] = normed.astype(BF)
                rstd_o[r, :] = inverse
                low_o[r, :] = (normed * spots(v, "gain_one") + spots(v, "shift_one")).astype(BF)

            def up():
                act, slope = gelu_both(plain(low_o[r, :], wu[...]) + spots(v, "b_up"))
                act_o[r, :] = act
                slope_o[r, :] = slope

            def down():
                part_o[r, :] = plain(act_o[r, :], wd[...]).astype(BF)

            io.step([(0, c), (1, c), (2, c), (3, 0), (4, 0), (5, 0)], [(0, c), (1, c), (5, c)], norm)
            io.step([(6, 0)], [(2, c), (3, c)], up)
            io.step([(7, 0)], [(4, c)], down)

    ins = [(a, by_rows(a)) for a in (ctx, ctx_far, flat)]
    ins += [(a, everything(a)) for a in (w_output, wo_far, vec, w_up, w_down)]
    return stream(body, order, ins, [(o, by_rows(o)) for o in outs])


def forward_far(order, low, wu_parts, wd_far, part, normed, vec, vec_far, cotangent, act_own, spots, split):
    tokens, width = low.shape
    wide, hidden = wu_parts[0].shape[1], wd_far.shape[0]
    outs = [shape((tokens, w), BF) for w in (width, width, hidden)]
    sums = shape((3, width), F32)

    def body(io, me, full, acts):
        low_r, wu_one, wu_two, vf, wd, v, part_r, normed_r, tan_r, act_r = io.ins
        dffn_o, out_o, slope_o, sums_o = io.outs[2:]
        for c, r in enumerate(row_blocks(tokens)):

            def up():
                bias = spots(vf, "b_up")
                for j, wu in enumerate((wu_one, wu_two)):
                    lanes = slice(j * wide, (j + 1) * wide)
                    acts[:, lanes], slope_o[r, lanes] = gelu_both(plain(low_r[r, :], wu[...]) + bias[:, lanes])

            def down():
                ffn = part_r[r, :].astype(F32) + plain(acts[...], wd[...]) + spots(v, "b_down")
                first = normed_r[r, :].astype(F32) * spots(v, "gain_one") + spots(v, "shift_one")
                normed_two, inverse = normalize(first + ffn)
                gain = spots(v, "gain_two")
                out_o[r, :] = (normed_two * gain + spots(v, "shift_two")).astype(BF)
                tangent = tan_r[r, :].astype(F32)
                d_second = norm_backward(tangent, normed_two, inverse, gain)
                dffn_o[r, :] = d_second.astype(BF)
                more = [column_sum(d_second), column_sum(tangent * normed_two), column_sum(tangent)]
                add_to(sums_o, c == 0, jnp.concatenate(more, axis=0))

            io.step([(0, c), (1, 0), (2, 0), (3, 0)], [(4, c)], up)
            io.step([(4, 0), (5, 0), (6, c), (7, c), (8, c)], [(2, c), (3, c)], down)
        io.emit(5)
        for j in range(split.width // split.block):
            lanes = slice(j * split.block, (j + 1) * split.block)
            work = functools.partial(lambda j, lanes: split.write(io, 0, me, full, j, dffn_o[...], act_r[:, lanes]), j, lanes)
            io.step([(9, j)], [(0, j), (1, j)], work)

    ins = [(low, by_rows(low))] + [(a, everything(a)) for a in (*wu_parts, vec_far, wd_far, vec)]
    ins += [(a, by_rows(a)) for a in (part, normed, cotangent)] + [(act_own, by_columns(act_own, split.block), True)]
    outs = split.outs + [(o, by_rows(o)) for o in outs] + [(sums, everything(sums))]
    return stream(body, order, ins, outs, [split.scratch, pltpu.VMEM((ROWS, hidden), BF)])


def backward_own(order, d_ffn, slope, w_up, w_down, low, split):
    tokens, width = d_ffn.shape
    hidden = w_up.shape[1]

    def body(io, me, full, d_pres):
        d, wd, slope_r, wu, low_r = io.ins
        part_o, sums_o = io.outs[2:]
        for c, r in enumerate(row_blocks(tokens)):

            def pre():
                d_pre = (against(d[r, :], wd[...]) * slope_r[r, :].astype(F32)).astype(BF)
                d_pres[r, :] = d_pre
                add_to(sums_o, c == 0, column_sum(d_pre.astype(F32)))

            def first():
                part_o[r, :] = against(d_pres[r, :], wu[...]).astype(BF)

            io.step([(0, c), (1, 0), (2, c)], [], pre)
            io.step([(3, 0)], [(2, c)], first)
        io.emit(3)
        for j in range(split.width // split.block):
            lanes = slice(j * split.block, (j + 1) * split.block)
            work = functools.partial(lambda j, lanes: split.write(io, 0, me, full, j, low_r[...], d_pres[:, lanes]), j, lanes)
            io.step([(4, 0)], [(0, j), (1, j)], work)

    ins = [(d_ffn, by_rows(d_ffn)), (w_down, everything(w_down)), (slope, by_rows(slope))]
    ins += [(w_up, everything(w_up)), (low, everything(low), True)]
    part, sums = shape((tokens, width), BF), shape((1, hidden), F32)
    outs = split.outs + [(part, by_rows(part)), (sums, everything(sums))]
    return stream(body, order, ins, outs, [split.scratch, pltpu.VMEM((tokens, hidden), BF)])


def backward_far(order, d_ffn, slope, wu_parts, wd_far, part, normed, inverse, w_output, wo_far, vec, spots):
    tokens, width = d_ffn.shape
    local, wide, hidden = w_output.shape[0], wu_parts[0].shape[1], wd_far.shape[0]

    def body(io, me, d_pres):
        d, wd, slope_r, wu_one, wu_two, part_r, norm, inv, wo, wof, v = io.ins
        dattn_o, dctx_o, dfar_o, sums_o = io.outs
        for c, r in enumerate(row_blocks(tokens)):

            def pre():
                d_pres[...] = (against(d[r, :], wd[...]) * slope_r[r, :].astype(F32)).astype(BF)

            def first():
                d_first = d[r, :].astype(F32) + part_r[r, :].astype(F32)
                for j, wu in enumerate((wu_one, wu_two)):
                    d_first = d_first + against(d_pres[:, j * wide : (j + 1) * wide], wu[...])
                normed_one = norm[r, :].astype(F32)
                d_res = norm_backward(d_first, normed_one, inv[r, :], spots(v, "gain_one"))
                dattn_o[r, :] = d_res.astype(BF)
                more = [column_sum(d_res), column_sum(d_first * normed_one), column_sum(d_first)]
                add_to(sums_o, c == 0, jnp.concatenate(more, axis=0))

            def heads():
                dctx_o[r, :] = against(dattn_o[r, :], wo[...]).astype(BF)
                dfar_o[r, :] = against(dattn_o[r, :], wof[...]).astype(BF)

            io.step([(0, c), (1, 0), (2, c)], [], pre)
            io.step([(3, 0), (4, 0), (5, c), (6, c), (7, c), (10, 0)], [(0, c)], first)
            io.step([(8, 0), (9, 0)], [(1, c), (2, c)], heads)
        io.emit(3)

    ins = [(d_ffn, by_rows(d_ffn)), (wd_far, everything(wd_far)), (slope, by_rows(slope))]
    ins += [(a, everything(a)) for a in wu_parts]
    ins += [(a, by_rows(a)) for a in (part, normed, inverse)]
    ins += [(a, everything(a)) for a in (w_output, wo_far, vec)]
    outs = [shape((tokens, w), BF) for w in (width, local, local)]
    sums = shape((3, width), F32)
    outs = [(o, by_rows(o)) for o in outs] + [(sums, everything(sums))]
    return stream(body, order, ins, outs, [pltpu.VMEM((ROWS, hidden), BF)])


def weight_grad(order, pairs, split):
    ins, sums = [], shape((1, split.width), F32)
    for left, right, start, width in pairs:
        lanes = [(slice(None), slice(i, i + split.block)) for i in range(start, start + width, split.block)]
        ins += [(left, everything(left)), (right, lanes)]

    def body(io, me, full):
        done = 0
        for p, (_, _, start, width) in enumerate(pairs):
            for c in range(width // split.block):

                def work(p, c, done, start):
                    at = start + c * split.block
                    block = io.ins[2 * p + 1][:, at : at + split.block]
                    lanes = slice(done * split.block, (done + 1) * split.block)
                    io.outs[2][:, lanes] = column_sum(block.astype(F32))
                    split.write(io, 0, me, full, done, io.ins[2 * p][...], block)

                work = functools.partial(work, p, c, done, start)
                io.step([(2 * p, 0), (2 * p + 1, c)], [(0, done), (1, done)], work)
                done += 1
        io.emit(2)

    outs = split.outs + [(sums, everything(sums))]
    return stream(body, order, ins, outs, [split.scratch])


def small_call(body, order, args, out):
    return pl.pallas_call(
        lambda *refs: body(*refs[: len(args)], refs[-1]),
        in_specs=[VMEM] * len(args) + [ANY] * len(order.last),
        out_specs=VMEM,
        out_shape=out,
        compiler_params=pltpu.CompilerParams(vmem_limit_bytes=GRANT),
        cost_estimate=LONG,
    )(*args, *order.last)


def line_up_sums(order, parts):
    total = sum(v.shape[0] * (v.shape[1] - first) for v, first in parts)

    def body(*refs):
        at = 0
        for ref, (v, first) in zip(refs, parts):
            for row in range(v.shape[0]):
                size = v.shape[1] - first
                refs[-1][:, at : at + size] = ref[row : row + 1, first:]
                at += size

    result = small_call(body, order, [v for v, _ in parts], shape((1, total), F32))
    order.now(result)
    return result


def add_all(order, *values):
    def body(*refs):
        refs[-1][...] = sum(r[...] for r in refs[1:-1]) + refs[0][...]

    result = small_call(body, order, values, shape(values[0].shape, F32))
    order.now(result)
    return result


def finish_vectors(line, me, n, width, local, hidden):
    rows, heads_at = width // n, 3 * width
    late = heads_at + 3 * local
    starts = [0, width, 2 * width, late, late + width, late + 2 * width]

    def body(me_ref, line_ref, *outs):
        shift = jnp.where(me_ref[0] == 0, 0, width - me_ref[0] * rows)
        for start, out in zip(starts, outs):
            turned = pltpu.roll(jnp.broadcast_to(line_ref[:, start : start + width], (8, width)), shift, 1)
            out[...] = turned[0:1, :rows].reshape(rows)
        for j, out in ((0, outs[6]), (2, outs[7])):
            for p in range(local // PAIR):
                at = heads_at + (3 * p + j) * PAIR
                out[p * PAIR : (p + 1) * PAIR] = line_ref[:, at : at + PAIR].reshape(PAIR)
        outs[8][...] = line_ref[:, late + heads_at : late + heads_at + hidden].reshape(hidden)

    sizes = [rows] * 6 + [local] * 2 + [hidden]
    return pl.pallas_call(
        body,
        in_specs=[SMEM, VMEM],
        out_specs=[VMEM] * 9,
        out_shape=[shape((size,), F32) for size in sizes],
    )(me, line)


def finish_heads(one, two, local):
    rows = one.shape[0]

    def body(one_ref, two_ref, q, k, v, out):
        for j, ref in enumerate((q, k, v)):
            ref[:, :PAIR] = one_ref[:, local + j * PAIR : local + (j + 1) * PAIR]
            for p in range(1, local // PAIR):
                at = (3 * (p - 1) + j) * PAIR
                ref[:, p * PAIR : (p + 1) * PAIR] = two_ref[:, at : at + PAIR]
        out[...] = one_ref[:, :local].T

    return pl.pallas_call(
        body,
        in_specs=[VMEM, VMEM],
        out_specs=[VMEM] * 4,
        out_shape=[shape((rows, local), F32)] * 3 + [shape((local, rows), F32)],
    )(one, two)


def inputs_grad(order, d_res, grads, w_own, w_far):
    tokens, width = d_res.shape
    pairs = w_own[0].shape[1] // PAIR
    wide = 6 * PAIR * pairs
    after, many, blocks = order.last, len(grads), tokens // ROWS

    def body(me_ref, *refs):
        always = me_ref[0] >= 0
        res_far, gs, (wq, wk, wv) = refs[0], refs[1 : 1 + many], refs[1 + many : 4 + many]
        wfs = refs[4 + many : 4 + many + len(w_far)]
        out_far, res, g_all, w_all, out, w_sem, g_sem, res_sem, out_sem = refs[4 + many + len(w_far) + len(after) :]
        w_copies, g_copies = [], []
        for p in range(pairs):
            for j, w in enumerate((wq, wk, wv)):
                at = (3 * p + j) * PAIR
                src, dst = w.at[:, p * PAIR : (p + 1) * PAIR], w_all.at[:, at : at + PAIR]
                w_copies.append(pltpu.make_async_copy(src, dst, w_sem.at[3 * p + j]))
        at = wide // 2
        for k, w in enumerate(wfs):
            size = w.shape[1]
            w_copies.append(pltpu.make_async_copy(w, w_all.at[:, at : at + size], w_sem.at[3 * pairs + k]))
            at += size
        for c, r in enumerate(row_blocks(tokens)):
            at, copies = 0, []
            for k, g in enumerate(gs):
                size = g.shape[1]
                copies.append(pltpu.make_async_copy(g.at[r, :], g_all.at[r, at : at + size], g_sem.at[c, k]))
                at += size
            copies.append(pltpu.make_async_copy(res_far.at[r, :], res.at[r, :], res_sem.at[c]))
            g_copies.append(copies)
        for copy in w_copies + [x for copies in g_copies for x in copies]:
            copy.start()
        for copy in w_copies:
            copy.wait()
        sent = []
        for c, r in enumerate(row_blocks(tokens)):
            for copy in g_copies[c]:
                copy.wait()

            @pl.when(always)
            def _():
                out[r, :] = (res[r, :].astype(F32) + against(g_all[r, :], w_all[...])).astype(BF)

            sent.append(pltpu.make_async_copy(out.at[r, :], out_far.at[r, :], out_sem.at[c]))
            sent[-1].start()
        for copy in sent:
            copy.wait()

    result = pl.pallas_call(
        body,
        in_specs=[SMEM] + [ANY] * (4 + many + len(w_far) + len(after)),
        out_specs=ANY,
        out_shape=shape((tokens, width), BF),
        scratch_shapes=[
            pltpu.VMEM((tokens, width), BF),
            pltpu.VMEM((tokens, wide), BF),
            pltpu.VMEM((width, wide), BF),
            pltpu.VMEM((tokens, width), BF),
            pltpu.SemaphoreType.DMA((3 * pairs + len(w_far),)),
            pltpu.SemaphoreType.DMA((blocks, many)),
            pltpu.SemaphoreType.DMA((blocks,)),
            pltpu.SemaphoreType.DMA((blocks,)),
        ],
        compiler_params=pltpu.CompilerParams(vmem_limit_bytes=GRANT),
        cost_estimate=LONG,
    )(order.me, d_res, *grads, *w_own, *w_far, *after)
    order.now(result)
    return result


def per_device(
    inputs,
    lengths,
    w_query,
    b_query,
    w_key,
    w_value,
    b_value,
    w_output,
    b_output,
    gain_one,
    shift_one,
    w_up,
    b_up,
    w_down,
    b_down,
    gain_two,
    shift_two,
    cotangent,
    *,
    n,
):
    count, length, width = inputs.shape
    local, hidden = w_query.shape[1], w_up.shape[1]
    pairs = local // PAIR
    tokens = count * length
    flat = inputs.reshape(tokens, width)
    tangent = cotangent.reshape(tokens, width)
    me = lax.axis_index("dp").astype(jnp.int32).reshape(1)
    names = ("b_up", "b_query", "b_value", "b_output", "gain_one", "shift_one", "b_down", "gain_two", "shift_two")
    given = (b_up, b_query, b_value, b_output, gain_one, shift_one, b_down, gain_two, shift_two)
    offsets, at = {}, 0
    for name, v in zip(names, given):
        offsets[name] = (at, v.shape[0])
        at += v.shape[0]

    def line_up(*refs):
        for name, ref in zip(names, refs):
            start, size = offsets[name]
            refs[-1][:, start : start + size] = ref[...].astype(F32).reshape(1, size)

    vec = pl.pallas_call(
        line_up,
        in_specs=[VMEM] * len(given),
        out_specs=VMEM,
        out_shape=shape((1, at), F32),
    )(*given)

    def spots(ref, name):
        start, size = offsets[name]
        return ref[:, start : start + size]

    y_bits, z_bits = (1, 2), (1, 4)
    quarter, half, few = width // 4, hidden // 2, local // 4

    def heads(w3, p, out, at):
        for j, w in enumerate(w3):
            out[:, at + j * PAIR : at + (j + 1) * PAIR] = w[:, p * PAIR : (p + 1) * PAIR].astype(F32)

    def prepare_one(me_ref, wq, wk, wv, one):
        heads((wq, wk, wv), 0, one, 0)

    def prepare_two(me_ref, wq, wk, wv, wo, before, two):
        for p in range(1, pairs):
            heads((wq, wk, wv), p, two, 3 * PAIR * (p - 1))
        rest = 3 * PAIR * (pairs - 1)
        two[:few, rest:] = wo[:, : width // 2].astype(F32)
        two[few:, rest:] = wo[:, width // 2 :].astype(F32)

    def prepare_piece(me_ref, w, before, out):
        out[...] = w[...].astype(F32)

    def piece(rows, cols, which, col=0):
        return pl.BlockSpec((rows, cols), lambda i, m: (index_of(m[0], which), col))

    def pieces_of(body, in_specs, sizes, *args):
        return pl.pallas_call(
            body,
            grid_spec=pltpu.PrefetchScalarGridSpec(
                num_scalar_prefetch=1,
                grid=(1,),
                in_specs=in_specs,
                out_specs=[pl.BlockSpec(size, lambda i, m: (0, 0)) for size in sizes],
            ),
            out_shape=[shape(size, F32) for size in sizes],
            compiler_params=pltpu.CompilerParams(vmem_limit_bytes=GRANT),
            cost_estimate=LONG,
        )(me, *args)

    d_bits, d_rows = (1, 2, 4), hidden // 8
    own_w = (w_query, w_key, w_value)
    order = Order(me)

    def prepare(body, in_specs, size, which, *args):
        (send,) = pieces_of(body, in_specs + [ANY] * len(order.last), [size], *args, *order.last)
        order.now(send)
        return Gather(send, which, n)

    one = prepare(prepare_one, [piece(quarter, PAIR, y_bits)] * 3, (quarter, 3 * PAIR), y_bits, *own_w)
    two = prepare(
        prepare_two,
        [piece(quarter, local, z_bits)] * 3 + [piece(few, width, z_bits)],
        (quarter, 3 * PAIR * (pairs - 1) + width // 2),
        z_bits,
        *own_w,
        w_output,
    )
    vec_far = swap_x(vec)
    bias_at = [offsets["b_query"][0], offsets["b_value"][0]]
    own_bias = [(vec, a) for a in bias_at]
    own = attend(order, lengths, flat, own_w, own_bias, count, pairs, (0,))
    down = prepare(prepare_piece, [piece(d_rows, width, d_bits)], (d_rows, width), d_bits, w_down)
    one.hop(order, 0, 1, 0)
    vec_far = order.then(vec_far)
    far_bias = [(vec_far, a) for a in bias_at]
    qkv, ctx, lse = attend(order, lengths, flat, own_w, own_bias, count, pairs, range(1, pairs), own)
    up_one = prepare(prepare_piece, [piece(quarter, half, y_bits)], (quarter, half), y_bits, w_up)
    one.hop(order, 1)
    one.hop(order, 2, 0)
    one.hop(order, 3)
    w_one = one.place(order, me, [(width, 3 * PAIR)], put_rows)
    two.hop(order, 0, 1, 0)
    far = attend(order, lengths, flat, w_one, far_bias, count, pairs, (0,))
    up_two = prepare(prepare_piece, [piece(quarter, half, y_bits, 1)], (quarter, half), y_bits, w_up)
    two.hop(order, 1)
    down.hop(order, 0, 1, 2, 0)
    down.hop(order, 1)
    two.hop(order, 2, 0)
    up_one.hop(order, 0, 1, 0)
    two.hop(order, 3)
    w_two, wo_far = two.place(order, me, [(width, 3 * PAIR * (pairs - 1)), (local, width)], put_with_output)
    down.hop(order, 2, 2, 0)
    up_one.hop(order, 1)
    far = attend(order, lengths, flat, (w_two,), far_bias, count, pairs, range(1, pairs), far)
    qkv_far, ctx_far, lse_far = far
    up_two.hop(order, 0, 1, 0)
    down.hop(order, 3)
    down.hop(order, 4, 0)
    low, normed, act, slope, part, inverse = forward_own(
        order, ctx, ctx_far, flat, w_output, wo_far, w_up, w_down, vec, spots
    )
    up_one.hop(order, 2, 0)
    up_two.hop(order, 1)
    down.hop(order, 6, 0)
    down.hop(order, 5)
    up_one.hop(order, 3)
    wu_one = up_one.place(order, me, [(width, half)], put_rows)
    down.hop(order, 7)
    (wd_far,) = down.place(order, me, [(hidden, width)], put_rows)
    up_two.hop(order, 2, 0)
    up_two.hop(order, 3)
    wu_far = (*wu_one, *up_two.place(order, me, [(width, half)], put_rows))

    bits = [1 << i for i in range(n.bit_length() - 1)]
    y_first = tuple(bits)
    z_first = (bits[0], bits[2], bits[1]) + tuple(bits[3:])
    block = WIDE if hidden % WIDE == 0 else hidden
    down_split, up_split = Split(width, hidden, block, n, y_first), Split(width, hidden, block, n, z_first)
    group_splits = [Split(width, 6 * PAIR, 3 * PAIR, n, bits_of) for bits_of in (y_first, z_first)]
    send, keep, d_ffn, layer_out, slope_far, sums_two = forward_far(
        order, low, wu_far, wd_far, part, normed, vec, vec_far, tangent, act, spots, down_split
    )
    down_sum = down_split.scatter(me, send, keep, order)
    send, keep, d_part, sums_up = backward_own(order, d_ffn, slope, w_up, w_down, low, up_split)
    up_sum = up_split.scatter(me, send, keep, order)

    class Vectors:
        def __init__(self, parts):
            self.value, self.arriving = line_up_sums(order, parts), []

        def send(self, *over):
            masks = [sum(b for j, b in enumerate(over) if (m >> j) & 1) for m in range(1, 1 << len(over))]
            self.arriving = [swap_dp(self.value, mask, n) for mask in masks]

        def add(self):
            self.value = add_all(order, self.value, *[order.then(v) for v in self.arriving])

    early = Vectors([(sums_two, 0), (sums_up, 0)])
    early.send(bits[0])
    wide = 3 * PAIR
    st = {}

    def far_back(which):
        st.setdefault("far", []).append(attend_back(order, lengths, qkv_far, lse_far, d_ctx_far, count, which))

    def own_back(which):
        st.setdefault("own", []).append(attend_back(order, lengths, qkv, lse, d_ctx, count, which))

    for step in PLAN:
        if step == "B2":
            d_attn, d_ctx, d_ctx_far, sums_one = backward_far(
                order, d_ffn, slope_far, wu_far, wd_far, d_part, normed, inverse, w_output, wo_far, vec, spots
            )
        elif step == "OA":
            own_back(range(pairs))
        elif step == "O0":
            own_back((0,))
        elif step == "O1":
            own_back(range(1, pairs))
        elif step == "FA":
            far_back(range(pairs))
        elif step == "F0":
            far_back((0,))
        elif step == "F1":
            far_back(range(1, pairs))
        elif step == "G1":
            parts = [(d_attn, ctx, 0, local), (flat, st["own"][0], 0, wide)]
            send, keep, sums_a = weight_grad(order, parts, group_splits[0])
            group_one = group_splits[0].scatter(me, send, keep, order)
        elif step == "G2":
            own = (flat, st["own"][0], wide, wide * (pairs - 1)) if len(st["own"]) == 1 else (flat, st["own"][1], 0, wide * (pairs - 1))
            send, keep, sums_b = weight_grad(order, [own], group_splits[1])
            group_two = group_splits[1].scatter(me, send, keep, order)
        elif step == "IG":
            grad_inputs = inputs_grad(order, d_attn, [*st["own"], *st["far"]], own_w, (*w_one, w_two))
        elif step == "L":
            late = Vectors([(sums_one, 0), (sums_a, local), (sums_b, 0)])
            late.send(bits[0])
        elif step == "L1":
            late.add()
            late.value = line_up_sums(order, [(late.value, 0), (early.value, 0)])
            left = [bits[i : i + 2] for i in range(1, len(bits), 2)]
            late.send(*left[0])
        elif step == "L2":
            late.add()
            left = left[1:]
            late.send(*left[0])
        elif step == "L3":
            late.add()
        elif step == "E":
            early.add()
        else:
            names_of = {"D": down_sum, "U": up_sum}
            if "A" in step or "B" in step:
                names_of["A"] = group_one
            if "B" in step:
                names_of["B"] = group_two
            advance(order, *[names_of[k] for k in step])
    for s in (down_sum, up_sum, group_one, group_two):
        while s.step < len(bits):
            advance(order, s)
    for over in left[1:]:
        late.send(*over)
        late.add()
    rows = width // n
    small = finish_vectors(late.value, me, n, width, local, hidden)
    by_columns_of = group_one.result, group_two.result
    if rows % 8 == 0:
        g_query, g_key, g_value, g_output = finish_heads(*by_columns_of, local)
    else:
        g_output = group_one.result[:, :local].T
        heads_of = jnp.concatenate([group_one.result[:, local:], group_two.result], axis=1)
        g_query, g_key, g_value = [heads_of.reshape(rows, pairs, 3, PAIR)[:, :, j].reshape(rows, local) for j in range(3)]
    b_output_g, gain_one_g, shift_one_g, b_down_g, gain_two_g, shift_two_g, b_query_g, b_value_g, b_up_g = small
    return (
        layer_out.reshape(count, length, width),
        grad_inputs.reshape(count, length, width),
        g_query,
        b_query_g,
        g_key,
        g_value,
        b_value_g,
        g_output,
        b_output_g,
        gain_one_g,
        shift_one_g,
        up_sum.result,
        b_up_g,
        down_sum.result.T,
        b_down_g,
        gain_two_g,
        shift_two_g,
    )


def solution(mesh):
    in_specs = (
        P("dp", None, None),
        P("dp"),
        P(None, "tensor"),
        P("tensor"),
        P(None, "tensor"),
        P(None, "tensor"),
        P("tensor"),
        P("tensor", None),
        P(),
        P(),
        P(),
        P(None, "tensor"),
        P("tensor"),
        P("tensor", None),
        P(),
        P(),
        P(),
        P("dp", None, None),
    )
    out_specs = (
        P("dp", None, None),
        P("dp", None, None),
        P("dp", "tensor"),
        P("tensor"),
        P("dp", "tensor"),
        P("dp", "tensor"),
        P("tensor"),
        P("tensor", "dp"),
        P("dp"),
        P("dp"),
        P("dp"),
        P("dp", "tensor"),
        P("tensor"),
        P("tensor", "dp"),
        P("dp"),
        P("dp"),
        P("dp"),
    )
    return jax.shard_map(
        functools.partial(per_device, n=mesh.shape["dp"]),
        mesh=mesh,
        in_specs=in_specs,
        out_specs=out_specs,
        check_vma=False,
    )
```

```python
import functools
import math

import jax
import jax.numpy as jnp
from jax import lax
from jax.experimental import pallas as pl
from jax.experimental.pallas import tpu as pltpu
from jax.sharding import PartitionSpec as P

DH = 64
PAIR = 2 * DH
PLAN = ('D', 'U', 'E', 'B2', 'O0', 'G1', 'D', 'U', 'A', 'O1', 'G2', 'D', 'U', 'B', 'L', 'FA', 'A', 'B', 'L1', 'IG', 'D', 'U', 'A', 'B', 'L2', 'A', 'B', 'L3')
ROWS = 512
WIDE = 512
GRANT = 60 * 1024 * 1024
FLYING = 6 * 1024 * 1024
LONG = pl.CostEstimate(flops=10**13, bytes_accessed=10**6, transcendentals=0)

norm_eps = 1e-12
masked_score = -1000000000.0
BF = jnp.bfloat16
F32 = jnp.float32
SMEM = pl.BlockSpec(memory_space=pltpu.SMEM)
VMEM = pl.BlockSpec(memory_space=pltpu.VMEM)
ANY = pl.BlockSpec(memory_space=pl.ANY)


def shape(dims, kind):
    return jax.ShapeDtypeStruct(tuple(dims), kind)


def against(left, right):
    return lax.dot_general(left, right, (((1,), (1,)), ((), ())), preferred_element_type=F32)


def over_rows(left, right):
    return lax.dot_general(left, right, (((0,), (0,)), ((), ())), preferred_element_type=F32)


def plain(left, right):
    return jnp.dot(left, right, preferred_element_type=F32)


def tie(value, *before):
    return pl.pallas_call(
        lambda *refs: None,
        in_specs=[ANY] * (1 + len(before)),
        out_specs=ANY,
        out_shape=shape(value.shape, value.dtype),
        input_output_aliases={0: 0},
        compiler_params=pltpu.CompilerParams(vmem_limit_bytes=GRANT),
        cost_estimate=LONG,
    )(value, *before)


def pause(*before):
    return pl.pallas_call(
        lambda *refs: None,
        in_specs=[ANY] * len(before),
        out_specs=ANY,
        out_shape=shape((8, PAIR), F32),
        cost_estimate=LONG,
    )(*before)


class Order:
    def __init__(self, me):
        self.me, self.last = me, ()

    def then(self, value):
        self.last = (pause(*self.last),)
        value = tie(value, *self.last)
        self.last = (value,)
        return value

    def now(self, *values):
        self.last = tuple(values)


def call(body, order, args, outs, in_specs, out_specs, grid, scratch=(), alias=None):
    count, after = len(args), order.last

    def run(*refs):
        body(*refs[:count], *refs[count + len(after) :])

    result = pl.pallas_call(
        run,
        grid=grid,
        in_specs=list(in_specs) + [ANY] * len(after),
        out_specs=list(out_specs),
        out_shape=outs,
        scratch_shapes=list(scratch),
        input_output_aliases=alias or {},
        compiler_params=pltpu.CompilerParams(vmem_limit_bytes=GRANT),
        cost_estimate=LONG,
    )(*args, *after)
    order.now(result[0])
    return result


def everything(array):
    return [(slice(None),) * len(array.shape)]


def by_rows(array):
    return [(slice(i, i + ROWS), slice(None)) for i in range(0, array.shape[0], ROWS)]


def by_columns(array, width):
    return [(slice(None), slice(i, i + width)) for i in range(0, array.shape[1], width)]


class Stream:
    def __init__(self, ins, in_parts, out_parts, far, near, sems, queue, always):
        self.always = always
        self.in_far, self.out_far = far[:ins], far[ins:]
        self.ins, self.outs = near[:ins], near[ins:]
        self.in_parts, self.out_parts = in_parts, out_parts
        self.in_sems, self.out_sems = sems[:ins], sems[ins:]
        self.queue, self.started, self.waited, self.flying, self.sent = queue, 0, set(), 0, []
        self.top_up()

    def fetch(self, k, c):
        at = self.in_parts[k][c]
        return pltpu.make_async_copy(self.in_far[k].at[at], self.ins[k].at[at], self.in_sems[k].at[c])

    def size(self, k, c):
        return math.prod(self.ins[k].at[self.in_parts[k][c]].shape) * self.ins[k].dtype.itemsize

    def start_next(self):
        k, c = self.queue[self.started]
        self.fetch(k, c).start()
        self.flying += self.size(k, c)
        self.started += 1

    def top_up(self):
        while self.started < len(self.queue) and self.flying < FLYING:
            self.start_next()

    def need(self, k, c=0):
        if (k, c) not in self.waited:
            self.waited.add((k, c))
            while (k, c) not in self.queue[: self.started]:
                self.start_next()
            self.fetch(k, c).wait()
            self.flying -= self.size(k, c)
            self.top_up()
        return self.ins[k]

    def step(self, needs, emits, work):
        for k, c in needs:
            self.need(k, c)
        pl.when(self.always)(work)
        for k, c in emits:
            self.emit(k, c)

    def emit(self, k, c=0):
        at = self.out_parts[k][c]
        copy = pltpu.make_async_copy(self.outs[k].at[at], self.out_far[k].at[at], self.out_sems[k].at[c])
        copy.start()
        self.sent.append(copy)


def stream(body, order, ins, outs, scratch=()):
    smem = (order.me,)
    arrays = [i[0] for i in ins]
    in_parts, out_parts = [i[1] for i in ins], [o[1] for o in outs]
    after, n_in, n_out = order.last, len(ins), len(outs)
    queue = [(c, k) for k, p in enumerate(in_parts) for c in range(len(p))]
    queue = [(k, c) for late, c, k in sorted((len(ins[k]) > 2, c, k) for c, k in queue)]

    def run(*refs):
        small, refs = refs[: len(smem)], refs[len(smem) :]
        far_in, refs = refs[:n_in], refs[n_in + len(after) :]
        far_out, refs = refs[:n_out], refs[n_out:]
        near, refs = refs[: n_in + n_out], refs[n_in + n_out :]
        sems, rest = refs[: n_in + n_out], refs[n_in + n_out :]
        io = Stream(n_in, in_parts, out_parts, far_in + far_out, near, sems, queue, small[0][0] >= 0)
        body(io, small[0][0], *rest)
        for k, c in queue:
            io.need(k, c)
        for copy in io.sent:
            copy.wait()

    result = pl.pallas_call(
        run,
        in_specs=[SMEM] * len(smem) + [ANY] * (n_in + len(after)),
        out_specs=[ANY] * n_out,
        out_shape=[o[0] for o in outs],
        scratch_shapes=[pltpu.VMEM(a.shape, a.dtype) for a in arrays]
        + [pltpu.VMEM(o[0].shape, o[0].dtype) for o in outs]
        + [pltpu.SemaphoreType.DMA((len(p),)) for p in in_parts + out_parts]
        + list(scratch),
        compiler_params=pltpu.CompilerParams(vmem_limit_bytes=GRANT),
        cost_estimate=LONG,
    )(*smem, *arrays, *after)
    order.now(result[0])
    return result


def whole(*dims):
    return pl.BlockSpec(dims, lambda *i: (0,) * len(dims))


def row_blocks(tokens):
    return [slice(i, i + ROWS) for i in range(0, tokens, ROWS)]


def swap_x(value):
    return lax.ppermute(value, "tensor", [(0, 1), (1, 0)])


def swap_dp(value, bit, n):
    return lax.ppermute(value, "dp", [(i, i ^ bit) for i in range(n)])


def index_of(me, bits):
    total = 0
    for j, bit in enumerate(bits):
        total = total + jnp.where(jnp.bitwise_and(me, bit) != 0, 1 << j, 0)
    return total


class Gather:
    def __init__(self, mine, bits, n):
        self.bits, self.n = bits, n
        self.pieces = {0: swap_x(mine)}

    def hop(self, order, slot, *steps):
        self.pieces[slot] = order.then(self.pieces[slot])
        for j in steps:
            self.pieces[slot | (1 << j)] = swap_dp(self.pieces[slot], self.bits[j], self.n)

    def place(self, order, me, outs, cut):
        slots = list(self.pieces)
        count, after = len(slots), order.last
        dims = self.pieces[0].shape
        many = len(cut(0))

        def body(me_ref, *refs):
            far, refs = refs[:count], refs[count + len(after) :]
            out, (wide, low, in_sem, out_sem) = refs[: len(outs)], refs[len(outs) :]
            always = me_ref[0] >= 0
            base = index_of(me_ref[0], self.bits)
            ins = [pltpu.make_async_copy(far[k], wide.at[k], in_sem.at[k]) for k in range(count)]
            for copy in ins:
                copy.start()
            sent = []
            for k, slot in enumerate(slots):
                ins[k].wait()

                @pl.when(always)
                def _():
                    low[k] = wide[k].astype(BF)

                for j, (inner, which, outer) in enumerate(cut(jnp.bitwise_xor(base, slot))):
                    sent.append(pltpu.make_async_copy(low.at[(k, *inner)], out[which].at[outer], out_sem.at[k, j]))
                    sent[-1].start()
            for copy in sent:
                copy.wait()

        result = pl.pallas_call(
            body,
            in_specs=[SMEM] + [ANY] * (count + len(after)),
            out_specs=[ANY] * len(outs),
            out_shape=[shape(o, BF) for o in outs],
            scratch_shapes=[
                pltpu.VMEM((count, *dims), F32),
                pltpu.VMEM((count, *dims), BF),
                pltpu.SemaphoreType.DMA((count,)),
                pltpu.SemaphoreType.DMA((count, many)),
            ],
            compiler_params=pltpu.CompilerParams(vmem_limit_bytes=GRANT),
            cost_estimate=LONG,
        )(me, *[self.pieces[s] for s in slots], *after)
        order.now(result[0])
        return result


def rows_at(place, rows):
    return pl.ds(pl.multiple_of(place * rows, rows), rows)


def in_rows(rows):
    everything = slice(None)
    return lambda place: [((everything, everything), 0, (rows_at(place, rows), everything))]


class Split:
    def __init__(self, rows, width, block, n, order_of_bits):
        self.rows, self.width, self.block, self.n, self.bits = rows, width, block, n, order_of_bits
        steps = len(order_of_bits)
        self.chunks = [
            sum(bit for j, bit in enumerate(order_of_bits) if (r >> (steps - 1 - j)) & 1) for r in range(n)
        ]
        self.inside = (rows // n) % 8 == 0
        half = shape((rows // 2, width), F32)
        self.outs = [(half, by_columns(half, block))] * 2
        self.scratch = pltpu.VMEM((rows, block), F32)

    def write(self, io, first, me, full, done, left, right):
        send, keep = io.outs[first : first + 2]
        small, half = self.rows // self.n, self.rows // 2
        lanes = slice(done * self.block, (done + 1) * self.block)
        full[...] = over_rows(left, right)
        for r, chunk in enumerate(self.chunks):
            out, low = (keep, r * small) if r < self.n // 2 else (send, r * small - half)
            at = jnp.bitwise_xor(me, chunk) * small if self.inside else r * small
            at = pl.multiple_of(at, small) if self.inside else at
            out[low : low + small, lanes] = full[pl.ds(at, small), :]

    def scatter(self, me, send, keep, order):
        if not self.inside:
            wanted = jnp.bitwise_xor(me[0], jnp.array(self.chunks, jnp.int32))
            full = jnp.concatenate([keep, send], axis=0).reshape(self.n, -1, self.width)[wanted]
            full = full.reshape(self.rows, self.width)
            keep, send = full[: self.rows // 2], full[self.rows // 2 :]
        order.now(send)
        return Scatter(send, keep, self.n, self.bits)


def add_rows(order, sums):
    ins, outs, places = [], [], []
    for parts, low, high in sums:
        width = parts[0].shape[1]
        lanes = [slice(i, i + width // 2) for i in (0, width // 2)]
        out = shape((high - low, width), F32)
        places.append((len(ins), len(parts), low, high, lanes))
        ins += [(p, [(slice(low, high), lane) for lane in lanes]) for p in parts]
        outs.append((out, [(slice(None), lane) for lane in lanes]))

    def body(io, me):
        for c in range(2):
            for k, (first, count, low, high, lanes) in enumerate(places):

                def work():
                    total = io.ins[first][low:high, lanes[c]]
                    for j in range(1, count):
                        total = total + io.ins[first + j][low:high, lanes[c]]
                    io.outs[k][:, lanes[c]] = total

                io.step([(first + j, c) for j in range(count)], [(k, c)], work)

    return stream(body, order, ins, outs)


def advance(order, *scatters):
    sums = []
    for s in scatters:
        s.step += 1
        s.parts[-1] = order.then(s.parts[-1])
        size = s.parts[-1].shape[0]
        sums.append((s.parts, *((0, size) if s.step == len(s.bits) else (size // 2, size))))
    if all((high - low) % 8 == 0 for _, low, high in sums):
        totals = add_rows(order, sums)
    else:
        totals = [sum(p[low:high] for p in parts[1:]) + parts[0][low:high] for parts, low, high in sums]
        order.now(*totals)
    for s, total in zip(scatters, totals):
        if s.step == len(s.bits):
            s.result = total
        else:
            s.parts.append(swap_dp(total, s.bits[s.step], s.n))


class Scatter:
    def __init__(self, send, keep, n, order_of_bits):
        self.n, self.bits, self.step = n, order_of_bits, 0
        self.parts = [keep, swap_dp(send, self.bits[0], n)]


def by_length(real, length, work):
    quarter = length // 4
    for k in range(1, 5):
        fits = real <= quarter if k == 1 else (real > quarter * (k - 1)) & (real <= quarter * k)
        pl.when(real > quarter * 3 if k == 4 else fits)(functools.partial(work, quarter * k))


def attend_body(real, x, w, bias, qkv_ref, ctx_ref, lse_ref):
    length = x.shape[0]
    qkv_ref[...] = (plain(x, w) + bias).astype(BF)
    lane = lax.broadcasted_iota(jnp.int32, (1, PAIR), 1)

    def work(count):
        valid = lax.broadcasted_iota(jnp.int32, (count, 1), 0) < real
        query = qkv_ref[:, 0:PAIR] * BF(0.125)
        keys = qkv_ref[:count, PAIR : 2 * PAIR]
        values_t = qkv_ref[:count, 2 * PAIR : 3 * PAIR].T
        outs, logs = [], []
        for h in range(2):
            mine = (lane < DH) if h == 0 else (lane >= DH)
            q = jnp.where(mine, query, BF(0))
            s = against(keys, q)
            s = jnp.where(valid, s, masked_score)
            top = jnp.max(s, axis=0, keepdims=True)
            e = jnp.exp(s - top)
            total = jnp.sum(e, axis=0, keepdims=True)
            p = (e * (1.0 / total)).astype(BF)
            outs.append(plain(values_t[h * DH : (h + 1) * DH, :], p))
            logs.append(top + jnp.log(total))
        ctx_ref[...] = jnp.concatenate(outs, axis=0).T.astype(BF)
        lse_ref[0, 0] = jnp.concatenate(logs, axis=0)

    by_length(real, length, work)


def attend(order, lengths, flat, weights, biases, count, pairs, which, kept=()):
    tokens, width = flat.shape
    length = tokens // count
    own = len(weights) == 3
    first, steps = which[0], len(which)
    if own:
        w_specs = [pl.BlockSpec((width, PAIR), lambda p, s: (0, first + p))] * 3
    else:
        w_specs = [pl.BlockSpec((width, 3 * PAIR), lambda p, s: (0, p))]
    b_specs = [pl.BlockSpec((1, PAIR), lambda p, s, at=at: (0, at // PAIR + first + p)) for _, at in biases]
    many = len(weights)

    def body(len_ref, x_ref, *refs):
        ws, bs, outs = refs[:many], refs[many : many + 2], refs[many + 2 + len(kept) :]
        w = jnp.concatenate([r[...] for r in ws], axis=1) if own else ws[0][...]
        bias = jnp.concatenate([bs[0][...], jnp.zeros((1, PAIR), F32), bs[1][...]], axis=1)
        attend_body(len_ref[pl.program_id(1)], x_ref[...], w, bias, *outs)

    return call(
        body,
        order,
        (lengths, flat, *weights, *[b for b, _ in biases], *kept),
        [
            shape((tokens, 3 * PAIR * pairs), BF),
            shape((tokens, PAIR * pairs), BF),
            shape((count, pairs, 2, length), F32),
        ],
        [SMEM, pl.BlockSpec((length, width), lambda p, s: (s, 0))] + w_specs + b_specs + [ANY] * len(kept),
        [
            pl.BlockSpec((length, 3 * PAIR), lambda p, s: (s, first + p)),
            pl.BlockSpec((length, PAIR), lambda p, s: (s, first + p)),
            pl.BlockSpec((1, 1, 2, length), lambda p, s: (s, first + p, 0, 0)),
        ],
        (steps, count),
        alias={4 + many + j: j for j in range(len(kept))})


def attend_back_body(len_ref, x_ref, lse_ref, dc_ref, out_ref):
    length = x_ref.shape[0]
    real = len_ref[pl.program_id(1)]
    lane = lax.broadcasted_iota(jnp.int32, (1, PAIR), 1)

    def work(count):
        valid = lax.broadcasted_iota(jnp.int32, (count, 1), 0) < real
        query = x_ref[:, 0:PAIR] * BF(0.125)
        keys = x_ref[:count, PAIR : 2 * PAIR]
        keys_t = keys.T
        values = x_ref[:count, 2 * PAIR : 3 * PAIR]
        d_ctx = dc_ref[...]
        dq, dk, dv = [], [], []
        for h in range(2):
            mine = (lane < DH) if h == 0 else (lane >= DH)
            q = jnp.where(mine, query, BF(0))
            s = against(keys, q)
            s = jnp.where(valid, s, masked_score)
            p = jnp.exp(s - lse_ref[0, 0, h : h + 1, :])
            dv.append(plain(p.astype(BF), d_ctx))
            dp = against(values, jnp.where(mine, d_ctx, BF(0)))
            row = jnp.sum(p * dp, axis=0, keepdims=True)
            ds = (p * (dp - row)).astype(BF)
            dk.append(plain(ds, query))
            dq.append(plain(keys_t[h * DH : (h + 1) * DH, :], ds))
        first = lane < DH
        out_ref[:, 0:PAIR] = (jnp.concatenate(dq, axis=0) * 0.125).T.astype(BF)
        out_ref[:count, PAIR : 2 * PAIR] = jnp.where(first, dk[0], dk[1]).astype(BF)
        out_ref[:count, 2 * PAIR : 3 * PAIR] = jnp.where(first, dv[0], dv[1]).astype(BF)
        if count < length:
            out_ref[count:, PAIR : 3 * PAIR] = jnp.zeros((length - count, 2 * PAIR), BF)

    by_length(real, length, work)


def attend_back(order, lengths, qkv, lse, d_ctx, count, which):
    tokens = qkv.shape[0]
    length = tokens // count
    first, steps = which[0], len(which)
    return call(
        attend_back_body,
        order,
        (lengths, qkv, lse, d_ctx),
        [shape((tokens, 3 * PAIR * steps), BF)],
        [
            SMEM,
            pl.BlockSpec((length, 3 * PAIR), lambda p, s: (s, first + p)),
            pl.BlockSpec((1, 1, 2, length), lambda p, s: (s, first + p, 0, 0)),
            pl.BlockSpec((length, PAIR), lambda p, s: (s, first + p)),
        ],
        [pl.BlockSpec((length, 3 * PAIR), lambda p, s: (s, p))],
        (steps, count))[0]


def gelu_both(value):
    phi_big = 0.5 + 0.5 * lax.erf(value * math.sqrt(0.5))
    phi_small = jnp.exp(-0.5 * value * value) * (1.0 / math.sqrt(2.0 * math.pi))
    return (value * phi_big).astype(BF), (phi_big + value * phi_small).astype(BF)


def normalize(values):
    center = values - jnp.mean(values, axis=-1, keepdims=True)
    spread = jnp.mean(center * center, axis=-1, keepdims=True)
    inverse = lax.rsqrt(spread + norm_eps)
    return center * inverse, inverse


def norm_backward(grad, normed, inverse, gain):
    scaled = grad * gain
    mean_one = jnp.mean(scaled, axis=-1, keepdims=True)
    mean_two = jnp.mean(scaled * normed, axis=-1, keepdims=True)
    return inverse * (scaled - mean_one - normed * mean_two)


def column_sum(values):
    return jnp.sum(values, axis=0, keepdims=True)


def add_to(ref, first, values):
    ref[...] = values if first else ref[...] + values


def forward_own(order, ctx, ctx_far, flat, w_output, wo_far, w_up, w_down, vec, spots):
    tokens, width = flat.shape
    hidden = w_up.shape[1]
    outs = [shape((tokens, w), BF) for w in (width, width, hidden, hidden, width)] + [shape((tokens, 1), F32)]

    def body(io, me):
        own, far, x, wo, wof, v, wu, wd = io.ins
        low_o, normed_o, act_o, slope_o, part_o, rstd_o = io.outs
        for c, r in enumerate(row_blocks(tokens)):

            def norm():
                attn = plain(own[r, :], wo[...]) + plain(far[r, :], wof[...])
                residual = x[r, :].astype(F32) + attn + spots(v, "b_output")
                normed, inverse = normalize(residual)
                normed_o[r, :] = normed.astype(BF)
                rstd_o[r, :] = inverse
                low_o[r, :] = (normed * spots(v, "gain_one") + spots(v, "shift_one")).astype(BF)

            def up():
                act, slope = gelu_both(plain(low_o[r, :], wu[...]) + spots(v, "b_up"))
                act_o[r, :] = act
                slope_o[r, :] = slope

            def down():
                part_o[r, :] = plain(act_o[r, :], wd[...]).astype(BF)

            io.step([(0, c), (1, c), (2, c), (3, 0), (4, 0), (5, 0)], [(0, c), (1, c), (5, c)], norm)
            io.step([(6, 0)], [(2, c), (3, c)], up)
            io.step([(7, 0)], [(4, c)], down)

    ins = [(a, by_rows(a)) for a in (ctx, ctx_far, flat)]
    ins += [(a, everything(a)) for a in (w_output, wo_far, vec, w_up, w_down)]
    return stream(body, order, ins, [(o, by_rows(o)) for o in outs])


def forward_far(order, low, wu_parts, wd_far, part, normed, vec, vec_far, cotangent, act_own, spots, split):
    tokens, width = low.shape
    wide, hidden = wu_parts[0].shape[1], wd_far.shape[0]
    outs = [shape((tokens, w), BF) for w in (width, width, hidden)]
    sums = shape((3, width), F32)

    def body(io, me, full, acts):
        low_r, wu_one, wu_two, vf, wd, v, part_r, normed_r, tan_r, act_r = io.ins
        dffn_o, out_o, slope_o, sums_o = io.outs[2:]
        for c, r in enumerate(row_blocks(tokens)):

            def up():
                bias = spots(vf, "b_up")
                for j, wu in enumerate((wu_one, wu_two)):
                    lanes = slice(j * wide, (j + 1) * wide)
                    acts[:, lanes], slope_o[r, lanes] = gelu_both(plain(low_r[r, :], wu[...]) + bias[:, lanes])

            def down():
                ffn = part_r[r, :].astype(F32) + plain(acts[...], wd[...]) + spots(v, "b_down")
                first = normed_r[r, :].astype(F32) * spots(v, "gain_one") + spots(v, "shift_one")
                normed_two, inverse = normalize(first + ffn)
                gain = spots(v, "gain_two")
                out_o[r, :] = (normed_two * gain + spots(v, "shift_two")).astype(BF)
                tangent = tan_r[r, :].astype(F32)
                d_second = norm_backward(tangent, normed_two, inverse, gain)
                dffn_o[r, :] = d_second.astype(BF)
                more = [column_sum(d_second), column_sum(tangent * normed_two), column_sum(tangent)]
                add_to(sums_o, c == 0, jnp.concatenate(more, axis=0))

            io.step([(0, c), (1, 0), (2, 0), (3, 0)], [(4, c)], up)
            io.step([(4, 0), (5, 0), (6, c), (7, c), (8, c)], [(2, c), (3, c)], down)
        io.emit(5)
        for j in range(split.width // split.block):
            lanes = slice(j * split.block, (j + 1) * split.block)
            work = functools.partial(lambda j, lanes: split.write(io, 0, me, full, j, dffn_o[...], act_r[:, lanes]), j, lanes)
            io.step([(9, j)], [(0, j), (1, j)], work)

    ins = [(low, by_rows(low))] + [(a, everything(a)) for a in (*wu_parts, vec_far, wd_far, vec)]
    ins += [(a, by_rows(a)) for a in (part, normed, cotangent)] + [(act_own, by_columns(act_own, split.block), True)]
    outs = split.outs + [(o, by_rows(o)) for o in outs] + [(sums, everything(sums))]
    return stream(body, order, ins, outs, [split.scratch, pltpu.VMEM((ROWS, hidden), BF)])


def backward_own(order, d_ffn, slope, w_up, w_down, low, split):
    tokens, width = d_ffn.shape
    hidden = w_up.shape[1]

    def body(io, me, full, d_pres):
        d, wd, slope_r, wu, low_r = io.ins
        part_o, sums_o = io.outs[2:]
        for c, r in enumerate(row_blocks(tokens)):

            def pre():
                d_pre = (against(d[r, :], wd[...]) * slope_r[r, :].astype(F32)).astype(BF)
                d_pres[r, :] = d_pre
                add_to(sums_o, c == 0, column_sum(d_pre.astype(F32)))

            def first():
                part_o[r, :] = against(d_pres[r, :], wu[...]).astype(BF)

            io.step([(0, c), (1, 0), (2, c)], [], pre)
            io.step([(3, 0)], [(2, c)], first)
        io.emit(3)
        for j in range(split.width // split.block):
            lanes = slice(j * split.block, (j + 1) * split.block)
            work = functools.partial(lambda j, lanes: split.write(io, 0, me, full, j, low_r[...], d_pres[:, lanes]), j, lanes)
            io.step([(4, 0)], [(0, j), (1, j)], work)

    ins = [(d_ffn, by_rows(d_ffn)), (w_down, everything(w_down)), (slope, by_rows(slope))]
    ins += [(w_up, everything(w_up)), (low, everything(low), True)]
    part, sums = shape((tokens, width), BF), shape((1, hidden), F32)
    outs = split.outs + [(part, by_rows(part)), (sums, everything(sums))]
    return stream(body, order, ins, outs, [split.scratch, pltpu.VMEM((tokens, hidden), BF)])


def backward_far(order, d_ffn, slope, wu_parts, wd_far, part, normed, inverse, w_output, wo_far, vec, spots):
    tokens, width = d_ffn.shape
    local, wide, hidden = w_output.shape[0], wu_parts[0].shape[1], wd_far.shape[0]

    def body(io, me, d_pres):
        d, wd, slope_r, wu_one, wu_two, part_r, norm, inv, wo, wof, v = io.ins
        dattn_o, dctx_o, dfar_o, sums_o = io.outs
        for c, r in enumerate(row_blocks(tokens)):

            def pre():
                d_pres[...] = (against(d[r, :], wd[...]) * slope_r[r, :].astype(F32)).astype(BF)

            def first():
                d_first = d[r, :].astype(F32) + part_r[r, :].astype(F32)
                for j, wu in enumerate((wu_one, wu_two)):
                    d_first = d_first + against(d_pres[:, j * wide : (j + 1) * wide], wu[...])
                normed_one = norm[r, :].astype(F32)
                d_res = norm_backward(d_first, normed_one, inv[r, :], spots(v, "gain_one"))
                dattn_o[r, :] = d_res.astype(BF)
                more = [column_sum(d_res), column_sum(d_first * normed_one), column_sum(d_first)]
                add_to(sums_o, c == 0, jnp.concatenate(more, axis=0))

            def heads():
                dctx_o[r, :] = against(dattn_o[r, :], wo[...]).astype(BF)
                dfar_o[r, :] = against(dattn_o[r, :], wof[...]).astype(BF)

            io.step([(0, c), (1, 0), (2, c)], [], pre)
            io.step([(3, 0), (4, 0), (5, c), (6, c), (7, c), (10, 0)], [(0, c)], first)
            io.step([(8, 0), (9, 0)], [(1, c), (2, c)], heads)
        io.emit(3)

    ins = [(d_ffn, by_rows(d_ffn)), (wd_far, everything(wd_far)), (slope, by_rows(slope))]
    ins += [(a, everything(a)) for a in wu_parts]
    ins += [(a, by_rows(a)) for a in (part, normed, inverse)]
    ins += [(a, everything(a)) for a in (w_output, wo_far, vec)]
    outs = [shape((tokens, w), BF) for w in (width, local, local)]
    sums = shape((3, width), F32)
    outs = [(o, by_rows(o)) for o in outs] + [(sums, everything(sums))]
    return stream(body, order, ins, outs, [pltpu.VMEM((ROWS, hidden), BF)])


def weight_grad(order, pairs, split):
    ins, sums = [], shape((1, split.width), F32)
    for left, right, start, width in pairs:
        lanes = [(slice(None), slice(i, i + split.block)) for i in range(start, start + width, split.block)]
        ins += [(left, everything(left)), (right, lanes)]

    def body(io, me, full):
        done = 0
        for p, (_, _, start, width) in enumerate(pairs):
            for c in range(width // split.block):

                def work(p, c, done, start):
                    at = start + c * split.block
                    block = io.ins[2 * p + 1][:, at : at + split.block]
                    lanes = slice(done * split.block, (done + 1) * split.block)
                    io.outs[2][:, lanes] = column_sum(block.astype(F32))
                    split.write(io, 0, me, full, done, io.ins[2 * p][...], block)

                work = functools.partial(work, p, c, done, start)
                io.step([(2 * p, 0), (2 * p + 1, c)], [(0, done), (1, done)], work)
                done += 1
        io.emit(2)

    outs = split.outs + [(sums, everything(sums))]
    return stream(body, order, ins, outs, [split.scratch])


def small_call(body, order, args, out):
    return pl.pallas_call(
        lambda *refs: body(*refs[: len(args)], refs[-1]),
        in_specs=[VMEM] * len(args) + [ANY] * len(order.last),
        out_specs=VMEM,
        out_shape=out,
        compiler_params=pltpu.CompilerParams(vmem_limit_bytes=GRANT),
        cost_estimate=LONG,
    )(*args, *order.last)


def line_up_sums(order, parts):
    total = sum(v.shape[0] * (v.shape[1] - first) for v, first in parts)

    def body(*refs):
        at = 0
        for ref, (v, first) in zip(refs, parts):
            for row in range(v.shape[0]):
                size = v.shape[1] - first
                refs[-1][:, at : at + size] = ref[row : row + 1, first:]
                at += size

    result = small_call(body, order, [v for v, _ in parts], shape((1, total), F32))
    order.now(result)
    return result


def add_all(order, *values):
    def body(*refs):
        refs[-1][...] = sum(r[...] for r in refs[1:-1]) + refs[0][...]

    result = small_call(body, order, values, shape(values[0].shape, F32))
    order.now(result)
    return result


def finish_vectors(line, me, n, width, local, hidden):
    rows, heads_at = width // n, 3 * width
    late = heads_at + 3 * local
    starts = [0, width, 2 * width, late, late + width, late + 2 * width]

    def body(me_ref, line_ref, *outs):
        shift = jnp.where(me_ref[0] == 0, 0, width - me_ref[0] * rows)
        for start, out in zip(starts, outs):
            turned = pltpu.roll(jnp.broadcast_to(line_ref[:, start : start + width], (8, width)), shift, 1)
            out[...] = turned[0:1, :rows].reshape(rows)
        for j, out in ((0, outs[6]), (2, outs[7])):
            for p in range(local // PAIR):
                at = heads_at + (3 * p + j) * PAIR
                out[p * PAIR : (p + 1) * PAIR] = line_ref[:, at : at + PAIR].reshape(PAIR)
        outs[8][...] = line_ref[:, late + heads_at : late + heads_at + hidden].reshape(hidden)

    sizes = [rows] * 6 + [local] * 2 + [hidden]
    return pl.pallas_call(
        body,
        in_specs=[SMEM, VMEM],
        out_specs=[VMEM] * 9,
        out_shape=[shape((size,), F32) for size in sizes],
    )(me, line)


def finish_heads(one, two, local):
    rows = one.shape[0]

    def body(one_ref, two_ref, q, k, v, out):
        for j, ref in enumerate((q, k, v)):
            ref[:, :PAIR] = one_ref[:, local + j * PAIR : local + (j + 1) * PAIR]
            for p in range(1, local // PAIR):
                at = (3 * (p - 1) + j) * PAIR
                ref[:, p * PAIR : (p + 1) * PAIR] = two_ref[:, at : at + PAIR]
        out[...] = one_ref[:, :local].T

    return pl.pallas_call(
        body,
        in_specs=[VMEM, VMEM],
        out_specs=[VMEM] * 4,
        out_shape=[shape((rows, local), F32)] * 3 + [shape((local, rows), F32)],
    )(one, two)


def inputs_grad(order, d_res, grads, w_own, w_far):
    tokens, width = d_res.shape
    pairs = w_own[0].shape[1] // PAIR
    wide = 6 * PAIR * pairs
    after, many, blocks = order.last, len(grads), tokens // ROWS

    def body(me_ref, *refs):
        always = me_ref[0] >= 0
        res_far, gs, (wq, wk, wv) = refs[0], refs[1 : 1 + many], refs[1 + many : 4 + many]
        wfs = refs[4 + many : 4 + many + len(w_far)]
        out_far, res, g_all, w_all, out, w_sem, g_sem, res_sem, out_sem = refs[4 + many + len(w_far) + len(after) :]
        w_copies, g_copies = [], []
        for p in range(pairs):
            for j, w in enumerate((wq, wk, wv)):
                at = (3 * p + j) * PAIR
                src, dst = w.at[:, p * PAIR : (p + 1) * PAIR], w_all.at[:, at : at + PAIR]
                w_copies.append(pltpu.make_async_copy(src, dst, w_sem.at[3 * p + j]))
        at = wide // 2
        for k, w in enumerate(wfs):
            size = w.shape[1]
            w_copies.append(pltpu.make_async_copy(w, w_all.at[:, at : at + size], w_sem.at[3 * pairs + k]))
            at += size
        for c, r in enumerate(row_blocks(tokens)):
            at, copies = 0, []
            for k, g in enumerate(gs):
                size = g.shape[1]
                copies.append(pltpu.make_async_copy(g.at[r, :], g_all.at[r, at : at + size], g_sem.at[c, k]))
                at += size
            copies.append(pltpu.make_async_copy(res_far.at[r, :], res.at[r, :], res_sem.at[c]))
            g_copies.append(copies)
        for copy in w_copies + [x for copies in g_copies for x in copies]:
            copy.start()
        for copy in w_copies:
            copy.wait()
        sent = []
        for c, r in enumerate(row_blocks(tokens)):
            for copy in g_copies[c]:
                copy.wait()

            @pl.when(always)
            def _():
                out[r, :] = (res[r, :].astype(F32) + against(g_all[r, :], w_all[...])).astype(BF)

            sent.append(pltpu.make_async_copy(out.at[r, :], out_far.at[r, :], out_sem.at[c]))
            sent[-1].start()
        for copy in sent:
            copy.wait()

    result = pl.pallas_call(
        body,
        in_specs=[SMEM] + [ANY] * (4 + many + len(w_far) + len(after)),
        out_specs=ANY,
        out_shape=shape((tokens, width), BF),
        scratch_shapes=[
            pltpu.VMEM((tokens, width), BF),
            pltpu.VMEM((tokens, wide), BF),
            pltpu.VMEM((width, wide), BF),
            pltpu.VMEM((tokens, width), BF),
            pltpu.SemaphoreType.DMA((3 * pairs + len(w_far),)),
            pltpu.SemaphoreType.DMA((blocks, many)),
            pltpu.SemaphoreType.DMA((blocks,)),
            pltpu.SemaphoreType.DMA((blocks,)),
        ],
        compiler_params=pltpu.CompilerParams(vmem_limit_bytes=GRANT),
        cost_estimate=LONG,
    )(order.me, d_res, *grads, *w_own, *w_far, *after)
    order.now(result)
    return result


def per_device(
    inputs,
    lengths,
    w_query,
    b_query,
    w_key,
    w_value,
    b_value,
    w_output,
    b_output,
    gain_one,
    shift_one,
    w_up,
    b_up,
    w_down,
    b_down,
    gain_two,
    shift_two,
    cotangent,
    *,
    n,
):
    count, length, width = inputs.shape
    local, hidden = w_query.shape[1], w_up.shape[1]
    pairs = local // PAIR
    tokens = count * length
    flat = inputs.reshape(tokens, width)
    tangent = cotangent.reshape(tokens, width)
    me = lax.axis_index("dp").astype(jnp.int32).reshape(1)
    names = ("b_up", "b_query", "b_value", "b_output", "gain_one", "shift_one", "b_down", "gain_two", "shift_two")
    given = (b_up, b_query, b_value, b_output, gain_one, shift_one, b_down, gain_two, shift_two)
    offsets, at = {}, 0
    for name, v in zip(names, given):
        offsets[name] = (at, v.shape[0])
        at += v.shape[0]

    def line_up(*refs):
        for name, ref in zip(names, refs):
            start, size = offsets[name]
            refs[-1][:, start : start + size] = ref[...].astype(F32).reshape(1, size)

    vec = pl.pallas_call(
        line_up,
        in_specs=[VMEM] * len(given),
        out_specs=VMEM,
        out_shape=shape((1, at), F32),
    )(*given)

    def spots(ref, name):
        start, size = offsets[name]
        return ref[:, start : start + size]

    y_bits, z_bits = (1, 2), (1, 4)
    quarter, half, few = width // 4, hidden // 2, local // 4

    def heads(w3, p, out, at):
        for j, w in enumerate(w3):
            out[:, at + j * PAIR : at + (j + 1) * PAIR] = w[:, p * PAIR : (p + 1) * PAIR].astype(F32)

    def prepare_one(me_ref, wq, wk, wv, one):
        heads((wq, wk, wv), 0, one, 0)

    def prepare_two(me_ref, wq, wk, wv, before, two):
        for p in range(1, pairs):
            heads((wq, wk, wv), p, two, 3 * PAIR * (p - 1))

    def prepare_pieces(me_ref, w_one, w_two, before, out_one, out_two):
        out_one[...] = w_one[...].astype(F32)
        out_two[...] = w_two[...].astype(F32)

    def prepare_piece(me_ref, w, before, out):
        out[...] = w[...].astype(F32)

    def piece(rows, cols, which, col=0):
        return pl.BlockSpec((rows, cols), lambda i, m: (index_of(m[0], which), col))

    def pieces_of(body, in_specs, sizes, *args):
        return pl.pallas_call(
            body,
            grid_spec=pltpu.PrefetchScalarGridSpec(
                num_scalar_prefetch=1,
                grid=(1,),
                in_specs=in_specs,
                out_specs=[pl.BlockSpec(size, lambda i, m: (0, 0)) for size in sizes],
            ),
            out_shape=[shape(size, F32) for size in sizes],
            compiler_params=pltpu.CompilerParams(vmem_limit_bytes=GRANT),
            cost_estimate=LONG,
        )(me, *args)

    d_bits, d_rows = (1, 2, 4), hidden // 8
    own_w = (w_query, w_key, w_value)
    order = Order(me)

    def prepare(body, in_specs, groups, *args):
        made = pieces_of(body, in_specs + [ANY] * len(order.last), [size for size, _ in groups], *args, *order.last)
        order.now(made[0])
        return [Gather(send, which, n) for send, (_, which) in zip(made, groups)]

    rest = 3 * PAIR * (pairs - 1)
    (one,) = prepare(prepare_one, [piece(quarter, PAIR, y_bits)] * 3, [((quarter, 3 * PAIR), y_bits)], *own_w)
    (two,) = prepare(prepare_two, [piece(quarter, local, z_bits)] * 3, [((quarter, rest), z_bits)], *own_w)
    vec_far = swap_x(vec)
    bias_at = [offsets["b_query"][0], offsets["b_value"][0]]
    own_bias = [(vec, a) for a in bias_at]
    own = attend(order, lengths, flat, own_w, own_bias, count, pairs, (0,))
    out, down = prepare(
        prepare_pieces,
        [piece(few, width, y_bits), piece(d_rows, width, d_bits)],
        [((few, width), y_bits), ((d_rows, width), d_bits)],
        w_output,
        w_down,
    )
    one.hop(order, 0, 1, 0)
    vec_far = order.then(vec_far)
    far_bias = [(vec_far, a) for a in bias_at]
    qkv, ctx, lse = attend(order, lengths, flat, own_w, own_bias, count, pairs, range(1, pairs), own)
    (up_one,) = prepare(prepare_piece, [piece(quarter, half, y_bits)], [((quarter, half), y_bits)], w_up)
    one.hop(order, 1)
    two.hop(order, 0, 1, 0)
    one.hop(order, 2, 0)
    one.hop(order, 3)
    w_one = one.place(order, me, [(width, 3 * PAIR)], in_rows(quarter))
    two.hop(order, 1)
    far = attend(order, lengths, flat, w_one, far_bias, count, pairs, (0,))
    (up_two,) = prepare(prepare_piece, [piece(quarter, half, y_bits, 1)], [((quarter, half), y_bits)], w_up)
    out.hop(order, 0, 1, 0)
    two.hop(order, 2, 0)
    down.hop(order, 0, 1, 2, 0)
    two.hop(order, 3)
    w_two = two.place(order, me, [(width, rest)], in_rows(quarter))
    out.hop(order, 1)
    out.hop(order, 2, 0)
    down.hop(order, 1)
    far = attend(order, lengths, flat, w_two, far_bias, count, pairs, range(1, pairs), far)
    qkv_far, ctx_far, lse_far = far
    up_one.hop(order, 0, 1, 0)
    down.hop(order, 2, 2, 0)
    out.hop(order, 3)
    (wo_far,) = out.place(order, me, [(local, width)], in_rows(few))
    down.hop(order, 3)
    down.hop(order, 4, 0)
    up_two.hop(order, 0, 1, 0)
    low, normed, act, slope, part, inverse = forward_own(
        order, ctx, ctx_far, flat, w_output, wo_far, w_up, w_down, vec, spots
    )
    up_one.hop(order, 1)
    up_one.hop(order, 2, 0)
    down.hop(order, 5)
    down.hop(order, 6, 0)
    up_one.hop(order, 3)
    wu_one = up_one.place(order, me, [(width, half)], in_rows(quarter))
    down.hop(order, 7)
    (wd_far,) = down.place(order, me, [(hidden, width)], in_rows(d_rows))
    up_two.hop(order, 1)
    up_two.hop(order, 2, 0)
    up_two.hop(order, 3)
    wu_far = (*wu_one, *up_two.place(order, me, [(width, half)], in_rows(quarter)))

    bits = [1 << i for i in range(n.bit_length() - 1)]
    y_first = tuple(bits)
    z_first = (bits[0], bits[2], bits[1]) + tuple(bits[3:])
    block = WIDE if hidden % WIDE == 0 else hidden
    down_split, up_split = Split(width, hidden, block, n, y_first), Split(width, hidden, block, n, z_first)
    group_splits = [Split(width, 6 * PAIR, 3 * PAIR, n, bits_of) for bits_of in (y_first, y_first)]
    send, keep, d_ffn, layer_out, slope_far, sums_two = forward_far(
        order, low, wu_far, wd_far, part, normed, vec, vec_far, tangent, act, spots, down_split
    )
    down_sum = down_split.scatter(me, send, keep, order)
    send, keep, d_part, sums_up = backward_own(order, d_ffn, slope, w_up, w_down, low, up_split)
    up_sum = up_split.scatter(me, send, keep, order)

    class Vectors:
        def __init__(self, parts):
            self.value, self.arriving = line_up_sums(order, parts), []

        def send(self, *over):
            masks = [sum(b for j, b in enumerate(over) if (m >> j) & 1) for m in range(1, 1 << len(over))]
            self.arriving = [swap_dp(self.value, mask, n) for mask in masks]

        def add(self):
            self.value = add_all(order, self.value, *[order.then(v) for v in self.arriving])

    early = Vectors([(sums_two, 0), (sums_up, 0)])
    early.send(bits[0])
    wide = 3 * PAIR
    st = {}

    def far_back(which):
        st.setdefault("far", []).append(attend_back(order, lengths, qkv_far, lse_far, d_ctx_far, count, which))

    def own_back(which):
        st.setdefault("own", []).append(attend_back(order, lengths, qkv, lse, d_ctx, count, which))

    for step in PLAN:
        if step == "B2":
            d_attn, d_ctx, d_ctx_far, sums_one = backward_far(
                order, d_ffn, slope_far, wu_far, wd_far, d_part, normed, inverse, w_output, wo_far, vec, spots
            )
        elif step == "OA":
            own_back(range(pairs))
        elif step == "O0":
            own_back((0,))
        elif step == "O1":
            own_back(range(1, pairs))
        elif step == "FA":
            far_back(range(pairs))
        elif step == "F0":
            far_back((0,))
        elif step == "F1":
            far_back(range(1, pairs))
        elif step == "G1":
            parts = [(d_attn, ctx, 0, local), (flat, st["own"][0], 0, wide)]
            send, keep, sums_a = weight_grad(order, parts, group_splits[0])
            group_one = group_splits[0].scatter(me, send, keep, order)
        elif step == "G2":
            own = (flat, st["own"][0], wide, wide * (pairs - 1)) if len(st["own"]) == 1 else (flat, st["own"][1], 0, wide * (pairs - 1))
            send, keep, sums_b = weight_grad(order, [own], group_splits[1])
            group_two = group_splits[1].scatter(me, send, keep, order)
        elif step == "IG":
            grad_inputs = inputs_grad(order, d_attn, [*st["own"], *st["far"]], own_w, (*w_one, *w_two))
        elif step == "L":
            late = Vectors([(sums_one, 0), (sums_a, local), (sums_b, 0)])
            late.send(bits[0])
        elif step == "L1":
            late.add()
            late.value = line_up_sums(order, [(late.value, 0), (early.value, 0)])
            left = [bits[i : i + 2] for i in range(1, len(bits), 2)]
            late.send(*left[0])
        elif step == "L2":
            late.add()
            left = left[1:]
            late.send(*left[0])
        elif step == "L3":
            late.add()
        elif step == "E":
            early.add()
        else:
            names_of = {"D": down_sum, "U": up_sum}
            if "A" in step or "B" in step:
                names_of["A"] = group_one
            if "B" in step:
                names_of["B"] = group_two
            advance(order, *[names_of[k] for k in step])
    for s in (down_sum, up_sum, group_one, group_two):
        while s.step < len(bits):
            advance(order, s)
    for over in left[1:]:
        late.send(*over)
        late.add()
    rows = width // n
    small = finish_vectors(late.value, me, n, width, local, hidden)
    by_columns_of = group_one.result, group_two.result
    if rows % 8 == 0:
        g_query, g_key, g_value, g_output = finish_heads(*by_columns_of, local)
    else:
        g_output = group_one.result[:, :local].T
        heads_of = jnp.concatenate([group_one.result[:, local:], group_two.result], axis=1)
        g_query, g_key, g_value = [heads_of.reshape(rows, pairs, 3, PAIR)[:, :, j].reshape(rows, local) for j in range(3)]
    b_output_g, gain_one_g, shift_one_g, b_down_g, gain_two_g, shift_two_g, b_query_g, b_value_g, b_up_g = small
    return (
        layer_out.reshape(count, length, width),
        grad_inputs.reshape(count, length, width),
        g_query,
        b_query_g,
        g_key,
        g_value,
        b_value_g,
        g_output,
        b_output_g,
        gain_one_g,
        shift_one_g,
        up_sum.result,
        b_up_g,
        down_sum.result.T,
        b_down_g,
        gain_two_g,
        shift_two_g,
    )


def solution(mesh):
    in_specs = (
        P("dp", None, None),
        P("dp"),
        P(None, "tensor"),
        P("tensor"),
        P(None, "tensor"),
        P(None, "tensor"),
        P("tensor"),
        P("tensor", None),
        P(),
        P(),
        P(),
        P(None, "tensor"),
        P("tensor"),
        P("tensor", None),
        P(),
        P(),
        P(),
        P("dp", None, None),
    )
    out_specs = (
        P("dp", None, None),
        P("dp", None, None),
        P("dp", "tensor"),
        P("tensor"),
        P("dp", "tensor"),
        P("dp", "tensor"),
        P("tensor"),
        P("tensor", "dp"),
        P("dp"),
        P("dp"),
        P("dp"),
        P("dp", "tensor"),
        P("tensor"),
        P("tensor", "dp"),
        P("dp"),
        P("dp"),
        P("dp"),
    )
    return jax.shard_map(
        functools.partial(per_device, n=mesh.shape["dp"]),
        mesh=mesh,
        in_specs=in_specs,
        out_specs=out_specs,
        check_vma=False,
    )
```

```python
import functools
import math

import jax
import jax.numpy as jnp
from jax import lax
from jax.experimental import pallas as pl
from jax.experimental.pallas import tpu as pltpu
from jax.sharding import PartitionSpec as P

DH = 64
PAIR = 2 * DH
PLAN = ('D', 'U', 'E', 'B2', 'O0', 'G1', 'D', 'U', 'A', 'O1', 'G2', 'D', 'U', 'B', 'L', 'FA', 'A', 'B', 'L1', 'IG', 'D', 'U', 'A', 'B', 'A', 'L2', 'B', 'L3')
ROWS = 512
WIDE = 512
GRANT = 60 * 1024 * 1024
FLYING = 6 * 1024 * 1024
LONG = pl.CostEstimate(flops=10**13, bytes_accessed=10**6, transcendentals=0)

norm_eps = 1e-12
masked_score = -1000000000.0
BF = jnp.bfloat16
F32 = jnp.float32
SMEM = pl.BlockSpec(memory_space=pltpu.SMEM)
VMEM = pl.BlockSpec(memory_space=pltpu.VMEM)
ANY = pl.BlockSpec(memory_space=pl.ANY)


def shape(dims, kind):
    return jax.ShapeDtypeStruct(tuple(dims), kind)


def against(left, right):
    return lax.dot_general(left, right, (((1,), (1,)), ((), ())), preferred_element_type=F32)


def over_rows(left, right):
    return lax.dot_general(left, right, (((0,), (0,)), ((), ())), preferred_element_type=F32)


def plain(left, right):
    return jnp.dot(left, right, preferred_element_type=F32)


def tie(value, *before):
    return pl.pallas_call(
        lambda *refs: None,
        in_specs=[ANY] * (1 + len(before)),
        out_specs=ANY,
        out_shape=shape(value.shape, value.dtype),
        input_output_aliases={0: 0},
        compiler_params=pltpu.CompilerParams(vmem_limit_bytes=GRANT),
        cost_estimate=LONG,
    )(value, *before)


def pause(*before):
    return pl.pallas_call(
        lambda *refs: None,
        in_specs=[ANY] * len(before),
        out_specs=ANY,
        out_shape=shape((8, PAIR), F32),
        cost_estimate=LONG,
    )(*before)


class Order:
    def __init__(self, me):
        self.me, self.last = me, ()

    def then(self, value):
        self.last = (pause(*self.last),)
        value = tie(value, *self.last)
        self.last = (value,)
        return value

    def now(self, *values):
        self.last = tuple(values)


def call(body, order, args, outs, in_specs, out_specs, grid, scratch=(), alias=None):
    count, after = len(args), order.last

    def run(*refs):
        body(*refs[:count], *refs[count + len(after) :])

    result = pl.pallas_call(
        run,
        grid=grid,
        in_specs=list(in_specs) + [ANY] * len(after),
        out_specs=list(out_specs),
        out_shape=outs,
        scratch_shapes=list(scratch),
        input_output_aliases=alias or {},
        compiler_params=pltpu.CompilerParams(vmem_limit_bytes=GRANT),
        cost_estimate=LONG,
    )(*args, *after)
    order.now(result[0])
    return result


def everything(array):
    return [(slice(None),) * len(array.shape)]


def by_rows(array):
    return [(slice(i, i + ROWS), slice(None)) for i in range(0, array.shape[0], ROWS)]


def by_columns(array, width):
    return [(slice(None), slice(i, i + width)) for i in range(0, array.shape[1], width)]


class Stream:
    def __init__(self, ins, in_parts, out_parts, far, near, sems, queue, always):
        self.always = always
        self.in_far, self.out_far = far[:ins], far[ins:]
        self.ins, self.outs = near[:ins], near[ins:]
        self.in_parts, self.out_parts = in_parts, out_parts
        self.in_sems, self.out_sems = sems[:ins], sems[ins:]
        self.queue, self.started, self.waited, self.flying, self.sent = queue, 0, set(), 0, []
        self.top_up()

    def fetch(self, k, c):
        at = self.in_parts[k][c]
        return pltpu.make_async_copy(self.in_far[k].at[at], self.ins[k].at[at], self.in_sems[k].at[c])

    def size(self, k, c):
        return math.prod(self.ins[k].at[self.in_parts[k][c]].shape) * self.ins[k].dtype.itemsize

    def start_next(self):
        k, c = self.queue[self.started]
        self.fetch(k, c).start()
        self.flying += self.size(k, c)
        self.started += 1

    def top_up(self):
        while self.started < len(self.queue) and self.flying < FLYING:
            self.start_next()

    def need(self, k, c=0):
        if (k, c) not in self.waited:
            self.waited.add((k, c))
            while (k, c) not in self.queue[: self.started]:
                self.start_next()
            self.fetch(k, c).wait()
            self.flying -= self.size(k, c)
            self.top_up()
        return self.ins[k]

    def step(self, needs, emits, work):
        for k, c in needs:
            self.need(k, c)
        pl.when(self.always)(work)
        for k, c in emits:
            self.emit(k, c)

    def emit(self, k, c=0):
        at = self.out_parts[k][c]
        copy = pltpu.make_async_copy(self.outs[k].at[at], self.out_far[k].at[at], self.out_sems[k].at[c])
        copy.start()
        self.sent.append(copy)


def stream(body, order, ins, outs, scratch=()):
    smem = (order.me,)
    arrays = [i[0] for i in ins]
    in_parts, out_parts = [i[1] for i in ins], [o[1] for o in outs]
    after, n_in, n_out = order.last, len(ins), len(outs)
    queue = [(c, k) for k, p in enumerate(in_parts) for c in range(len(p))]
    queue = [(k, c) for late, c, k in sorted((len(ins[k]) > 2, c, k) for c, k in queue)]

    def run(*refs):
        small, refs = refs[: len(smem)], refs[len(smem) :]
        far_in, refs = refs[:n_in], refs[n_in + len(after) :]
        far_out, refs = refs[:n_out], refs[n_out:]
        near, refs = refs[: n_in + n_out], refs[n_in + n_out :]
        sems, rest = refs[: n_in + n_out], refs[n_in + n_out :]
        io = Stream(n_in, in_parts, out_parts, far_in + far_out, near, sems, queue, small[0][0] >= 0)
        body(io, small[0][0], *rest)
        for k, c in queue:
            io.need(k, c)
        for copy in io.sent:
            copy.wait()

    result = pl.pallas_call(
        run,
        in_specs=[SMEM] * len(smem) + [ANY] * (n_in + len(after)),
        out_specs=[ANY] * n_out,
        out_shape=[o[0] for o in outs],
        scratch_shapes=[pltpu.VMEM(a.shape, a.dtype) for a in arrays]
        + [pltpu.VMEM(o[0].shape, o[0].dtype) for o in outs]
        + [pltpu.SemaphoreType.DMA((len(p),)) for p in in_parts + out_parts]
        + list(scratch),
        compiler_params=pltpu.CompilerParams(vmem_limit_bytes=GRANT),
        cost_estimate=LONG,
    )(*smem, *arrays, *after)
    order.now(result[0])
    return result


def whole(*dims):
    return pl.BlockSpec(dims, lambda *i: (0,) * len(dims))


def row_blocks(tokens):
    return [slice(i, i + ROWS) for i in range(0, tokens, ROWS)]


def swap_x(value):
    return lax.ppermute(value, "tensor", [(0, 1), (1, 0)])


def swap_dp(value, bit, n):
    return lax.ppermute(value, "dp", [(i, i ^ bit) for i in range(n)])


def index_of(me, bits):
    total = 0
    for j, bit in enumerate(bits):
        total = total + jnp.where(jnp.bitwise_and(me, bit) != 0, 1 << j, 0)
    return total


class Gather:
    def __init__(self, mine, bits, n):
        self.bits, self.n = bits, n
        self.pieces = {0: swap_x(mine)}

    def hop(self, order, slot, *steps):
        self.pieces[slot] = order.then(self.pieces[slot])
        for j in steps:
            self.pieces[slot | (1 << j)] = swap_dp(self.pieces[slot], self.bits[j], self.n)

    def place(self, order, me, outs, cut):
        slots = list(self.pieces)
        count, after = len(slots), order.last
        dims = self.pieces[0].shape
        many = len(cut(0))

        def body(me_ref, *refs):
            far, refs = refs[:count], refs[count + len(after) :]
            out, (wide, low, in_sem, out_sem) = refs[: len(outs)], refs[len(outs) :]
            always = me_ref[0] >= 0
            base = index_of(me_ref[0], self.bits)
            ins = [pltpu.make_async_copy(far[k], wide.at[k], in_sem.at[k]) for k in range(count)]
            for copy in ins:
                copy.start()
            sent = []
            for k, slot in enumerate(slots):
                ins[k].wait()

                @pl.when(always)
                def _():
                    low[k] = wide[k].astype(BF)

                for j, (inner, which, outer) in enumerate(cut(jnp.bitwise_xor(base, slot))):
                    sent.append(pltpu.make_async_copy(low.at[(k, *inner)], out[which].at[outer], out_sem.at[k, j]))
                    sent[-1].start()
            for copy in sent:
                copy.wait()

        result = pl.pallas_call(
            body,
            in_specs=[SMEM] + [ANY] * (count + len(after)),
            out_specs=[ANY] * len(outs),
            out_shape=[shape(o, BF) for o in outs],
            scratch_shapes=[
                pltpu.VMEM((count, *dims), F32),
                pltpu.VMEM((count, *dims), BF),
                pltpu.SemaphoreType.DMA((count,)),
                pltpu.SemaphoreType.DMA((count, many)),
            ],
            compiler_params=pltpu.CompilerParams(vmem_limit_bytes=GRANT),
            cost_estimate=LONG,
        )(me, *[self.pieces[s] for s in slots], *after)
        order.now(result[0])
        return result


def rows_at(place, rows):
    return pl.ds(pl.multiple_of(place * rows, rows), rows)


def in_rows(rows):
    everything = slice(None)
    return lambda place: [((everything, everything), 0, (rows_at(place, rows), everything))]


class Split:
    def __init__(self, rows, width, block, n, order_of_bits):
        self.rows, self.width, self.block, self.n, self.bits = rows, width, block, n, order_of_bits
        steps = len(order_of_bits)
        self.chunks = [
            sum(bit for j, bit in enumerate(order_of_bits) if (r >> (steps - 1 - j)) & 1) for r in range(n)
        ]
        self.inside = (rows // n) % 8 == 0
        half = shape((rows // 2, width), F32)
        self.outs = [(half, by_columns(half, block))] * 2
        self.scratch = pltpu.VMEM((rows, block), F32)

    def write(self, io, first, me, full, done, left, right):
        send, keep = io.outs[first : first + 2]
        small, half = self.rows // self.n, self.rows // 2
        lanes = slice(done * self.block, (done + 1) * self.block)
        full[...] = over_rows(left, right)
        for r, chunk in enumerate(self.chunks):
            out, low = (keep, r * small) if r < self.n // 2 else (send, r * small - half)
            at = jnp.bitwise_xor(me, chunk) * small if self.inside else r * small
            at = pl.multiple_of(at, small) if self.inside else at
            out[low : low + small, lanes] = full[pl.ds(at, small), :]

    def scatter(self, me, send, keep, order):
        if not self.inside:
            wanted = jnp.bitwise_xor(me[0], jnp.array(self.chunks, jnp.int32))
            full = jnp.concatenate([keep, send], axis=0).reshape(self.n, -1, self.width)[wanted]
            full = full.reshape(self.rows, self.width)
            keep, send = full[: self.rows // 2], full[self.rows // 2 :]
        order.now(send)
        return Scatter(send, keep, self.n, self.bits)


def add_rows(order, sums):
    ins, outs, places = [], [], []
    for parts, low, high in sums:
        width = parts[0].shape[1]
        lanes = [slice(i, i + width // 2) for i in (0, width // 2)]
        out = shape((high - low, width), F32)
        places.append((len(ins), len(parts), low, high, lanes))
        ins += [(p, [(slice(low, high), lane) for lane in lanes]) for p in parts]
        outs.append((out, [(slice(None), lane) for lane in lanes]))

    def body(io, me):
        for c in range(2):
            for k, (first, count, low, high, lanes) in enumerate(places):

                def work():
                    total = io.ins[first][low:high, lanes[c]]
                    for j in range(1, count):
                        total = total + io.ins[first + j][low:high, lanes[c]]
                    io.outs[k][:, lanes[c]] = total

                io.step([(first + j, c) for j in range(count)], [(k, c)], work)

    return stream(body, order, ins, outs)


def advance(order, *scatters):
    sums = []
    for s in scatters:
        s.step += 1
        s.parts[-1] = order.then(s.parts[-1])
        size = s.parts[-1].shape[0]
        sums.append((s.parts, *((0, size) if s.step == len(s.bits) else (size // 2, size))))
    if all((high - low) % 8 == 0 for _, low, high in sums):
        totals = add_rows(order, sums)
    else:
        totals = [sum(p[low:high] for p in parts[1:]) + parts[0][low:high] for parts, low, high in sums]
        order.now(*totals)
    for s, total in zip(scatters, totals):
        if s.step == len(s.bits):
            s.result = total
        else:
            s.parts.append(swap_dp(total, s.bits[s.step], s.n))


class Scatter:
    def __init__(self, send, keep, n, order_of_bits):
        self.n, self.bits, self.step = n, order_of_bits, 0
        self.parts = [keep, swap_dp(send, self.bits[0], n)]


def by_length(real, length, work):
    quarter = length // 4
    for k in range(1, 5):
        fits = real <= quarter if k == 1 else (real > quarter * (k - 1)) & (real <= quarter * k)
        pl.when(real > quarter * 3 if k == 4 else fits)(functools.partial(work, quarter * k))


def attend_body(real, x, w, bias, qkv_ref, ctx_ref, lse_ref):
    length = x.shape[0]
    qkv_ref[...] = (plain(x, w) + bias).astype(BF)
    lane = lax.broadcasted_iota(jnp.int32, (1, PAIR), 1)

    def work(count):
        valid = lax.broadcasted_iota(jnp.int32, (count, 1), 0) < real
        query = qkv_ref[:, 0:PAIR] * BF(0.125)
        keys = qkv_ref[:count, PAIR : 2 * PAIR]
        values_t = qkv_ref[:count, 2 * PAIR : 3 * PAIR].T
        outs, logs = [], []
        for h in range(2):
            mine = (lane < DH) if h == 0 else (lane >= DH)
            q = jnp.where(mine, query, BF(0))
            s = against(keys, q)
            s = jnp.where(valid, s, masked_score)
            top = jnp.max(s, axis=0, keepdims=True)
            e = jnp.exp(s - top)
            total = jnp.sum(e, axis=0, keepdims=True)
            p = (e * (1.0 / total)).astype(BF)
            outs.append(plain(values_t[h * DH : (h + 1) * DH, :], p))
            logs.append(top + jnp.log(total))
        ctx_ref[...] = jnp.concatenate(outs, axis=0).T.astype(BF)
        lse_ref[0, 0] = jnp.concatenate(logs, axis=0)

    by_length(real, length, work)


def attend(order, lengths, flat, weights, biases, count, pairs, which, kept=()):
    tokens, width = flat.shape
    length = tokens // count
    own = len(weights) == 3
    first, steps = which[0], len(which)
    if own:
        w_specs = [pl.BlockSpec((width, PAIR), lambda p, s: (0, first + p))] * 3
    else:
        w_specs = [pl.BlockSpec((width, 3 * PAIR), lambda p, s: (0, p))]
    b_specs = [pl.BlockSpec((1, PAIR), lambda p, s, at=at: (0, at // PAIR + first + p)) for _, at in biases]
    many = len(weights)

    def body(len_ref, x_ref, *refs):
        ws, bs, outs = refs[:many], refs[many : many + 2], refs[many + 2 + len(kept) :]
        w = jnp.concatenate([r[...] for r in ws], axis=1) if own else ws[0][...]
        bias = jnp.concatenate([bs[0][...], jnp.zeros((1, PAIR), F32), bs[1][...]], axis=1)
        attend_body(len_ref[pl.program_id(1)], x_ref[...], w, bias, *outs)

    return call(
        body,
        order,
        (lengths, flat, *weights, *[b for b, _ in biases], *kept),
        [
            shape((tokens, 3 * PAIR * pairs), BF),
            shape((tokens, PAIR * pairs), BF),
            shape((count, pairs, 2, length), F32),
        ],
        [SMEM, pl.BlockSpec((length, width), lambda p, s: (s, 0))] + w_specs + b_specs + [ANY] * len(kept),
        [
            pl.BlockSpec((length, 3 * PAIR), lambda p, s: (s, first + p)),
            pl.BlockSpec((length, PAIR), lambda p, s: (s, first + p)),
            pl.BlockSpec((1, 1, 2, length), lambda p, s: (s, first + p, 0, 0)),
        ],
        (steps, count),
        alias={4 + many + j: j for j in range(len(kept))})


def attend_back_body(len_ref, x_ref, lse_ref, dc_ref, out_ref):
    length = x_ref.shape[0]
    real = len_ref[pl.program_id(1)]
    lane = lax.broadcasted_iota(jnp.int32, (1, PAIR), 1)

    def work(count):
        valid = lax.broadcasted_iota(jnp.int32, (count, 1), 0) < real
        query = x_ref[:, 0:PAIR] * BF(0.125)
        keys = x_ref[:count, PAIR : 2 * PAIR]
        keys_t = keys.T
        values = x_ref[:count, 2 * PAIR : 3 * PAIR]
        d_ctx = dc_ref[...]
        dq, dk, dv = [], [], []
        for h in range(2):
            mine = (lane < DH) if h == 0 else (lane >= DH)
            q = jnp.where(mine, query, BF(0))
            s = against(keys, q)
            s = jnp.where(valid, s, masked_score)
            p = jnp.exp(s - lse_ref[0, 0, h : h + 1, :])
            dv.append(plain(p.astype(BF), d_ctx))
            dp = against(values, jnp.where(mine, d_ctx, BF(0)))
            row = jnp.sum(p * dp, axis=0, keepdims=True)
            ds = (p * (dp - row)).astype(BF)
            dk.append(plain(ds, query))
            dq.append(plain(keys_t[h * DH : (h + 1) * DH, :], ds))
        first = lane < DH
        out_ref[:, 0:PAIR] = (jnp.concatenate(dq, axis=0) * 0.125).T.astype(BF)
        out_ref[:count, PAIR : 2 * PAIR] = jnp.where(first, dk[0], dk[1]).astype(BF)
        out_ref[:count, 2 * PAIR : 3 * PAIR] = jnp.where(first, dv[0], dv[1]).astype(BF)
        if count < length:
            out_ref[count:, PAIR : 3 * PAIR] = jnp.zeros((length - count, 2 * PAIR), BF)

    by_length(real, length, work)


def attend_back(order, lengths, qkv, lse, d_ctx, count, which):
    tokens = qkv.shape[0]
    length = tokens // count
    first, steps = which[0], len(which)
    return call(
        attend_back_body,
        order,
        (lengths, qkv, lse, d_ctx),
        [shape((tokens, 3 * PAIR * steps), BF)],
        [
            SMEM,
            pl.BlockSpec((length, 3 * PAIR), lambda p, s: (s, first + p)),
            pl.BlockSpec((1, 1, 2, length), lambda p, s: (s, first + p, 0, 0)),
            pl.BlockSpec((length, PAIR), lambda p, s: (s, first + p)),
        ],
        [pl.BlockSpec((length, 3 * PAIR), lambda p, s: (s, p))],
        (steps, count))[0]


def gelu_both(value):
    phi_big = 0.5 + 0.5 * lax.erf(value * math.sqrt(0.5))
    phi_small = jnp.exp(-0.5 * value * value) * (1.0 / math.sqrt(2.0 * math.pi))
    return (value * phi_big).astype(BF), (phi_big + value * phi_small).astype(BF)


def normalize(values):
    center = values - jnp.mean(values, axis=-1, keepdims=True)
    spread = jnp.mean(center * center, axis=-1, keepdims=True)
    inverse = lax.rsqrt(spread + norm_eps)
    return center * inverse, inverse


def norm_backward(grad, normed, inverse, gain):
    scaled = grad * gain
    mean_one = jnp.mean(scaled, axis=-1, keepdims=True)
    mean_two = jnp.mean(scaled * normed, axis=-1, keepdims=True)
    return inverse * (scaled - mean_one - normed * mean_two)


def column_sum(values):
    return jnp.sum(values, axis=0, keepdims=True)


def add_to(ref, first, values):
    ref[...] = values if first else ref[...] + values


def forward_own(order, ctx, ctx_far, flat, w_output, wo_far, w_up, w_down, vec, spots):
    tokens, width = flat.shape
    hidden = w_up.shape[1]
    outs = [shape((tokens, w), BF) for w in (width, width, hidden, hidden, width)] + [shape((tokens, 1), F32)]

    def body(io, me):
        own, far, x, wo, wof, v, wu, wd = io.ins
        low_o, normed_o, act_o, slope_o, part_o, rstd_o = io.outs
        for c, r in enumerate(row_blocks(tokens)):

            def norm():
                attn = plain(own[r, :], wo[...]) + plain(far[r, :], wof[...])
                residual = x[r, :].astype(F32) + attn + spots(v, "b_output")
                normed, inverse = normalize(residual)
                normed_o[r, :] = normed.astype(BF)
                rstd_o[r, :] = inverse
                low_o[r, :] = (normed * spots(v, "gain_one") + spots(v, "shift_one")).astype(BF)

            def up():
                act, slope = gelu_both(plain(low_o[r, :], wu[...]) + spots(v, "b_up"))
                act_o[r, :] = act
                slope_o[r, :] = slope

            def down():
                part_o[r, :] = plain(act_o[r, :], wd[...]).astype(BF)

            io.step([(0, c), (1, c), (2, c), (3, 0), (4, 0), (5, 0)], [(0, c), (1, c), (5, c)], norm)
            io.step([(6, 0)], [(2, c), (3, c)], up)
            io.step([(7, 0)], [(4, c)], down)

    ins = [(a, by_rows(a)) for a in (ctx, ctx_far, flat)]
    ins += [(a, everything(a)) for a in (w_output, wo_far, vec, w_up, w_down)]
    return stream(body, order, ins, [(o, by_rows(o)) for o in outs])


def forward_far(order, low, wu_parts, wd_far, part, normed, vec, vec_far, cotangent, act_own, spots, split):
    tokens, width = low.shape
    wide, hidden = wu_parts[0].shape[1], wd_far.shape[0]
    outs = [shape((tokens, w), BF) for w in (width, width, hidden)]
    sums = shape((3, width), F32)

    def body(io, me, full, acts):
        low_r, wu_one, wu_two, vf, wd, v, part_r, normed_r, tan_r, act_r = io.ins
        dffn_o, out_o, slope_o, sums_o = io.outs[2:]
        for c, r in enumerate(row_blocks(tokens)):

            def up():
                bias = spots(vf, "b_up")
                for j, wu in enumerate((wu_one, wu_two)):
                    lanes = slice(j * wide, (j + 1) * wide)
                    acts[:, lanes], slope_o[r, lanes] = gelu_both(plain(low_r[r, :], wu[...]) + bias[:, lanes])

            def down():
                ffn = part_r[r, :].astype(F32) + plain(acts[...], wd[...]) + spots(v, "b_down")
                first = normed_r[r, :].astype(F32) * spots(v, "gain_one") + spots(v, "shift_one")
                normed_two, inverse = normalize(first + ffn)
                gain = spots(v, "gain_two")
                out_o[r, :] = (normed_two * gain + spots(v, "shift_two")).astype(BF)
                tangent = tan_r[r, :].astype(F32)
                d_second = norm_backward(tangent, normed_two, inverse, gain)
                dffn_o[r, :] = d_second.astype(BF)
                more = [column_sum(d_second), column_sum(tangent * normed_two), column_sum(tangent)]
                add_to(sums_o, c == 0, jnp.concatenate(more, axis=0))

            io.step([(0, c), (1, 0), (2, 0), (3, 0)], [(4, c)], up)
            io.step([(4, 0), (5, 0), (6, c), (7, c), (8, c)], [(2, c), (3, c)], down)
        io.emit(5)
        for j in range(split.width // split.block):
            lanes = slice(j * split.block, (j + 1) * split.block)
            work = functools.partial(lambda j, lanes: split.write(io, 0, me, full, j, dffn_o[...], act_r[:, lanes]), j, lanes)
            io.step([(9, j)], [(0, j), (1, j)], work)

    ins = [(low, by_rows(low))] + [(a, everything(a)) for a in (*wu_parts, vec_far, wd_far, vec)]
    ins += [(a, by_rows(a)) for a in (part, normed, cotangent)] + [(act_own, by_columns(act_own, split.block), True)]
    outs = split.outs + [(o, by_rows(o)) for o in outs] + [(sums, everything(sums))]
    return stream(body, order, ins, outs, [split.scratch, pltpu.VMEM((ROWS, hidden), BF)])


def backward_own(order, d_ffn, slope, w_up, w_down, low, split):
    tokens, width = d_ffn.shape
    hidden = w_up.shape[1]

    def body(io, me, full, d_pres):
        d, wd, slope_r, wu, low_r = io.ins
        part_o, sums_o = io.outs[2:]
        for c, r in enumerate(row_blocks(tokens)):

            def pre():
                d_pre = (against(d[r, :], wd[...]) * slope_r[r, :].astype(F32)).astype(BF)
                d_pres[r, :] = d_pre
                add_to(sums_o, c == 0, column_sum(d_pre.astype(F32)))

            def first():
                part_o[r, :] = against(d_pres[r, :], wu[...]).astype(BF)

            io.step([(0, c), (1, 0), (2, c)], [], pre)
            io.step([(3, 0)], [(2, c)], first)
        io.emit(3)
        for j in range(split.width // split.block):
            lanes = slice(j * split.block, (j + 1) * split.block)
            work = functools.partial(lambda j, lanes: split.write(io, 0, me, full, j, low_r[...], d_pres[:, lanes]), j, lanes)
            io.step([(4, 0)], [(0, j), (1, j)], work)

    ins = [(d_ffn, by_rows(d_ffn)), (w_down, everything(w_down)), (slope, by_rows(slope))]
    ins += [(w_up, everything(w_up)), (low, everything(low), True)]
    part, sums = shape((tokens, width), BF), shape((1, hidden), F32)
    outs = split.outs + [(part, by_rows(part)), (sums, everything(sums))]
    return stream(body, order, ins, outs, [split.scratch, pltpu.VMEM((tokens, hidden), BF)])


def backward_far(order, d_ffn, slope, wu_parts, wd_far, part, normed, inverse, w_output, wo_far, vec, spots):
    tokens, width = d_ffn.shape
    local, wide, hidden = w_output.shape[0], wu_parts[0].shape[1], wd_far.shape[0]

    def body(io, me, d_pres):
        d, wd, slope_r, wu_one, wu_two, part_r, norm, inv, wo, wof, v = io.ins
        dattn_o, dctx_o, dfar_o, sums_o = io.outs
        for c, r in enumerate(row_blocks(tokens)):

            def pre():
                d_pres[...] = (against(d[r, :], wd[...]) * slope_r[r, :].astype(F32)).astype(BF)

            def first():
                d_first = d[r, :].astype(F32) + part_r[r, :].astype(F32)
                for j, wu in enumerate((wu_one, wu_two)):
                    d_first = d_first + against(d_pres[:, j * wide : (j + 1) * wide], wu[...])
                normed_one = norm[r, :].astype(F32)
                d_res = norm_backward(d_first, normed_one, inv[r, :], spots(v, "gain_one"))
                dattn_o[r, :] = d_res.astype(BF)
                more = [column_sum(d_res), column_sum(d_first * normed_one), column_sum(d_first)]
                add_to(sums_o, c == 0, jnp.concatenate(more, axis=0))

            def heads():
                dctx_o[r, :] = against(dattn_o[r, :], wo[...]).astype(BF)
                dfar_o[r, :] = against(dattn_o[r, :], wof[...]).astype(BF)

            io.step([(0, c), (1, 0), (2, c)], [], pre)
            io.step([(3, 0), (4, 0), (5, c), (6, c), (7, c), (10, 0)], [(0, c)], first)
            io.step([(8, 0), (9, 0)], [(1, c), (2, c)], heads)
        io.emit(3)

    ins = [(d_ffn, by_rows(d_ffn)), (wd_far, everything(wd_far)), (slope, by_rows(slope))]
    ins += [(a, everything(a)) for a in wu_parts]
    ins += [(a, by_rows(a)) for a in (part, normed, inverse)]
    ins += [(a, everything(a)) for a in (w_output, wo_far, vec)]
    outs = [shape((tokens, w), BF) for w in (width, local, local)]
    sums = shape((3, width), F32)
    outs = [(o, by_rows(o)) for o in outs] + [(sums, everything(sums))]
    return stream(body, order, ins, outs, [pltpu.VMEM((ROWS, hidden), BF)])


def weight_grad(order, pairs, split):
    ins, sums = [], shape((1, split.width), F32)
    for left, right, start, width in pairs:
        lanes = [(slice(None), slice(i, i + split.block)) for i in range(start, start + width, split.block)]
        ins += [(left, everything(left)), (right, lanes)]

    def body(io, me, full):
        done = 0
        for p, (_, _, start, width) in enumerate(pairs):
            for c in range(width // split.block):

                def work(p, c, done, start):
                    at = start + c * split.block
                    block = io.ins[2 * p + 1][:, at : at + split.block]
                    lanes = slice(done * split.block, (done + 1) * split.block)
                    io.outs[2][:, lanes] = column_sum(block.astype(F32))
                    split.write(io, 0, me, full, done, io.ins[2 * p][...], block)

                work = functools.partial(work, p, c, done, start)
                io.step([(2 * p, 0), (2 * p + 1, c)], [(0, done), (1, done)], work)
                done += 1
        io.emit(2)

    outs = split.outs + [(sums, everything(sums))]
    return stream(body, order, ins, outs, [split.scratch])


def small_call(body, order, args, out):
    return pl.pallas_call(
        lambda *refs: body(*refs[: len(args)], refs[-1]),
        in_specs=[VMEM] * len(args) + [ANY] * len(order.last),
        out_specs=VMEM,
        out_shape=out,
        compiler_params=pltpu.CompilerParams(vmem_limit_bytes=GRANT),
        cost_estimate=LONG,
    )(*args, *order.last)


def line_up_sums(order, parts):
    total = sum(v.shape[0] * (v.shape[1] - first) for v, first in parts)

    def body(*refs):
        at = 0
        for ref, (v, first) in zip(refs, parts):
            for row in range(v.shape[0]):
                size = v.shape[1] - first
                refs[-1][:, at : at + size] = ref[row : row + 1, first:]
                at += size

    result = small_call(body, order, [v for v, _ in parts], shape((1, total), F32))
    order.now(result)
    return result


def add_all(order, *values):
    def body(*refs):
        refs[-1][...] = sum(r[...] for r in refs[1:-1]) + refs[0][...]

    result = small_call(body, order, values, shape(values[0].shape, F32))
    order.now(result)
    return result


def finish_vectors(line, me, n, width, local, hidden):
    rows, heads_at = width // n, 3 * width
    late = heads_at + 3 * local
    starts = [0, width, 2 * width, late, late + width, late + 2 * width]

    def body(me_ref, line_ref, *outs):
        shift = jnp.where(me_ref[0] == 0, 0, width - me_ref[0] * rows)
        for start, out in zip(starts, outs):
            turned = pltpu.roll(jnp.broadcast_to(line_ref[:, start : start + width], (8, width)), shift, 1)
            out[...] = turned[0:1, :rows].reshape(rows)
        for j, out in ((0, outs[6]), (2, outs[7])):
            for p in range(local // PAIR):
                at = heads_at + (3 * p + j) * PAIR
                out[p * PAIR : (p + 1) * PAIR] = line_ref[:, at : at + PAIR].reshape(PAIR)
        outs[8][...] = line_ref[:, late + heads_at : late + heads_at + hidden].reshape(hidden)

    sizes = [rows] * 6 + [local] * 2 + [hidden]
    return pl.pallas_call(
        body,
        in_specs=[SMEM, VMEM],
        out_specs=[VMEM] * 9,
        out_shape=[shape((size,), F32) for size in sizes],
    )(me, line)


def finish_heads(one, two, local):
    rows = one.shape[0]

    def body(one_ref, two_ref, q, k, v, out):
        for j, ref in enumerate((q, k, v)):
            ref[:, :PAIR] = one_ref[:, local + j * PAIR : local + (j + 1) * PAIR]
            for p in range(1, local // PAIR):
                at = (3 * (p - 1) + j) * PAIR
                ref[:, p * PAIR : (p + 1) * PAIR] = two_ref[:, at : at + PAIR]
        out[...] = one_ref[:, :local].T

    return pl.pallas_call(
        body,
        in_specs=[VMEM, VMEM],
        out_specs=[VMEM] * 4,
        out_shape=[shape((rows, local), F32)] * 3 + [shape((local, rows), F32)],
    )(one, two)


def inputs_grad(order, d_res, grads, w_own, w_far):
    tokens, width = d_res.shape
    pairs = w_own[0].shape[1] // PAIR
    wide = 6 * PAIR * pairs
    after, many, blocks = order.last, len(grads), tokens // ROWS

    def body(me_ref, *refs):
        always = me_ref[0] >= 0
        res_far, gs, (wq, wk, wv) = refs[0], refs[1 : 1 + many], refs[1 + many : 4 + many]
        wfs = refs[4 + many : 4 + many + len(w_far)]
        out_far, res, g_all, w_all, out, w_sem, g_sem, res_sem, out_sem = refs[4 + many + len(w_far) + len(after) :]
        w_copies, g_copies = [], []
        for p in range(pairs):
            for j, w in enumerate((wq, wk, wv)):
                at = (3 * p + j) * PAIR
                src, dst = w.at[:, p * PAIR : (p + 1) * PAIR], w_all.at[:, at : at + PAIR]
                w_copies.append(pltpu.make_async_copy(src, dst, w_sem.at[3 * p + j]))
        at = wide // 2
        for k, w in enumerate(wfs):
            size = w.shape[1]
            w_copies.append(pltpu.make_async_copy(w, w_all.at[:, at : at + size], w_sem.at[3 * pairs + k]))
            at += size
        for c, r in enumerate(row_blocks(tokens)):
            at, copies = 0, []
            for k, g in enumerate(gs):
                size = g.shape[1]
                copies.append(pltpu.make_async_copy(g.at[r, :], g_all.at[r, at : at + size], g_sem.at[c, k]))
                at += size
            copies.append(pltpu.make_async_copy(res_far.at[r, :], res.at[r, :], res_sem.at[c]))
            g_copies.append(copies)
        for copy in w_copies + [x for copies in g_copies for x in copies]:
            copy.start()
        for copy in w_copies:
            copy.wait()
        sent = []
        for c, r in enumerate(row_blocks(tokens)):
            for copy in g_copies[c]:
                copy.wait()

            @pl.when(always)
            def _():
                out[r, :] = (res[r, :].astype(F32) + against(g_all[r, :], w_all[...])).astype(BF)

            sent.append(pltpu.make_async_copy(out.at[r, :], out_far.at[r, :], out_sem.at[c]))
            sent[-1].start()
        for copy in sent:
            copy.wait()

    result = pl.pallas_call(
        body,
        in_specs=[SMEM] + [ANY] * (4 + many + len(w_far) + len(after)),
        out_specs=ANY,
        out_shape=shape((tokens, width), BF),
        scratch_shapes=[
            pltpu.VMEM((tokens, width), BF),
            pltpu.VMEM((tokens, wide), BF),
            pltpu.VMEM((width, wide), BF),
            pltpu.VMEM((tokens, width), BF),
            pltpu.SemaphoreType.DMA((3 * pairs + len(w_far),)),
            pltpu.SemaphoreType.DMA((blocks, many)),
            pltpu.SemaphoreType.DMA((blocks,)),
            pltpu.SemaphoreType.DMA((blocks,)),
        ],
        compiler_params=pltpu.CompilerParams(vmem_limit_bytes=GRANT),
        cost_estimate=LONG,
    )(order.me, d_res, *grads, *w_own, *w_far, *after)
    order.now(result)
    return result


def per_device(
    inputs,
    lengths,
    w_query,
    b_query,
    w_key,
    w_value,
    b_value,
    w_output,
    b_output,
    gain_one,
    shift_one,
    w_up,
    b_up,
    w_down,
    b_down,
    gain_two,
    shift_two,
    cotangent,
    *,
    n,
):
    count, length, width = inputs.shape
    local, hidden = w_query.shape[1], w_up.shape[1]
    pairs = local // PAIR
    tokens = count * length
    flat = inputs.reshape(tokens, width)
    tangent = cotangent.reshape(tokens, width)
    me = lax.axis_index("dp").astype(jnp.int32).reshape(1)
    names = ("b_up", "b_query", "b_value", "b_output", "gain_one", "shift_one", "b_down", "gain_two", "shift_two")
    given = (b_up, b_query, b_value, b_output, gain_one, shift_one, b_down, gain_two, shift_two)
    offsets, at = {}, 0
    for name, v in zip(names, given):
        offsets[name] = (at, v.shape[0])
        at += v.shape[0]

    def line_up(*refs):
        for name, ref in zip(names, refs):
            start, size = offsets[name]
            refs[-1][:, start : start + size] = ref[...].astype(F32).reshape(1, size)

    vec = pl.pallas_call(
        line_up,
        in_specs=[VMEM] * len(given),
        out_specs=VMEM,
        out_shape=shape((1, at), F32),
    )(*given)

    def spots(ref, name):
        start, size = offsets[name]
        return ref[:, start : start + size]

    y_bits, z_bits = (1, 2), (1, 4)
    quarter, half, few = width // 4, hidden // 2, local // 4

    def heads(w3, p, out, at):
        for j, w in enumerate(w3):
            out[:, at + j * PAIR : at + (j + 1) * PAIR] = w[:, p * PAIR : (p + 1) * PAIR].astype(F32)

    def prepare_one(me_ref, wq, wk, wv, one):
        heads((wq, wk, wv), 0, one, 0)

    def prepare_two(me_ref, wq, wk, wv, before, two):
        for p in range(1, pairs):
            heads((wq, wk, wv), p, two, 3 * PAIR * (p - 1))

    def prepare_pieces(me_ref, w_one, w_two, before, out_one, out_two):
        out_one[...] = w_one[...].astype(F32)
        out_two[...] = w_two[...].astype(F32)

    def prepare_piece(me_ref, w, before, out):
        out[...] = w[...].astype(F32)

    def piece(rows, cols, which, col=0):
        return pl.BlockSpec((rows, cols), lambda i, m: (index_of(m[0], which), col))

    def pieces_of(body, in_specs, sizes, *args):
        return pl.pallas_call(
            body,
            grid_spec=pltpu.PrefetchScalarGridSpec(
                num_scalar_prefetch=1,
                grid=(1,),
                in_specs=in_specs,
                out_specs=[pl.BlockSpec(size, lambda i, m: (0, 0)) for size in sizes],
            ),
            out_shape=[shape(size, F32) for size in sizes],
            compiler_params=pltpu.CompilerParams(vmem_limit_bytes=GRANT),
            cost_estimate=LONG,
        )(me, *args)

    d_bits, d_rows = (1, 2, 4), hidden // 8
    own_w = (w_query, w_key, w_value)
    order = Order(me)

    def prepare(body, in_specs, groups, *args):
        made = pieces_of(body, in_specs + [ANY] * len(order.last), [size for size, _ in groups], *args, *order.last)
        order.now(made[0])
        return [Gather(send, which, n) for send, (_, which) in zip(made, groups)]

    rest = 3 * PAIR * (pairs - 1)
    (one,) = prepare(prepare_one, [piece(quarter, PAIR, y_bits)] * 3, [((quarter, 3 * PAIR), y_bits)], *own_w)
    (two,) = prepare(prepare_two, [piece(quarter, local, z_bits)] * 3, [((quarter, rest), z_bits)], *own_w)
    vec_far = swap_x(vec)
    bias_at = [offsets["b_query"][0], offsets["b_value"][0]]
    own_bias = [(vec, a) for a in bias_at]
    own = attend(order, lengths, flat, own_w, own_bias, count, pairs, (0,))
    out, down = prepare(
        prepare_pieces,
        [piece(few, width, y_bits), piece(d_rows, width, d_bits)],
        [((few, width), y_bits), ((d_rows, width), d_bits)],
        w_output,
        w_down,
    )
    one.hop(order, 0, 1, 0)
    vec_far = order.then(vec_far)
    far_bias = [(vec_far, a) for a in bias_at]
    qkv, ctx, lse = attend(order, lengths, flat, own_w, own_bias, count, pairs, range(1, pairs), own)
    (up_one,) = prepare(prepare_piece, [piece(quarter, half, y_bits)], [((quarter, half), y_bits)], w_up)
    one.hop(order, 1)
    two.hop(order, 0, 1, 0)
    one.hop(order, 2, 0)
    one.hop(order, 3)
    w_one = one.place(order, me, [(width, 3 * PAIR)], in_rows(quarter))
    two.hop(order, 1)
    far = attend(order, lengths, flat, w_one, far_bias, count, pairs, (0,))
    (up_two,) = prepare(prepare_piece, [piece(quarter, half, y_bits, 1)], [((quarter, half), y_bits)], w_up)
    out.hop(order, 0, 1, 0)
    two.hop(order, 2, 0)
    down.hop(order, 0, 1, 2, 0)
    two.hop(order, 3)
    w_two = two.place(order, me, [(width, rest)], in_rows(quarter))
    out.hop(order, 1)
    out.hop(order, 2, 0)
    down.hop(order, 1)
    far = attend(order, lengths, flat, w_two, far_bias, count, pairs, range(1, pairs), far)
    qkv_far, ctx_far, lse_far = far
    up_one.hop(order, 0, 1, 0)
    down.hop(order, 2, 2, 0)
    out.hop(order, 3)
    (wo_far,) = out.place(order, me, [(local, width)], in_rows(few))
    down.hop(order, 3)
    down.hop(order, 4, 0)
    up_two.hop(order, 0, 1, 0)
    up_one.hop(order, 1)
    down.hop(order, 5)
    low, normed, act, slope, part, inverse = forward_own(
        order, ctx, ctx_far, flat, w_output, wo_far, w_up, w_down, vec, spots
    )
    up_one.hop(order, 2, 0)
    down.hop(order, 6, 0)
    up_one.hop(order, 3)
    wu_one = up_one.place(order, me, [(width, half)], in_rows(quarter))
    down.hop(order, 7)
    (wd_far,) = down.place(order, me, [(hidden, width)], in_rows(d_rows))
    up_two.hop(order, 1)
    up_two.hop(order, 2, 0)
    up_two.hop(order, 3)
    wu_far = (*wu_one, *up_two.place(order, me, [(width, half)], in_rows(quarter)))

    bits = [1 << i for i in range(n.bit_length() - 1)]
    y_first = tuple(bits)
    z_first = (bits[0], bits[2], bits[1]) + tuple(bits[3:])
    block = WIDE if hidden % WIDE == 0 else hidden
    down_split, up_split = Split(width, hidden, block, n, y_first), Split(width, hidden, block, n, z_first)
    group_splits = [Split(width, 6 * PAIR, 3 * PAIR, n, bits_of) for bits_of in (y_first, y_first)]
    send, keep, d_ffn, layer_out, slope_far, sums_two = forward_far(
        order, low, wu_far, wd_far, part, normed, vec, vec_far, tangent, act, spots, down_split
    )
    down_sum = down_split.scatter(me, send, keep, order)
    send, keep, d_part, sums_up = backward_own(order, d_ffn, slope, w_up, w_down, low, up_split)
    up_sum = up_split.scatter(me, send, keep, order)

    class Vectors:
        def __init__(self, parts):
            self.value, self.arriving = line_up_sums(order, parts), []

        def send(self, *over):
            masks = [sum(b for j, b in enumerate(over) if (m >> j) & 1) for m in range(1, 1 << len(over))]
            self.arriving = [swap_dp(self.value, mask, n) for mask in masks]

        def add(self):
            self.value = add_all(order, self.value, *[order.then(v) for v in self.arriving])

    early = Vectors([(sums_two, 0), (sums_up, 0)])
    early.send(bits[0])
    wide = 3 * PAIR
    st = {}

    def far_back(which):
        st.setdefault("far", []).append(attend_back(order, lengths, qkv_far, lse_far, d_ctx_far, count, which))

    def own_back(which):
        st.setdefault("own", []).append(attend_back(order, lengths, qkv, lse, d_ctx, count, which))

    for step in PLAN:
        if step == "B2":
            d_attn, d_ctx, d_ctx_far, sums_one = backward_far(
                order, d_ffn, slope_far, wu_far, wd_far, d_part, normed, inverse, w_output, wo_far, vec, spots
            )
        elif step == "OA":
            own_back(range(pairs))
        elif step == "O0":
            own_back((0,))
        elif step == "O1":
            own_back(range(1, pairs))
        elif step == "FA":
            far_back(range(pairs))
        elif step == "F0":
            far_back((0,))
        elif step == "F1":
            far_back(range(1, pairs))
        elif step == "G1":
            parts = [(d_attn, ctx, 0, local), (flat, st["own"][0], 0, wide)]
            send, keep, sums_a = weight_grad(order, parts, group_splits[0])
            group_one = group_splits[0].scatter(me, send, keep, order)
        elif step == "G2":
            own = (flat, st["own"][0], wide, wide * (pairs - 1)) if len(st["own"]) == 1 else (flat, st["own"][1], 0, wide * (pairs - 1))
            send, keep, sums_b = weight_grad(order, [own], group_splits[1])
            group_two = group_splits[1].scatter(me, send, keep, order)
        elif step == "IG":
            grad_inputs = inputs_grad(order, d_attn, [*st["own"], *st["far"]], own_w, (*w_one, *w_two))
        elif step == "L":
            late = Vectors([(sums_one, 0), (sums_a, local), (sums_b, 0)])
            late.send(bits[0])
        elif step == "L1":
            late.add()
            late.value = line_up_sums(order, [(late.value, 0), (early.value, 0)])
            left = [bits[i : i + 2] for i in range(1, len(bits), 2)]
            late.send(*left[0])
        elif step == "L2":
            late.add()
            left = left[1:]
            late.send(*left[0])
        elif step == "L3":
            late.add()
        elif step == "E":
            early.add()
        else:
            names_of = {"D": down_sum, "U": up_sum}
            if "A" in step or "B" in step:
                names_of["A"] = group_one
            if "B" in step:
                names_of["B"] = group_two
            advance(order, *[names_of[k] for k in step])
    for s in (down_sum, up_sum, group_one, group_two):
        while s.step < len(bits):
            advance(order, s)
    for over in left[1:]:
        late.send(*over)
        late.add()
    rows = width // n
    small = finish_vectors(late.value, me, n, width, local, hidden)
    by_columns_of = group_one.result, group_two.result
    if rows % 8 == 0:
        g_query, g_key, g_value, g_output = finish_heads(*by_columns_of, local)
    else:
        g_output = group_one.result[:, :local].T
        heads_of = jnp.concatenate([group_one.result[:, local:], group_two.result], axis=1)
        g_query, g_key, g_value = [heads_of.reshape(rows, pairs, 3, PAIR)[:, :, j].reshape(rows, local) for j in range(3)]
    b_output_g, gain_one_g, shift_one_g, b_down_g, gain_two_g, shift_two_g, b_query_g, b_value_g, b_up_g = small
    return (
        layer_out.reshape(count, length, width),
        grad_inputs.reshape(count, length, width),
        g_query,
        b_query_g,
        g_key,
        g_value,
        b_value_g,
        g_output,
        b_output_g,
        gain_one_g,
        shift_one_g,
        up_sum.result,
        b_up_g,
        down_sum.result.T,
        b_down_g,
        gain_two_g,
        shift_two_g,
    )


def solution(mesh):
    in_specs = (
        P("dp", None, None),
        P("dp"),
        P(None, "tensor"),
        P("tensor"),
        P(None, "tensor"),
        P(None, "tensor"),
        P("tensor"),
        P("tensor", None),
        P(),
        P(),
        P(),
        P(None, "tensor"),
        P("tensor"),
        P("tensor", None),
        P(),
        P(),
        P(),
        P("dp", None, None),
    )
    out_specs = (
        P("dp", None, None),
        P("dp", None, None),
        P("dp", "tensor"),
        P("tensor"),
        P("dp", "tensor"),
        P("dp", "tensor"),
        P("tensor"),
        P("tensor", "dp"),
        P("dp"),
        P("dp"),
        P("dp"),
        P("dp", "tensor"),
        P("tensor"),
        P("tensor", "dp"),
        P("dp"),
        P("dp"),
        P("dp"),
    )
    return jax.shard_map(
        functools.partial(per_device, n=mesh.shape["dp"]),
        mesh=mesh,
        in_specs=in_specs,
        out_specs=out_specs,
        check_vma=False,
    )
```

```python
import functools
import math

import jax
import jax.numpy as jnp
from jax import lax
from jax.experimental import pallas as pl
from jax.experimental.pallas import tpu as pltpu
from jax.sharding import PartitionSpec as P

DH = 64
PAIR = 2 * DH
PLAN = ('D', 'U', 'E', 'B2', 'O0', 'G1', 'D', 'U', 'A', 'O1', 'G2', 'D', 'U', 'B', 'L', 'FA', 'A', 'B', 'L1', 'IG', 'D', 'U', 'A', 'B', 'A', 'L2', 'B', 'L3')
ROWS = 512
WIDE = 512
GRANT = 60 * 1024 * 1024
FLYING = 6 * 1024 * 1024
LONG = pl.CostEstimate(flops=10**13, bytes_accessed=10**6, transcendentals=0)

norm_eps = 1e-12
masked_score = -1000000000.0
BF = jnp.bfloat16
F32 = jnp.float32
SMEM = pl.BlockSpec(memory_space=pltpu.SMEM)
VMEM = pl.BlockSpec(memory_space=pltpu.VMEM)
ANY = pl.BlockSpec(memory_space=pl.ANY)


def shape(dims, kind):
    return jax.ShapeDtypeStruct(tuple(dims), kind)


def against(left, right):
    return lax.dot_general(left, right, (((1,), (1,)), ((), ())), preferred_element_type=F32)


def over_rows(left, right):
    return lax.dot_general(left, right, (((0,), (0,)), ((), ())), preferred_element_type=F32)


def plain(left, right):
    return jnp.dot(left, right, preferred_element_type=F32)


def tie(value, *before):
    return pl.pallas_call(
        lambda *refs: None,
        in_specs=[ANY] * (1 + len(before)),
        out_specs=ANY,
        out_shape=shape(value.shape, value.dtype),
        input_output_aliases={0: 0},
        compiler_params=pltpu.CompilerParams(vmem_limit_bytes=GRANT),
        cost_estimate=LONG,
    )(value, *before)


def pause(*before):
    return pl.pallas_call(
        lambda *refs: None,
        in_specs=[ANY] * len(before),
        out_specs=ANY,
        out_shape=shape((8, PAIR), F32),
        cost_estimate=LONG,
    )(*before)


class Order:
    def __init__(self, me):
        self.me, self.last = me, ()

    def then(self, value):
        self.last = (pause(*self.last),)
        value = tie(value, *self.last)
        self.last = (value,)
        return value

    def now(self, *values):
        self.last = tuple(values)


def call(body, order, args, outs, in_specs, out_specs, grid, scratch=(), alias=None):
    count, after = len(args), order.last

    def run(*refs):
        body(*refs[:count], *refs[count + len(after) :])

    result = pl.pallas_call(
        run,
        grid=grid,
        in_specs=list(in_specs) + [ANY] * len(after),
        out_specs=list(out_specs),
        out_shape=outs,
        scratch_shapes=list(scratch),
        input_output_aliases=alias or {},
        compiler_params=pltpu.CompilerParams(vmem_limit_bytes=GRANT),
        cost_estimate=LONG,
    )(*args, *after)
    order.now(result[0])
    return result


def everything(array):
    return [(slice(None),) * len(array.shape)]


def by_rows(array):
    return [(slice(i, i + ROWS), slice(None)) for i in range(0, array.shape[0], ROWS)]


def by_columns(array, width):
    return [(slice(None), slice(i, i + width)) for i in range(0, array.shape[1], width)]


class Stream:
    def __init__(self, ins, in_parts, out_parts, far, near, sems, queue, always):
        self.always = always
        self.in_far, self.out_far = far[:ins], far[ins:]
        self.ins, self.outs = near[:ins], near[ins:]
        self.in_parts, self.out_parts = in_parts, out_parts
        self.in_sems, self.out_sems = sems[:ins], sems[ins:]
        self.queue, self.started, self.waited, self.flying, self.sent = queue, 0, set(), 0, []
        self.top_up()

    def fetch(self, k, c):
        at = self.in_parts[k][c]
        return pltpu.make_async_copy(self.in_far[k].at[at], self.ins[k].at[at], self.in_sems[k].at[c])

    def size(self, k, c):
        return math.prod(self.ins[k].at[self.in_parts[k][c]].shape) * self.ins[k].dtype.itemsize

    def start_next(self):
        k, c = self.queue[self.started]
        self.fetch(k, c).start()
        self.flying += self.size(k, c)
        self.started += 1

    def top_up(self):
        while self.started < len(self.queue) and self.flying < FLYING:
            self.start_next()

    def need(self, k, c=0):
        if (k, c) not in self.waited:
            self.waited.add((k, c))
            while (k, c) not in self.queue[: self.started]:
                self.start_next()
            self.fetch(k, c).wait()
            self.flying -= self.size(k, c)
            self.top_up()
        return self.ins[k]

    def step(self, needs, emits, work):
        for k, c in needs:
            self.need(k, c)
        pl.when(self.always)(work)
        for k, c in emits:
            self.emit(k, c)

    def emit(self, k, c=0):
        at = self.out_parts[k][c]
        copy = pltpu.make_async_copy(self.outs[k].at[at], self.out_far[k].at[at], self.out_sems[k].at[c])
        copy.start()
        self.sent.append(copy)


def stream(body, order, ins, outs, scratch=()):
    smem = (order.me,)
    arrays = [i[0] for i in ins]
    in_parts, out_parts = [i[1] for i in ins], [o[1] for o in outs]
    after, n_in, n_out = order.last, len(ins), len(outs)
    queue = [(c, k) for k, p in enumerate(in_parts) for c in range(len(p))]
    queue = [(k, c) for late, c, k in sorted((len(ins[k]) > 2, c, k) for c, k in queue)]

    def run(*refs):
        small, refs = refs[: len(smem)], refs[len(smem) :]
        far_in, refs = refs[:n_in], refs[n_in + len(after) :]
        far_out, refs = refs[:n_out], refs[n_out:]
        near, refs = refs[: n_in + n_out], refs[n_in + n_out :]
        sems, rest = refs[: n_in + n_out], refs[n_in + n_out :]
        io = Stream(n_in, in_parts, out_parts, far_in + far_out, near, sems, queue, small[0][0] >= 0)
        body(io, small[0][0], *rest)
        for k, c in queue:
            io.need(k, c)
        for copy in io.sent:
            copy.wait()

    result = pl.pallas_call(
        run,
        in_specs=[SMEM] * len(smem) + [ANY] * (n_in + len(after)),
        out_specs=[ANY] * n_out,
        out_shape=[o[0] for o in outs],
        scratch_shapes=[pltpu.VMEM(a.shape, a.dtype) for a in arrays]
        + [pltpu.VMEM(o[0].shape, o[0].dtype) for o in outs]
        + [pltpu.SemaphoreType.DMA((len(p),)) for p in in_parts + out_parts]
        + list(scratch),
        compiler_params=pltpu.CompilerParams(vmem_limit_bytes=GRANT),
        cost_estimate=LONG,
    )(*smem, *arrays, *after)
    order.now(result[0])
    return result


def whole(*dims):
    return pl.BlockSpec(dims, lambda *i: (0,) * len(dims))


def row_blocks(tokens):
    return [slice(i, i + ROWS) for i in range(0, tokens, ROWS)]


def swap_x(value):
    return lax.ppermute(value, "tensor", [(0, 1), (1, 0)])


def swap_dp(value, bit, n):
    return lax.ppermute(value, "dp", [(i, i ^ bit) for i in range(n)])


def index_of(me, bits):
    total = 0
    for j, bit in enumerate(bits):
        total = total + jnp.where(jnp.bitwise_and(me, bit) != 0, 1 << j, 0)
    return total


class Gather:
    def __init__(self, mine, bits, n):
        self.bits, self.n = bits, n
        self.pieces = {0: swap_x(mine)}

    def hop(self, order, slot, *steps):
        self.pieces[slot] = order.then(self.pieces[slot])
        for j in steps:
            self.pieces[slot | (1 << j)] = swap_dp(self.pieces[slot], self.bits[j], self.n)

    def place(self, order, me, outs, cut):
        slots = list(self.pieces)
        count, after = len(slots), order.last
        dims = self.pieces[0].shape
        many = len(cut(0))

        def body(me_ref, *refs):
            far, refs = refs[:count], refs[count + len(after) :]
            out, (wide, low, in_sem, out_sem) = refs[: len(outs)], refs[len(outs) :]
            always = me_ref[0] >= 0
            base = index_of(me_ref[0], self.bits)
            ins = [pltpu.make_async_copy(far[k], wide.at[k], in_sem.at[k]) for k in range(count)]
            for copy in ins:
                copy.start()
            sent = []
            for k, slot in enumerate(slots):
                ins[k].wait()

                @pl.when(always)
                def _():
                    low[k] = wide[k].astype(BF)

                for j, (inner, which, outer) in enumerate(cut(jnp.bitwise_xor(base, slot))):
                    sent.append(pltpu.make_async_copy(low.at[(k, *inner)], out[which].at[outer], out_sem.at[k, j]))
                    sent[-1].start()
            for copy in sent:
                copy.wait()

        result = pl.pallas_call(
            body,
            in_specs=[SMEM] + [ANY] * (count + len(after)),
            out_specs=[ANY] * len(outs),
            out_shape=[shape(o, BF) for o in outs],
            scratch_shapes=[
                pltpu.VMEM((count, *dims), F32),
                pltpu.VMEM((count, *dims), BF),
                pltpu.SemaphoreType.DMA((count,)),
                pltpu.SemaphoreType.DMA((count, many)),
            ],
            compiler_params=pltpu.CompilerParams(vmem_limit_bytes=GRANT),
            cost_estimate=LONG,
        )(me, *[self.pieces[s] for s in slots], *after)
        order.now(result[0])
        return result


def rows_at(place, rows):
    return pl.ds(pl.multiple_of(place * rows, rows), rows)


def in_rows(rows):
    everything = slice(None)
    return lambda place: [((everything, everything), 0, (rows_at(place, rows), everything))]


class Split:
    def __init__(self, rows, width, block, n, order_of_bits):
        self.rows, self.width, self.block, self.n, self.bits = rows, width, block, n, order_of_bits
        steps = len(order_of_bits)
        self.chunks = [
            sum(bit for j, bit in enumerate(order_of_bits) if (r >> (steps - 1 - j)) & 1) for r in range(n)
        ]
        self.inside = (rows // n) % 8 == 0
        half = shape((rows // 2, width), F32)
        self.outs = [(half, by_columns(half, block))] * 2
        self.scratch = pltpu.VMEM((rows, block), F32)

    def write(self, io, first, me, full, done, left, right):
        send, keep = io.outs[first : first + 2]
        small, half = self.rows // self.n, self.rows // 2
        lanes = slice(done * self.block, (done + 1) * self.block)
        full[...] = over_rows(left, right)
        for r, chunk in enumerate(self.chunks):
            out, low = (keep, r * small) if r < self.n // 2 else (send, r * small - half)
            at = jnp.bitwise_xor(me, chunk) * small if self.inside else r * small
            at = pl.multiple_of(at, small) if self.inside else at
            out[low : low + small, lanes] = full[pl.ds(at, small), :]

    def scatter(self, me, send, keep, order):
        if not self.inside:
            wanted = jnp.bitwise_xor(me[0], jnp.array(self.chunks, jnp.int32))
            full = jnp.concatenate([keep, send], axis=0).reshape(self.n, -1, self.width)[wanted]
            full = full.reshape(self.rows, self.width)
            keep, send = full[: self.rows // 2], full[self.rows // 2 :]
        order.now(send)
        return Scatter(send, keep, self.n, self.bits)


def add_rows(order, sums):
    ins, outs, places = [], [], []
    for parts, low, high in sums:
        width = parts[0].shape[1]
        lanes = [slice(i, i + width // 2) for i in (0, width // 2)]
        out = shape((high - low, width), F32)
        places.append((len(ins), len(parts), low, high, lanes))
        ins += [(p, [(slice(low, high), lane) for lane in lanes]) for p in parts]
        outs.append((out, [(slice(None), lane) for lane in lanes]))

    def body(io, me):
        for c in range(2):
            for k, (first, count, low, high, lanes) in enumerate(places):

                def work():
                    total = io.ins[first][low:high, lanes[c]]
                    for j in range(1, count):
                        total = total + io.ins[first + j][low:high, lanes[c]]
                    io.outs[k][:, lanes[c]] = total

                io.step([(first + j, c) for j in range(count)], [(k, c)], work)

    return stream(body, order, ins, outs)


def advance(order, *scatters):
    sums = []
    for s in scatters:
        s.step += 1
        s.parts[-1] = order.then(s.parts[-1])
        size = s.parts[-1].shape[0]
        sums.append((s.parts, *((0, size) if s.step == len(s.bits) else (size // 2, size))))
    if all((high - low) % 8 == 0 for _, low, high in sums):
        totals = add_rows(order, sums)
    else:
        totals = [sum(p[low:high] for p in parts[1:]) + parts[0][low:high] for parts, low, high in sums]
        order.now(*totals)
    for s, total in zip(scatters, totals):
        if s.step == len(s.bits):
            s.result = total
        else:
            s.parts.append(swap_dp(total, s.bits[s.step], s.n))


class Scatter:
    def __init__(self, send, keep, n, order_of_bits):
        self.n, self.bits, self.step = n, order_of_bits, 0
        self.parts = [keep, swap_dp(send, self.bits[0], n)]


def by_length(real, length, work):
    quarter = length // 4
    for k in range(1, 5):
        fits = real <= quarter if k == 1 else (real > quarter * (k - 1)) & (real <= quarter * k)
        pl.when(real > quarter * 3 if k == 4 else fits)(functools.partial(work, quarter * k))


def attend_body(real, x, w, bias, qkv_ref, ctx_ref, lse_ref):
    length = x.shape[0]
    qkv_ref[...] = (plain(x, w) + bias).astype(BF)
    lane = lax.broadcasted_iota(jnp.int32, (1, PAIR), 1)

    def work(count):
        valid = lax.broadcasted_iota(jnp.int32, (count, 1), 0) < real
        query = qkv_ref[:, 0:PAIR] * BF(0.125)
        keys = qkv_ref[:count, PAIR : 2 * PAIR]
        values_t = qkv_ref[:count, 2 * PAIR : 3 * PAIR].T
        outs, logs = [], []
        for h in range(2):
            mine = (lane < DH) if h == 0 else (lane >= DH)
            q = jnp.where(mine, query, BF(0))
            s = against(keys, q)
            s = jnp.where(valid, s, masked_score)
            top = jnp.max(s, axis=0, keepdims=True)
            e = jnp.exp(s - top)
            total = jnp.sum(e, axis=0, keepdims=True)
            p = (e * (1.0 / total)).astype(BF)
            outs.append(plain(values_t[h * DH : (h + 1) * DH, :], p))
            logs.append(top + jnp.log(total))
        ctx_ref[...] = jnp.concatenate(outs, axis=0).T.astype(BF)
        lse_ref[0, 0] = jnp.concatenate(logs, axis=0)

    by_length(real, length, work)


def attend(order, lengths, flat, weights, biases, count, pairs, which, kept=()):
    tokens, width = flat.shape
    length = tokens // count
    own = len(weights) == 3
    first, steps = which[0], len(which)
    if own:
        w_specs = [pl.BlockSpec((width, PAIR), lambda p, s: (0, first + p))] * 3
    else:
        w_specs = [pl.BlockSpec((width, 3 * PAIR), lambda p, s: (0, p))]
    b_specs = [pl.BlockSpec((1, PAIR), lambda p, s, at=at: (0, at // PAIR + first + p)) for _, at in biases]
    many = len(weights)

    def body(len_ref, x_ref, *refs):
        ws, bs, outs = refs[:many], refs[many : many + 2], refs[many + 2 + len(kept) :]
        w = jnp.concatenate([r[...] for r in ws], axis=1) if own else ws[0][...]
        bias = jnp.concatenate([bs[0][...], jnp.zeros((1, PAIR), F32), bs[1][...]], axis=1)
        attend_body(len_ref[pl.program_id(1)], x_ref[...], w, bias, *outs)

    return call(
        body,
        order,
        (lengths, flat, *weights, *[b for b, _ in biases], *kept),
        [
            shape((tokens, 3 * PAIR * pairs), BF),
            shape((tokens, PAIR * pairs), BF),
            shape((count, pairs, 2, length), F32),
        ],
        [SMEM, pl.BlockSpec((length, width), lambda p, s: (s, 0))] + w_specs + b_specs + [ANY] * len(kept),
        [
            pl.BlockSpec((length, 3 * PAIR), lambda p, s: (s, first + p)),
            pl.BlockSpec((length, PAIR), lambda p, s: (s, first + p)),
            pl.BlockSpec((1, 1, 2, length), lambda p, s: (s, first + p, 0, 0)),
        ],
        (steps, count),
        alias={4 + many + j: j for j in range(len(kept))})


def attend_back_body(len_ref, x_ref, lse_ref, dc_ref, out_ref):
    length = x_ref.shape[0]
    real = len_ref[pl.program_id(1)]
    lane = lax.broadcasted_iota(jnp.int32, (1, PAIR), 1)

    def work(count):
        valid = lax.broadcasted_iota(jnp.int32, (count, 1), 0) < real
        query = x_ref[:, 0:PAIR] * BF(0.125)
        keys = x_ref[:count, PAIR : 2 * PAIR]
        keys_t = keys.T
        values = x_ref[:count, 2 * PAIR : 3 * PAIR]
        d_ctx = dc_ref[...]
        dq, dk, dv = [], [], []
        for h in range(2):
            mine = (lane < DH) if h == 0 else (lane >= DH)
            q = jnp.where(mine, query, BF(0))
            s = against(keys, q)
            s = jnp.where(valid, s, masked_score)
            p = jnp.exp(s - lse_ref[0, 0, h : h + 1, :])
            dv.append(plain(p.astype(BF), d_ctx))
            dp = against(values, jnp.where(mine, d_ctx, BF(0)))
            row = jnp.sum(p * dp, axis=0, keepdims=True)
            ds = (p * (dp - row)).astype(BF)
            dk.append(plain(ds, query))
            dq.append(plain(keys_t[h * DH : (h + 1) * DH, :], ds))
        first = lane < DH
        out_ref[:, 0:PAIR] = (jnp.concatenate(dq, axis=0) * 0.125).T.astype(BF)
        out_ref[:count, PAIR : 2 * PAIR] = jnp.where(first, dk[0], dk[1]).astype(BF)
        out_ref[:count, 2 * PAIR : 3 * PAIR] = jnp.where(first, dv[0], dv[1]).astype(BF)
        if count < length:
            out_ref[count:, PAIR : 3 * PAIR] = jnp.zeros((length - count, 2 * PAIR), BF)

    by_length(real, length, work)


def attend_back(order, lengths, qkv, lse, d_ctx, count, which):
    tokens = qkv.shape[0]
    length = tokens // count
    first, steps = which[0], len(which)
    return call(
        attend_back_body,
        order,
        (lengths, qkv, lse, d_ctx),
        [shape((tokens, 3 * PAIR * steps), BF)],
        [
            SMEM,
            pl.BlockSpec((length, 3 * PAIR), lambda p, s: (s, first + p)),
            pl.BlockSpec((1, 1, 2, length), lambda p, s: (s, first + p, 0, 0)),
            pl.BlockSpec((length, PAIR), lambda p, s: (s, first + p)),
        ],
        [pl.BlockSpec((length, 3 * PAIR), lambda p, s: (s, p))],
        (steps, count))[0]


def gelu_both(value):
    phi_big = 0.5 + 0.5 * lax.erf(value * math.sqrt(0.5))
    phi_small = jnp.exp(-0.5 * value * value) * (1.0 / math.sqrt(2.0 * math.pi))
    return (value * phi_big).astype(BF), (phi_big + value * phi_small).astype(BF)


def normalize(values):
    center = values - jnp.mean(values, axis=-1, keepdims=True)
    spread = jnp.mean(center * center, axis=-1, keepdims=True)
    inverse = lax.rsqrt(spread + norm_eps)
    return center * inverse, inverse


def norm_backward(grad, normed, inverse, gain):
    scaled = grad * gain
    mean_one = jnp.mean(scaled, axis=-1, keepdims=True)
    mean_two = jnp.mean(scaled * normed, axis=-1, keepdims=True)
    return inverse * (scaled - mean_one - normed * mean_two)


def column_sum(values):
    return jnp.sum(values, axis=0, keepdims=True)


def add_to(ref, first, values):
    ref[...] = values if first else ref[...] + values


def forward_own(order, ctx, ctx_far, flat, w_output, wo_far, w_up, w_down, vec, spots):
    tokens, width = flat.shape
    hidden = w_up.shape[1]
    outs = [shape((tokens, w), BF) for w in (width, width, hidden, hidden, width)] + [shape((tokens, 1), F32)]

    def body(io, me):
        own, far, x, wo, wof, v, wu, wd = io.ins
        low_o, normed_o, act_o, slope_o, part_o, rstd_o = io.outs
        for c, r in enumerate(row_blocks(tokens)):

            def norm():
                attn = plain(own[r, :], wo[...]) + plain(far[r, :], wof[...])
                residual = x[r, :].astype(F32) + attn + spots(v, "b_output")
                normed, inverse = normalize(residual)
                normed_o[r, :] = normed.astype(BF)
                rstd_o[r, :] = inverse
                low_o[r, :] = (normed * spots(v, "gain_one") + spots(v, "shift_one")).astype(BF)

            def up():
                act, slope = gelu_both(plain(low_o[r, :], wu[...]) + spots(v, "b_up"))
                act_o[r, :] = act
                slope_o[r, :] = slope

            def down():
                part_o[r, :] = plain(act_o[r, :], wd[...]).astype(BF)

            io.step([(0, c), (1, c), (2, c), (3, 0), (4, 0), (5, 0)], [(0, c), (1, c), (5, c)], norm)
            io.step([(6, 0)], [(2, c), (3, c)], up)
            io.step([(7, 0)], [(4, c)], down)

    ins = [(a, by_rows(a)) for a in (ctx, ctx_far, flat)]
    ins += [(a, everything(a)) for a in (w_output, wo_far, vec, w_up, w_down)]
    return stream(body, order, ins, [(o, by_rows(o)) for o in outs])


def forward_far(order, low, wu_parts, wd_far, part, normed, vec, vec_far, cotangent, act_own, spots, split):
    tokens, width = low.shape
    wide, hidden = wu_parts[0].shape[1], wd_far.shape[0]
    outs = [shape((tokens, w), BF) for w in (width, width, hidden)]
    sums = shape((3, width), F32)

    def body(io, me, full, acts):
        low_r, wu_one, wu_two, vf, wd, v, part_r, normed_r, tan_r, act_r = io.ins
        dffn_o, out_o, slope_o, sums_o = io.outs[2:]
        for c, r in enumerate(row_blocks(tokens)):

            def up():
                bias = spots(vf, "b_up")
                for j, wu in enumerate((wu_one, wu_two)):
                    lanes = slice(j * wide, (j + 1) * wide)
                    acts[:, lanes], slope_o[r, lanes] = gelu_both(plain(low_r[r, :], wu[...]) + bias[:, lanes])

            def down():
                ffn = part_r[r, :].astype(F32) + plain(acts[...], wd[...]) + spots(v, "b_down")
                first = normed_r[r, :].astype(F32) * spots(v, "gain_one") + spots(v, "shift_one")
                normed_two, inverse = normalize(first + ffn)
                gain = spots(v, "gain_two")
                out_o[r, :] = (normed_two * gain + spots(v, "shift_two")).astype(BF)
                tangent = tan_r[r, :].astype(F32)
                d_second = norm_backward(tangent, normed_two, inverse, gain)
                dffn_o[r, :] = d_second.astype(BF)
                more = [column_sum(d_second), column_sum(tangent * normed_two), column_sum(tangent)]
                add_to(sums_o, c == 0, jnp.concatenate(more, axis=0))

            io.step([(0, c), (1, 0), (2, 0), (3, 0)], [(4, c)], up)
            io.step([(4, 0), (5, 0), (6, c), (7, c), (8, c)], [(2, c), (3, c)], down)
        io.emit(5)
        for j in range(split.width // split.block):
            lanes = slice(j * split.block, (j + 1) * split.block)
            work = functools.partial(lambda j, lanes: split.write(io, 0, me, full, j, dffn_o[...], act_r[:, lanes]), j, lanes)
            io.step([(9, j)], [(0, j), (1, j)], work)

    ins = [(low, by_rows(low))] + [(a, everything(a)) for a in (*wu_parts, vec_far, wd_far, vec)]
    ins += [(a, by_rows(a)) for a in (part, normed, cotangent)] + [(act_own, by_columns(act_own, split.block), True)]
    outs = split.outs + [(o, by_rows(o)) for o in outs] + [(sums, everything(sums))]
    return stream(body, order, ins, outs, [split.scratch, pltpu.VMEM((ROWS, hidden), BF)])


def backward_own(order, d_ffn, slope, w_up, w_down, low, split):
    tokens, width = d_ffn.shape
    hidden = w_up.shape[1]

    def body(io, me, full, d_pres):
        d, wd, slope_r, wu, low_r = io.ins
        part_o, sums_o = io.outs[2:]
        for c, r in enumerate(row_blocks(tokens)):

            def pre():
                d_pre = (against(d[r, :], wd[...]) * slope_r[r, :].astype(F32)).astype(BF)
                d_pres[r, :] = d_pre
                add_to(sums_o, c == 0, column_sum(d_pre.astype(F32)))

            def first():
                part_o[r, :] = against(d_pres[r, :], wu[...]).astype(BF)

            io.step([(0, c), (1, 0), (2, c)], [], pre)
            io.step([(3, 0)], [(2, c)], first)
        io.emit(3)
        for j in range(split.width // split.block):
            lanes = slice(j * split.block, (j + 1) * split.block)
            work = functools.partial(lambda j, lanes: split.write(io, 0, me, full, j, low_r[...], d_pres[:, lanes]), j, lanes)
            io.step([(4, 0)], [(0, j), (1, j)], work)

    ins = [(d_ffn, by_rows(d_ffn)), (w_down, everything(w_down)), (slope, by_rows(slope))]
    ins += [(w_up, everything(w_up)), (low, everything(low), True)]
    part, sums = shape((tokens, width), BF), shape((1, hidden), F32)
    outs = split.outs + [(part, by_rows(part)), (sums, everything(sums))]
    return stream(body, order, ins, outs, [split.scratch, pltpu.VMEM((tokens, hidden), BF)])


def backward_far(order, d_ffn, slope, wu_parts, wd_far, part, normed, inverse, w_output, wo_far, vec, spots):
    tokens, width = d_ffn.shape
    local, wide, hidden = w_output.shape[0], wu_parts[0].shape[1], wd_far.shape[0]

    def body(io, me, d_pres):
        d, wd, slope_r, wu_one, wu_two, part_r, norm, inv, wo, wof, v = io.ins
        dattn_o, dctx_o, dfar_o, sums_o = io.outs
        for c, r in enumerate(row_blocks(tokens)):

            def pre():
                d_pres[...] = (against(d[r, :], wd[...]) * slope_r[r, :].astype(F32)).astype(BF)

            def first():
                d_first = d[r, :].astype(F32) + part_r[r, :].astype(F32)
                for j, wu in enumerate((wu_one, wu_two)):
                    d_first = d_first + against(d_pres[:, j * wide : (j + 1) * wide], wu[...])
                normed_one = norm[r, :].astype(F32)
                d_res = norm_backward(d_first, normed_one, inv[r, :], spots(v, "gain_one"))
                dattn_o[r, :] = d_res.astype(BF)
                more = [column_sum(d_res), column_sum(d_first * normed_one), column_sum(d_first)]
                add_to(sums_o, c == 0, jnp.concatenate(more, axis=0))

            def heads():
                dctx_o[r, :] = against(dattn_o[r, :], wo[...]).astype(BF)
                dfar_o[r, :] = against(dattn_o[r, :], wof[...]).astype(BF)

            io.step([(0, c), (1, 0), (2, c)], [], pre)
            io.step([(3, 0), (4, 0), (5, c), (6, c), (7, c), (10, 0)], [(0, c)], first)
            io.step([(8, 0), (9, 0)], [(1, c), (2, c)], heads)
        io.emit(3)

    ins = [(d_ffn, by_rows(d_ffn)), (wd_far, everything(wd_far)), (slope, by_rows(slope))]
    ins += [(a, everything(a)) for a in wu_parts]
    ins += [(a, by_rows(a)) for a in (part, normed, inverse)]
    ins += [(a, everything(a)) for a in (w_output, wo_far, vec)]
    outs = [shape((tokens, w), BF) for w in (width, local, local)]
    sums = shape((3, width), F32)
    outs = [(o, by_rows(o)) for o in outs] + [(sums, everything(sums))]
    return stream(body, order, ins, outs, [pltpu.VMEM((ROWS, hidden), BF)])


def weight_grad(order, pairs, split):
    ins, sums = [], shape((1, split.width), F32)
    for left, right, start, width in pairs:
        lanes = [(slice(None), slice(i, i + split.block)) for i in range(start, start + width, split.block)]
        ins += [(left, everything(left)), (right, lanes)]

    def body(io, me, full):
        done = 0
        for p, (_, _, start, width) in enumerate(pairs):
            for c in range(width // split.block):

                def work(p, c, done, start):
                    at = start + c * split.block
                    block = io.ins[2 * p + 1][:, at : at + split.block]
                    lanes = slice(done * split.block, (done + 1) * split.block)
                    io.outs[2][:, lanes] = column_sum(block.astype(F32))
                    split.write(io, 0, me, full, done, io.ins[2 * p][...], block)

                work = functools.partial(work, p, c, done, start)
                io.step([(2 * p, 0), (2 * p + 1, c)], [(0, done), (1, done)], work)
                done += 1
        io.emit(2)

    outs = split.outs + [(sums, everything(sums))]
    return stream(body, order, ins, outs, [split.scratch])


def small_call(body, order, args, out):
    return pl.pallas_call(
        lambda *refs: body(*refs[: len(args)], refs[-1]),
        in_specs=[VMEM] * len(args) + [ANY] * len(order.last),
        out_specs=VMEM,
        out_shape=out,
        compiler_params=pltpu.CompilerParams(vmem_limit_bytes=GRANT),
        cost_estimate=LONG,
    )(*args, *order.last)


def line_up_sums(order, parts):
    total = sum(v.shape[0] * (v.shape[1] - first) for v, first in parts)

    def body(*refs):
        at = 0
        for ref, (v, first) in zip(refs, parts):
            for row in range(v.shape[0]):
                size = v.shape[1] - first
                refs[-1][:, at : at + size] = ref[row : row + 1, first:]
                at += size

    result = small_call(body, order, [v for v, _ in parts], shape((1, total), F32))
    order.now(result)
    return result


def add_all(order, *values):
    def body(*refs):
        refs[-1][...] = sum(r[...] for r in refs[1:-1]) + refs[0][...]

    result = small_call(body, order, values, shape(values[0].shape, F32))
    order.now(result)
    return result


def finish_vectors(line, me, n, width, local, hidden):
    rows, heads_at = width // n, 3 * width
    late = heads_at + 3 * local
    starts = [0, width, 2 * width, late, late + width, late + 2 * width]

    def body(me_ref, line_ref, *outs):
        shift = jnp.where(me_ref[0] == 0, 0, width - me_ref[0] * rows)
        for start, out in zip(starts, outs):
            turned = pltpu.roll(jnp.broadcast_to(line_ref[:, start : start + width], (8, width)), shift, 1)
            out[...] = turned[0:1, :rows].reshape(rows)
        for j, out in ((0, outs[6]), (2, outs[7])):
            for p in range(local // PAIR):
                at = heads_at + (3 * p + j) * PAIR
                out[p * PAIR : (p + 1) * PAIR] = line_ref[:, at : at + PAIR].reshape(PAIR)
        outs[8][...] = line_ref[:, late + heads_at : late + heads_at + hidden].reshape(hidden)

    sizes = [rows] * 6 + [local] * 2 + [hidden]
    return pl.pallas_call(
        body,
        in_specs=[SMEM, VMEM],
        out_specs=[VMEM] * 9,
        out_shape=[shape((size,), F32) for size in sizes],
    )(me, line)


def finish_heads(one, two, local):
    rows = one.shape[0]

    def body(one_ref, two_ref, q, k, v, out):
        for j, ref in enumerate((q, k, v)):
            ref[:, :PAIR] = one_ref[:, local + j * PAIR : local + (j + 1) * PAIR]
            for p in range(1, local // PAIR):
                at = (3 * (p - 1) + j) * PAIR
                ref[:, p * PAIR : (p + 1) * PAIR] = two_ref[:, at : at + PAIR]
        out[...] = one_ref[:, :local].T

    return pl.pallas_call(
        body,
        in_specs=[VMEM, VMEM],
        out_specs=[VMEM] * 4,
        out_shape=[shape((rows, local), F32)] * 3 + [shape((local, rows), F32)],
    )(one, two)


def inputs_grad(order, d_res, grads, w_own, w_far):
    tokens, width = d_res.shape
    pairs = w_own[0].shape[1] // PAIR
    wide = 6 * PAIR * pairs
    after, many, blocks = order.last, len(grads), tokens // ROWS

    def body(me_ref, *refs):
        always = me_ref[0] >= 0
        res_far, gs, (wq, wk, wv) = refs[0], refs[1 : 1 + many], refs[1 + many : 4 + many]
        wfs = refs[4 + many : 4 + many + len(w_far)]
        out_far, res, g_all, w_all, out, w_sem, g_sem, res_sem, out_sem = refs[4 + many + len(w_far) + len(after) :]
        w_copies, g_copies = [], []
        for p in range(pairs):
            for j, w in enumerate((wq, wk, wv)):
                at = (3 * p + j) * PAIR
                src, dst = w.at[:, p * PAIR : (p + 1) * PAIR], w_all.at[:, at : at + PAIR]
                w_copies.append(pltpu.make_async_copy(src, dst, w_sem.at[3 * p + j]))
        at = wide // 2
        for k, w in enumerate(wfs):
            size = w.shape[1]
            w_copies.append(pltpu.make_async_copy(w, w_all.at[:, at : at + size], w_sem.at[3 * pairs + k]))
            at += size
        for c, r in enumerate(row_blocks(tokens)):
            at, copies = 0, []
            for k, g in enumerate(gs):
                size = g.shape[1]
                copies.append(pltpu.make_async_copy(g.at[r, :], g_all.at[r, at : at + size], g_sem.at[c, k]))
                at += size
            copies.append(pltpu.make_async_copy(res_far.at[r, :], res.at[r, :], res_sem.at[c]))
            g_copies.append(copies)
        for copy in w_copies + [x for copies in g_copies for x in copies]:
            copy.start()
        for copy in w_copies:
            copy.wait()
        sent = []
        for c, r in enumerate(row_blocks(tokens)):
            for copy in g_copies[c]:
                copy.wait()

            @pl.when(always)
            def _():
                out[r, :] = (res[r, :].astype(F32) + against(g_all[r, :], w_all[...])).astype(BF)

            sent.append(pltpu.make_async_copy(out.at[r, :], out_far.at[r, :], out_sem.at[c]))
            sent[-1].start()
        for copy in sent:
            copy.wait()

    result = pl.pallas_call(
        body,
        in_specs=[SMEM] + [ANY] * (4 + many + len(w_far) + len(after)),
        out_specs=ANY,
        out_shape=shape((tokens, width), BF),
        scratch_shapes=[
            pltpu.VMEM((tokens, width), BF),
            pltpu.VMEM((tokens, wide), BF),
            pltpu.VMEM((width, wide), BF),
            pltpu.VMEM((tokens, width), BF),
            pltpu.SemaphoreType.DMA((3 * pairs + len(w_far),)),
            pltpu.SemaphoreType.DMA((blocks, many)),
            pltpu.SemaphoreType.DMA((blocks,)),
            pltpu.SemaphoreType.DMA((blocks,)),
        ],
        compiler_params=pltpu.CompilerParams(vmem_limit_bytes=GRANT),
        cost_estimate=LONG,
    )(order.me, d_res, *grads, *w_own, *w_far, *after)
    order.now(result)
    return result


def per_device(
    inputs,
    lengths,
    w_query,
    b_query,
    w_key,
    w_value,
    b_value,
    w_output,
    b_output,
    gain_one,
    shift_one,
    w_up,
    b_up,
    w_down,
    b_down,
    gain_two,
    shift_two,
    cotangent,
    *,
    n,
):
    count, length, width = inputs.shape
    local, hidden = w_query.shape[1], w_up.shape[1]
    pairs = local // PAIR
    tokens = count * length
    flat = inputs.reshape(tokens, width)
    tangent = cotangent.reshape(tokens, width)
    me = lax.axis_index("dp").astype(jnp.int32).reshape(1)
    names = ("b_up", "b_query", "b_value", "b_output", "gain_one", "shift_one", "b_down", "gain_two", "shift_two")
    given = (b_up, b_query, b_value, b_output, gain_one, shift_one, b_down, gain_two, shift_two)
    offsets, at = {}, 0
    for name, v in zip(names, given):
        offsets[name] = (at, v.shape[0])
        at += v.shape[0]

    def line_up(*refs):
        for name, ref in zip(names, refs):
            start, size = offsets[name]
            refs[-1][:, start : start + size] = ref[...].astype(F32).reshape(1, size)

    vec = pl.pallas_call(
        line_up,
        in_specs=[VMEM] * len(given),
        out_specs=VMEM,
        out_shape=shape((1, at), F32),
    )(*given)

    def spots(ref, name):
        start, size = offsets[name]
        return ref[:, start : start + size]

    y_bits, z_bits = (1, 2), (1, 4)
    quarter, half, few = width // 4, hidden // 2, local // 4

    def heads(w3, p, out, at):
        for j, w in enumerate(w3):
            out[:, at + j * PAIR : at + (j + 1) * PAIR] = w[:, p * PAIR : (p + 1) * PAIR].astype(F32)

    def prepare_one(me_ref, wq, wk, wv, one):
        heads((wq, wk, wv), 0, one, 0)

    def prepare_two(me_ref, wq, wk, wv, before, two):
        for p in range(1, pairs):
            heads((wq, wk, wv), p, two, 3 * PAIR * (p - 1))

    def prepare_pieces(me_ref, w_one, w_two, before, out_one, out_two):
        out_one[...] = w_one[...].astype(F32)
        out_two[...] = w_two[...].astype(F32)

    def prepare_piece(me_ref, w, before, out):
        out[...] = w[...].astype(F32)

    def piece(rows, cols, which, col=0):
        return pl.BlockSpec((rows, cols), lambda i, m: (index_of(m[0], which), col))

    def pieces_of(body, in_specs, sizes, *args):
        return pl.pallas_call(
            body,
            grid_spec=pltpu.PrefetchScalarGridSpec(
                num_scalar_prefetch=1,
                grid=(1,),
                in_specs=in_specs,
                out_specs=[pl.BlockSpec(size, lambda i, m: (0, 0)) for size in sizes],
            ),
            out_shape=[shape(size, F32) for size in sizes],
            compiler_params=pltpu.CompilerParams(vmem_limit_bytes=GRANT),
            cost_estimate=LONG,
        )(me, *args)

    d_bits, d_rows = (1, 2, 4), hidden // 8
    own_w = (w_query, w_key, w_value)
    order = Order(me)

    def prepare(body, in_specs, groups, *args):
        made = pieces_of(body, in_specs + [ANY] * len(order.last), [size for size, _ in groups], *args, *order.last)
        order.now(made[0])
        return [Gather(send, which, n) for send, (_, which) in zip(made, groups)]

    rest = 3 * PAIR * (pairs - 1)
    (one,) = prepare(prepare_one, [piece(quarter, PAIR, y_bits)] * 3, [((quarter, 3 * PAIR), y_bits)], *own_w)
    (two,) = prepare(prepare_two, [piece(quarter, local, z_bits)] * 3, [((quarter, rest), z_bits)], *own_w)
    vec_far = swap_x(vec)
    bias_at = [offsets["b_query"][0], offsets["b_value"][0]]
    own_bias = [(vec, a) for a in bias_at]
    own = attend(order, lengths, flat, own_w, own_bias, count, pairs, (0,))
    out, down = prepare(
        prepare_pieces,
        [piece(few, width, y_bits), piece(d_rows, width, d_bits)],
        [((few, width), y_bits), ((d_rows, width), d_bits)],
        w_output,
        w_down,
    )
    one.hop(order, 0, 1, 0)
    vec_far = order.then(vec_far)
    far_bias = [(vec_far, a) for a in bias_at]
    qkv, ctx, lse = attend(order, lengths, flat, own_w, own_bias, count, pairs, range(1, pairs), own)
    (up_one,) = prepare(prepare_piece, [piece(quarter, half, y_bits)], [((quarter, half), y_bits)], w_up)
    one.hop(order, 1)
    two.hop(order, 0, 1, 0)
    one.hop(order, 2, 0)
    one.hop(order, 3)
    w_one = one.place(order, me, [(width, 3 * PAIR)], in_rows(quarter))
    two.hop(order, 1)
    far = attend(order, lengths, flat, w_one, far_bias, count, pairs, (0,))
    (up_two,) = prepare(prepare_piece, [piece(quarter, half, y_bits, 1)], [((quarter, half), y_bits)], w_up)
    out.hop(order, 0, 1, 0)
    two.hop(order, 2, 0)
    down.hop(order, 0, 1, 2, 0)
    two.hop(order, 3)
    w_two = two.place(order, me, [(width, rest)], in_rows(quarter))
    out.hop(order, 1)
    out.hop(order, 2, 0)
    down.hop(order, 1)
    far = attend(order, lengths, flat, w_two, far_bias, count, pairs, range(1, pairs), far)
    qkv_far, ctx_far, lse_far = far
    up_one.hop(order, 0, 1, 0)
    down.hop(order, 2, 2, 0)
    out.hop(order, 3)
    (wo_far,) = out.place(order, me, [(local, width)], in_rows(few))
    down.hop(order, 3)
    down.hop(order, 4, 0)
    up_two.hop(order, 0, 1, 0)
    up_one.hop(order, 1)
    down.hop(order, 5)
    low, normed, act, slope, part, inverse = forward_own(
        order, ctx, ctx_far, flat, w_output, wo_far, w_up, w_down, vec, spots
    )
    up_one.hop(order, 2, 0)
    down.hop(order, 6, 0)
    up_one.hop(order, 3)
    wu_one = up_one.place(order, me, [(width, half)], in_rows(quarter))
    down.hop(order, 7)
    up_two.hop(order, 1)
    up_two.hop(order, 2, 0)
    (wd_far,) = down.place(order, me, [(hidden, width)], in_rows(d_rows))
    up_two.hop(order, 3)
    wu_far = (*wu_one, *up_two.place(order, me, [(width, half)], in_rows(quarter)))

    bits = [1 << i for i in range(n.bit_length() - 1)]
    y_first = tuple(bits)
    z_first = (bits[0], bits[2], bits[1]) + tuple(bits[3:])
    block = WIDE if hidden % WIDE == 0 else hidden
    down_split, up_split = Split(width, hidden, block, n, y_first), Split(width, hidden, block, n, z_first)
    group_splits = [Split(width, 6 * PAIR, 3 * PAIR, n, bits_of) for bits_of in (y_first, y_first)]
    send, keep, d_ffn, layer_out, slope_far, sums_two = forward_far(
        order, low, wu_far, wd_far, part, normed, vec, vec_far, tangent, act, spots, down_split
    )
    down_sum = down_split.scatter(me, send, keep, order)
    send, keep, d_part, sums_up = backward_own(order, d_ffn, slope, w_up, w_down, low, up_split)
    up_sum = up_split.scatter(me, send, keep, order)

    class Vectors:
        def __init__(self, parts):
            self.value, self.arriving = line_up_sums(order, parts), []

        def send(self, *over):
            masks = [sum(b for j, b in enumerate(over) if (m >> j) & 1) for m in range(1, 1 << len(over))]
            self.arriving = [swap_dp(self.value, mask, n) for mask in masks]

        def add(self):
            self.value = add_all(order, self.value, *[order.then(v) for v in self.arriving])

    early = Vectors([(sums_two, 0), (sums_up, 0)])
    early.send(bits[0])
    wide = 3 * PAIR
    st = {}

    def far_back(which):
        st.setdefault("far", []).append(attend_back(order, lengths, qkv_far, lse_far, d_ctx_far, count, which))

    def own_back(which):
        st.setdefault("own", []).append(attend_back(order, lengths, qkv, lse, d_ctx, count, which))

    for step in PLAN:
        if step == "B2":
            d_attn, d_ctx, d_ctx_far, sums_one = backward_far(
                order, d_ffn, slope_far, wu_far, wd_far, d_part, normed, inverse, w_output, wo_far, vec, spots
            )
        elif step == "OA":
            own_back(range(pairs))
        elif step == "O0":
            own_back((0,))
        elif step == "O1":
            own_back(range(1, pairs))
        elif step == "FA":
            far_back(range(pairs))
        elif step == "F0":
            far_back((0,))
        elif step == "F1":
            far_back(range(1, pairs))
        elif step == "G1":
            parts = [(d_attn, ctx, 0, local), (flat, st["own"][0], 0, wide)]
            send, keep, sums_a = weight_grad(order, parts, group_splits[0])
            group_one = group_splits[0].scatter(me, send, keep, order)
        elif step == "G2":
            own = (flat, st["own"][0], wide, wide * (pairs - 1)) if len(st["own"]) == 1 else (flat, st["own"][1], 0, wide * (pairs - 1))
            send, keep, sums_b = weight_grad(order, [own], group_splits[1])
            group_two = group_splits[1].scatter(me, send, keep, order)
        elif step == "IG":
            grad_inputs = inputs_grad(order, d_attn, [*st["own"], *st["far"]], own_w, (*w_one, *w_two))
        elif step == "L":
            late = Vectors([(sums_one, 0), (sums_a, local), (sums_b, 0)])
            late.send(bits[0])
        elif step == "L1":
            late.add()
            late.value = line_up_sums(order, [(late.value, 0), (early.value, 0)])
            left = [bits[i : i + 2] for i in range(1, len(bits), 2)]
            late.send(*left[0])
        elif step == "L2":
            late.add()
            left = left[1:]
            late.send(*left[0])
        elif step == "L3":
            late.add()
        elif step == "E":
            early.add()
        else:
            names_of = {"D": down_sum, "U": up_sum}
            if "A" in step or "B" in step:
                names_of["A"] = group_one
            if "B" in step:
                names_of["B"] = group_two
            advance(order, *[names_of[k] for k in step])
    for s in (down_sum, up_sum, group_one, group_two):
        while s.step < len(bits):
            advance(order, s)
    for over in left[1:]:
        late.send(*over)
        late.add()
    rows = width // n
    small = finish_vectors(late.value, me, n, width, local, hidden)
    by_columns_of = group_one.result, group_two.result
    if rows % 8 == 0:
        g_query, g_key, g_value, g_output = finish_heads(*by_columns_of, local)
    else:
        g_output = group_one.result[:, :local].T
        heads_of = jnp.concatenate([group_one.result[:, local:], group_two.result], axis=1)
        g_query, g_key, g_value = [heads_of.reshape(rows, pairs, 3, PAIR)[:, :, j].reshape(rows, local) for j in range(3)]
    b_output_g, gain_one_g, shift_one_g, b_down_g, gain_two_g, shift_two_g, b_query_g, b_value_g, b_up_g = small
    return (
        layer_out.reshape(count, length, width),
        grad_inputs.reshape(count, length, width),
        g_query,
        b_query_g,
        g_key,
        g_value,
        b_value_g,
        g_output,
        b_output_g,
        gain_one_g,
        shift_one_g,
        up_sum.result,
        b_up_g,
        down_sum.result.T,
        b_down_g,
        gain_two_g,
        shift_two_g,
    )


def solution(mesh):
    in_specs = (
        P("dp", None, None),
        P("dp"),
        P(None, "tensor"),
        P("tensor"),
        P(None, "tensor"),
        P(None, "tensor"),
        P("tensor"),
        P("tensor", None),
        P(),
        P(),
        P(),
        P(None, "tensor"),
        P("tensor"),
        P("tensor", None),
        P(),
        P(),
        P(),
        P("dp", None, None),
    )
    out_specs = (
        P("dp", None, None),
        P("dp", None, None),
        P("dp", "tensor"),
        P("tensor"),
        P("dp", "tensor"),
        P("dp", "tensor"),
        P("tensor"),
        P("tensor", "dp"),
        P("dp"),
        P("dp"),
        P("dp"),
        P("dp", "tensor"),
        P("tensor"),
        P("tensor", "dp"),
        P("dp"),
        P("dp"),
        P("dp"),
    )
    return jax.shard_map(
        functools.partial(per_device, n=mesh.shape["dp"]),
        mesh=mesh,
        in_specs=in_specs,
        out_specs=out_specs,
        check_vma=False,
    )
```
